32 devices in a mesh: dp: 8 (over z, x), seq: 4 (over y, core).
Axes of the slice: x: 2, y: 2, z: 4, core: 2. Of those that a mesh axis runs over, the one named last changes fastest.
Arguments:
- inputs: bfloat16 [8, 1024, 512], P('dp', 'seq'), may hold values from -6 to 6
- cotangent: bfloat16 [8, 1024, 512], P('dp', 'seq'), may hold values from -6 to 6
- w_qkv: bfloat16 [512, 1536], P(('dp', 'seq')), may hold values from -0.25 to 0.25
- b_qkv: bfloat16 [1536], P(('dp', 'seq')), may hold values from -2.5 to 2.5
- w_out: bfloat16 [512, 512], P(('dp', 'seq')), may hold values from -2 to 2
- b_out: bfloat16 [512], P(('dp', 'seq')), may hold values from -2.5 to 2.5
- w_up: bfloat16 [512, 2048], P(('dp', 'seq')), may hold values from -0.25 to 0.25
- b_up: bfloat16 [2048], P(('dp', 'seq')), may hold values from -2.5 to 2.5
- w_down: bfloat16 [2048, 512], P(('dp', 'seq')), may hold values from -0.125 to 0.125
- b_down: bfloat16 [512], P(('dp', 'seq')), may hold values from -2.5 to 2.5
- gain_one: bfloat16 [512], P(('dp', 'seq')), may hold values from 0.5 to 1.5
- shift_one: bfloat16 [512], P(('dp', 'seq')), may hold values from -2.5 to 2.5
- gain_two: bfloat16 [512], P(('dp', 'seq')), may hold values from 0.5 to 1.5
- shift_two: bfloat16 [512], P(('dp', 'seq')), may hold values from -2.5 to 2.5
Outputs:
- outputs: bfloat16 [8, 1024, 512], P('dp', 'seq')
- grad_inputs: bfloat16 [8, 1024, 512], P('dp', 'seq')
- grad_w_qkv: float32 [512, 1536], P(('dp', 'seq'))
- grad_b_qkv: float32 [1536], P(('dp', 'seq'))
- grad_w_out: float32 [512, 512], P(('dp', 'seq'))
- grad_b_out: float32 [512], P(('dp', 'seq'))
- grad_w_up: float32 [512, 2048], P(('dp', 'seq'))
- grad_b_up: float32 [2048], P(('dp', 'seq'))
- grad_w_down: float32 [2048, 512], P(('dp', 'seq'))
- grad_b_down: float32 [512], P(('dp', 'seq'))
- grad_gain_one: float32 [512], P(('dp', 'seq'))
- grad_shift_one: float32 [512], P(('dp', 'seq'))
- grad_gain_two: float32 [512], P(('dp', 'seq'))
- grad_shift_two: float32 [512], P(('dp', 'seq'))
The draws below stay inside these ranges and needn't reach their ends.
All inputs are finite; a program needn't handle non-finite values.
Results may differ from the reference program's by a relative error of at most 0.009.
Values may be sent and summed in bfloat16 or wider, within the bound.
No kernel may reach another device: no remote copies, remote signals or barrier semaphores. Data moves between devices by JAX's collectives and lax.ppermute only.
A program may use at most 128 MiB of HBM per device.

```python
import math
import jax
import jax.numpy as jnp
from jax import lax

D = 512
H = 8
HD = 64
ROT = 16
FF = 2048
LEN = 1024
SEQS = 8


def shard_levels(rng, shape, shards, smallest, high):
    factor_of, own = 1.0, jax.random.fold_in(rng, 6)
    for dim, shards_of in shards:
        heights = jnp.exp(jax.random.uniform(jax.random.fold_in(own, dim), (shards_of,), jnp.float32, smallest / len(shards), high / len(shards)))
        factor_of = factor_of * jnp.repeat(heights, shape[dim] // shards_of).reshape([-1 if axis == dim else 1 for axis in range(len(shape))])
    return factor_of


def scatter_about(key, extent, spread, bound, shards=(), kind=jnp.bfloat16):
    entries = spread * jax.random.normal(key, extent, jnp.float32)
    if shards:
        entries = entries * shard_levels(key, extent, shards, -0.22, 0.18)
    return jnp.clip(entries, -bound, bound).astype(kind)


def setup_inputs(seed: int = 0) -> dict:
    streams_of = jax.random.split(jax.random.key(seed), 15)
    return {
        "inputs": scatter_about(streams_of[0], (SEQS, LEN, D), 1.0, 6.0, ((0, 8), (1, 4))),
        "cotangent": scatter_about(streams_of[1], (SEQS, LEN, D), 1.0, 6.0, ((0, 8), (1, 4))),
        "w_qkv": scatter_about(streams_of[2], (D, 3 * D), D ** -0.5, 0.25, ((0, 32),)),
        "b_qkv": scatter_about(streams_of[3], (3 * D,), 0.3, 2.5, ((0, 32),)),
        "w_out": scatter_about(streams_of[4], (D, D), (D // 64) ** -0.5, 2.0, ((0, 32),)),
        "b_out": scatter_about(streams_of[5], (D,), 0.3, 2.5, ((0, 32),)),
        "w_up": scatter_about(streams_of[6], (D, FF), D ** -0.5, 0.25, ((0, 32),)),
        "b_up": scatter_about(streams_of[7], (FF,), 0.3, 2.5, ((0, 32),)),
        "w_down": scatter_about(streams_of[8], (FF, D), FF ** -0.5, 0.125, ((0, 32),)),
        "b_down": scatter_about(streams_of[9], (D,), 0.3, 2.5, ((0, 32),)),
        "gain_one": jnp.clip(1.0 + 0.1 * jax.random.normal(streams_of[10], (D,), jnp.float32), 0.5, 1.5).astype(jnp.bfloat16),
        "shift_one": scatter_about(streams_of[11], (D,), 0.3, 2.5, ((0, 32),)),
        "gain_two": jnp.clip(1.0 + 0.1 * jax.random.normal(streams_of[12], (D,), jnp.float32), 0.5, 1.5).astype(jnp.bfloat16),
        "shift_two": scatter_about(streams_of[13], (D,), 0.3, 2.5, ((0, 32),)),
    }


@jax.custom_vjp
def low(v):
    return lax.optimization_barrier(v.astype(jnp.bfloat16)).astype(jnp.float32)

@jax.custom_vjp
def low_back(v):
    return v

def low_keep(v):
    return (low(v), None)

def low_pass(kept, grad):
    return (grad,)

def back_keep(v):
    return (v, None)

def back_low(kept, grad):
    return (low(grad),)
low.defvjp(low_keep, low_pass)
low_back.defvjp(back_keep, back_low)
EPS = 1e-05

def product(left, right):
    return jnp.dot(left, right, precision=lax.Precision.HIGHEST, preferred_element_type=jnp.float32)

def norm_rows(values, gain_vec, shifts):
    average = lax.optimization_barrier(jnp.mean(values, axis=-1, keepdims=True))
    centered = values - average
    variance = lax.optimization_barrier(jnp.mean(centered * centered, axis=-1, keepdims=True))
    return centered * lax.rsqrt(variance + EPS) * gain_vec + shifts

def rotate(values, cosine_table, sine_table):
    half_width = cosine_table.shape[-1]
    front_part = values[..., :half_width]
    second = values[..., half_width:2 * half_width]
    remainder = values[..., 2 * half_width:]
    return jnp.concatenate([front_part * cosine_table - second * sine_table, second * cosine_table + front_part * sine_table, remainder], axis=-1)

def rotary_tables(positions):
    ladder = jnp.arange(ROT // 2).astype(jnp.float32)
    frequency = jnp.exp(ladder * (-2.0 * math.log(10000.0) / ROT))
    angles = positions.astype(jnp.float32)[:, None] * frequency[None, :]
    return (jnp.cos(angles)[:, None, :], jnp.sin(angles)[:, None, :])

def forward(params, rows_in, cosine_table, sine_table, allowed):
    w_qkv, b_qkv, w_out, b_out, w_up, b_up, w_down, b_down, gain_one, shift_one, gain_two, shift_two = params
    length = rows_in.shape[0]
    normed_a = low(norm_rows(rows_in, gain_one, shift_one))
    projected = low_back(product(normed_a, w_qkv) + b_qkv)
    queries = low(rotate(projected[:, :D].reshape(length, H, HD), cosine_table, sine_table))
    keys = low(rotate(projected[:, D:2 * D].reshape(length, H, HD), cosine_table, sine_table))
    values = low(projected[:, 2 * D:].reshape(length, H, HD))
    scores = jnp.einsum('qhd,khd->hqk', queries, keys, precision=lax.Precision.HIGHEST) * HD ** (-0.5)
    scores = low_back(scores)
    scores = jnp.where(allowed[None], scores, -1e+30)
    highest = lax.optimization_barrier(jnp.max(scores, axis=-1, keepdims=True))
    raised = jnp.exp(scores - highest)
    weights_attn = low(raised / lax.optimization_barrier(jnp.sum(raised, axis=-1, keepdims=True)))
    attended = jnp.einsum('hqk,khd->qhd', weights_attn, values, precision=lax.Precision.HIGHEST).reshape(length, D)
    attended = low(low_back(attended))
    branch_attn = product(attended, w_out) + b_out
    normed_b = low(norm_rows(rows_in, gain_two, shift_two))
    hidden = low_back(product(normed_b, w_up) + b_up)
    activated = low(jax.nn.gelu(hidden, approximate=False))
    branch_mlp = product(activated, w_down) + b_down
    return rows_in + branch_attn + branch_mlp

def reference(inputs, cotangent, w_qkv, b_qkv, w_out, b_out, w_up, b_up, w_down, b_down, gain_one, shift_one, gain_two, shift_two):
    params = tuple((item.astype(jnp.float32) for item in (w_qkv, b_qkv, w_out, b_out, w_up, b_up, w_down, b_down, gain_one, shift_one, gain_two, shift_two)))
    places = jnp.arange(LEN).astype(jnp.int32)
    cosine_table, sine_table = rotary_tables(places)
    allowed = places[:, None] >= places[None, :]

    def per_sequence(totals, seq_pair):
        seq_in, seq_cot = seq_pair

        def apply_layer(prm, rows_in):
            return forward(prm, rows_in, cosine_table, sine_table, allowed)
        result, pullback = jax.vjp(apply_layer, params, seq_in.astype(jnp.float32))
        grad_params, grad_rows = pullback(seq_cot.astype(jnp.float32))
        totals = jax.tree.map(jnp.add, totals, grad_params)
        return (totals, (result.astype(jnp.bfloat16), grad_rows.astype(jnp.bfloat16)))
    zero_grads = tuple((jnp.zeros(item.shape, jnp.float32) for item in params))
    totals, (outputs, grad_inputs) = lax.scan(per_sequence, zero_grads, (inputs, cotangent))
    return (outputs, grad_inputs, totals[0], totals[1], totals[2], totals[3], totals[4], totals[5], totals[6], totals[7], totals[8], totals[9], totals[10], totals[11])
```

```python
import functools
import math

import jax
import jax.numpy as jnp
import numpy as np
from jax import lax
from jax.experimental import pallas as pl
from jax.experimental.pallas import tpu as pltpu
from jax.sharding import PartitionSpec as P

HD = 64
ROT = 16
EPS = 1e-05
BLOCK = 256
F32 = jnp.float32
BF16 = jnp.bfloat16
PARAMS = pltpu.CompilerParams(vmem_limit_bytes=48 * 1024 * 1024)


def log2(count):
    assert count & (count - 1) == 0
    return count.bit_length() - 1


def exchange(value, axis, size, bit):
    return lax.ppermute(value, axis, [(i, i ^ (1 << bit)) for i in range(size)])


def flag_of(axis, bit):
    return (lax.axis_index(axis) >> bit) & 1 == 1


def gather_bits(value, axis, size):
    shape = value.shape
    for done, bit in enumerate(reversed(range(log2(size)))):
        other = exchange(value, axis, size, bit)
        upper = flag_of(axis, bit)
        value = jnp.where(
            upper,
            jnp.stack([other, value], done),
            jnp.stack([value, other], done),
        )
    return value.reshape((size,) + shape)


def swap_bits(blocks, axis, size):
    count = log2(size)
    rest = blocks.shape[1:]
    value = blocks.reshape((2,) * count + rest)
    for bit in range(count):
        place = count - 1 - bit
        low = lax.index_in_dim(value, 0, place, keepdims=False)
        high = lax.index_in_dim(value, 1, place, keepdims=False)
        upper = flag_of(axis, bit)
        other = exchange(jnp.where(upper, low, high), axis, size, bit)
        value = jnp.stack([jnp.where(upper, other, low), jnp.where(upper, high, other)], place)
    return value.reshape((size,) + rest)


def scatter_bits(blocks, axis, size):
    count = log2(size)
    rest = blocks.shape[1:]
    value = blocks.reshape((2,) * count + rest)
    for bit in range(count):
        place = count - 1 - bit
        low = lax.index_in_dim(value, 0, place, keepdims=False)
        high = lax.index_in_dim(value, 1, place, keepdims=False)
        upper = flag_of(axis, bit)
        sent = jnp.where(upper, low, high).astype(BF16)
        value = jnp.where(upper, high, low).astype(F32) + exchange(sent, axis, size, bit).astype(F32)
    return value


def dot(left, right):
    return lax.dot_general(left, right, (((1,), (0,)), ((), ())), preferred_element_type=F32)


def dot_rows(left, right):
    return lax.dot_general(left, right, (((0,), (0,)), ((), ())), preferred_element_type=F32)


def dot_last(left, right):
    return lax.dot_general(left, right, (((1,), (1,)), ((), ())), preferred_element_type=F32)


def standardize(rows):
    average = jnp.mean(rows, axis=-1, keepdims=True)
    centered = rows - average
    variance = jnp.mean(centered * centered, axis=-1, keepdims=True)
    scale = lax.rsqrt(variance + EPS)
    return centered * scale, scale


def norm_back(normal, scale, gain, upstream):
    inner = gain * upstream
    first = jnp.mean(inner, axis=-1, keepdims=True)
    second = jnp.mean(inner * normal, axis=-1, keepdims=True)
    return scale * (inner - first - normal * second)


def attention_kernel(
    xg_ref, wq_ref, wo_ref, vec_ref, bias_ref, cos_ref, sin_ref,
    out_ref, dx_ref, grad_ref,
    na_ref, q_ref, k_ref, v_ref, da_ref, qt_ref, dat_ref, att_ref, dq_ref, dkt_ref, dvt_ref, dp_ref,
):
    tokens = xg_ref.shape[0]
    width = xg_ref.shape[1] // 2
    part = wo_ref.shape[0]
    heads = part // HD
    owners, _, _ = grad_ref.shape
    own_rows = width // owners
    out_rows = part // owners
    gain = vec_ref[0:1, :]
    shift = vec_ref[1:2, :]
    lane = lax.broadcasted_iota(jnp.int32, (BLOCK, part), 1)
    turn = lane % HD < ROT // 2

    def partner(value):
        return jnp.where(
            turn, pltpu.roll(value, part - ROT // 2, 1), pltpu.roll(value, ROT // 2, 1)
        )

    for block in range(tokens // BLOCK):
        rows = pl.ds(block * BLOCK, BLOCK)
        normal, _ = standardize(xg_ref[rows, :width].astype(F32))
        normed = (normal * gain + shift).astype(BF16)
        na_ref[rows, :] = normed
        projected = dot(normed, wq_ref[...]) + bias_ref[...]
        cosine, sine = cos_ref[rows, :], sin_ref[rows, :]
        query = projected[:, :part]
        query = query * cosine + partner(query) * sine
        key = projected[:, part : 2 * part]
        key = key * cosine + partner(key) * sine
        query = query.astype(BF16).astype(F32) * HD**-0.5
        q_ref[rows, :] = query.astype(BF16)
        qt_ref[:, rows] = query.T.astype(BF16)
        k_ref[rows, :] = key.astype(BF16)
        v_ref[rows, :] = projected[:, 2 * part :].astype(BF16)
        grad_att = dot_last(xg_ref[rows, width:], wo_ref[...]).astype(BF16)
        da_ref[rows, :] = grad_att
        dat_ref[:, rows] = grad_att.astype(F32).T.astype(BF16)

    dkt_ref[...] = jnp.zeros_like(dkt_ref)
    dvt_ref[...] = jnp.zeros_like(dvt_ref)
    below = lax.broadcasted_iota(jnp.int32, (BLOCK, BLOCK), 0) >= lax.broadcasted_iota(
        jnp.int32, (BLOCK, BLOCK), 1
    )
    zero = jnp.zeros((), BF16)
    for block in range(tokens // BLOCK):
        rows = pl.ds(block * BLOCK, BLOCK)
        seen = (block + 1) * BLOCK
        attended = jnp.zeros((BLOCK, part), F32)
        grad_query = jnp.zeros((BLOCK, part), F32)
        for head in range(heads):
            mine = lane // HD == head
            mine_t = lax.broadcasted_iota(jnp.int32, (part, BLOCK), 0) // HD == head
            query = jnp.where(mine, q_ref[rows, :], zero)
            grad_att = jnp.where(mine, da_ref[rows, :], zero)
            scores = dot_last(query, k_ref[:seen, :])
            last = jnp.where(below, scores[:, seen - BLOCK :], -1e30)
            scores = last if block == 0 else jnp.concatenate([scores[:, : seen - BLOCK], last], 1)
            raised = jnp.exp(scores - jnp.max(scores, axis=-1, keepdims=True))
            probs = raised * (1.0 / jnp.sum(raised, axis=-1, keepdims=True))
            probs_low = probs.astype(BF16)
            attended = jnp.where(mine, dot(probs_low, v_ref[:seen, :]), attended)
            grad_probs = dot_last(grad_att, v_ref[:seen, :])
            inner = jnp.sum(probs * grad_probs, axis=-1, keepdims=True)
            grad_scores = (probs * (grad_probs - inner)).astype(BF16)
            grad_query = jnp.where(mine, dot(grad_scores, k_ref[:seen, :]), grad_query)
            query_t = jnp.where(mine_t, qt_ref[:, rows], zero)
            grad_att_t = jnp.where(mine_t, dat_ref[:, rows], zero)
            dkt_ref[:, :seen] += dot(query_t, grad_scores)
            dvt_ref[:, :seen] += dot(grad_att_t, probs_low)
        att_ref[rows, :] = attended.astype(BF16)
        dq_ref[rows, :] = grad_query * HD**-0.5

    vectors = [jnp.zeros((1, width), F32) for _ in range(3)]
    grad_bias = jnp.zeros((1, 3 * part), F32)
    for block in range(tokens // BLOCK):
        rows = pl.ds(block * BLOCK, BLOCK)
        cosine, sine = cos_ref[rows, :], sin_ref[rows, :]
        grad_query = dq_ref[rows, :]
        grad_query = grad_query * cosine - partner(grad_query) * sine
        grad_key = dkt_ref[:, rows].T
        grad_key = grad_key * cosine - partner(grad_key) * sine
        grad_value = dvt_ref[:, rows].T
        grad_proj = jnp.concatenate([grad_query, grad_key, grad_value], 1).astype(BF16)
        dp_ref[rows, :] = grad_proj
        grad_bias += jnp.sum(grad_proj.astype(F32), axis=0, keepdims=True)
        out_ref[rows, :] = dot(att_ref[rows, :], wo_ref[...])
        upstream = dot_last(grad_proj, wq_ref[...])
        normal, scale = standardize(xg_ref[rows, :width].astype(F32))
        vectors[0] += jnp.sum(normal * upstream, axis=0, keepdims=True)
        vectors[1] += jnp.sum(upstream, axis=0, keepdims=True)
        vectors[2] += jnp.sum(xg_ref[rows, width:].astype(F32), axis=0, keepdims=True)
        dx_ref[rows, :] = norm_back(normal, scale, gain, upstream)

    grad_qkv = dot_rows(na_ref[...], dp_ref[...])
    grad_out = dot_rows(att_ref[...], xg_ref[:, width:])
    rest = grad_ref.shape[1] - own_rows - out_rows
    tail = jnp.concatenate(
        [jnp.concatenate([grad_bias, jnp.zeros((1, width - 3 * part), F32)], 1)]
        + vectors
        + [jnp.zeros((rest - 4, width), F32)],
        0,
    )
    for owner in range(owners):
        grad_ref[owner, :own_rows, : 3 * part] = grad_qkv[owner * own_rows : (owner + 1) * own_rows, :]
        grad_ref[owner, :own_rows, 3 * part :] = jnp.zeros((own_rows, width - 3 * part), F32)
        grad_ref[owner, own_rows : own_rows + out_rows, :] = grad_out[
            owner * out_rows : (owner + 1) * out_rows, :
        ]
        grad_ref[owner, own_rows + out_rows :, :] = tail


def mlp_kernel(
    xg_ref, up_ref, down_ref, vec_ref, bias_ref, out_part_ref, dx_part_ref,
    out_ref, dx_ref, grad_ref,
    nb_ref, act_ref, dh_ref,
):
    tokens = xg_ref.shape[0]
    width = xg_ref.shape[1] // 2
    hidden_width = up_ref.shape[1]
    owners = grad_ref.shape[0]
    up_rows = width // owners
    down_rows = hidden_width // owners
    gain = vec_ref[2:3, :]
    shift = vec_ref[3:4, :]
    vectors = [jnp.zeros((1, width), F32) for _ in range(2)]
    grad_bias = jnp.zeros((1, hidden_width), F32)
    for block in range(tokens // BLOCK):
        rows = pl.ds(block * BLOCK, BLOCK)
        grad_rows = xg_ref[rows, width:]
        normal, scale = standardize(xg_ref[rows, :width].astype(F32))
        normed = (normal * gain + shift).astype(BF16)
        nb_ref[rows, :] = normed
        hidden = dot(normed, up_ref[...]) + bias_ref[...]
        half = 0.5 * (1.0 + lax.erf(hidden * math.sqrt(0.5)))
        active = (hidden * half).astype(BF16)
        act_ref[rows, :] = active
        slope = half + hidden * jnp.exp(-0.5 * hidden * hidden) * (1.0 / math.sqrt(2.0 * math.pi))
        grad_hidden = (dot_last(grad_rows, down_ref[...]) * slope).astype(BF16)
        dh_ref[rows, :] = grad_hidden
        grad_bias += jnp.sum(grad_hidden.astype(F32), axis=0, keepdims=True)
        out_ref[rows, :] = (out_part_ref[rows, :] + dot(active, down_ref[...])).astype(out_ref.dtype)
        upstream = dot_last(grad_hidden, up_ref[...])
        vectors[0] += jnp.sum(normal * upstream, axis=0, keepdims=True)
        vectors[1] += jnp.sum(upstream, axis=0, keepdims=True)
        dx_ref[rows, :] = (dx_part_ref[rows, :] + norm_back(normal, scale, gain, upstream)).astype(dx_ref.dtype)
    grad_up = dot_rows(nb_ref[...], dh_ref[...])
    grad_down = dot_rows(act_ref[...], xg_ref[:, width:])
    rest = grad_ref.shape[1] - up_rows - down_rows
    tail = jnp.concatenate([grad_bias] + vectors + [jnp.zeros((rest - 3, width), F32)], 0)
    for owner in range(owners):
        grad_ref[owner, :up_rows, :] = grad_up[owner * up_rows : (owner + 1) * up_rows, :]
        grad_ref[owner, up_rows : up_rows + down_rows, :] = grad_down[
            owner * down_rows : (owner + 1) * down_rows, :
        ]
        grad_ref[owner, up_rows + down_rows :, :] = tail


def whole(count):
    return [pl.BlockSpec(memory_space=pltpu.VMEM)] * count


def attention(xg, w_qkv, w_out, vectors, bias, cosine, sine, owners):
    tokens, width = xg.shape[0], xg.shape[1] // 2
    part = w_out.shape[0]
    rows = width // owners + part // owners + 16
    shape = jax.ShapeDtypeStruct
    flops = 2 * tokens * width * part * 12 + 2 * 5 * tokens * tokens * part
    return pl.pallas_call(
        attention_kernel,
        out_shape=(
            shape((tokens, width), F32),
            shape((tokens, width), F32),
            shape((owners, rows, width), F32),
        ),
        in_specs=whole(7),
        out_specs=tuple(whole(3)),
        scratch_shapes=[
            pltpu.VMEM((tokens, width), BF16),
            pltpu.VMEM((tokens, part), BF16),
            pltpu.VMEM((tokens, part), BF16),
            pltpu.VMEM((tokens, part), BF16),
            pltpu.VMEM((tokens, part), BF16),
            pltpu.VMEM((part, tokens), BF16),
            pltpu.VMEM((part, tokens), BF16),
            pltpu.VMEM((tokens, part), BF16),
            pltpu.VMEM((tokens, part), F32),
            pltpu.VMEM((part, tokens), F32),
            pltpu.VMEM((part, tokens), F32),
            pltpu.VMEM((tokens, 3 * part), BF16),
        ],
        compiler_params=PARAMS,
        cost_estimate=pl.CostEstimate(
            flops=4 * flops, bytes_accessed=8 * tokens * width * 4, transcendentals=tokens * tokens * 2
        ),
    )(xg, w_qkv, w_out, vectors, bias, cosine, sine)


def feed_forward(xg, w_up, w_down, vectors, bias, out_part, dx_part, owners):
    tokens, width = xg.shape[0], xg.shape[1] // 2
    hidden_width = w_up.shape[1]
    rows = width // owners + hidden_width // owners + 16
    shape = jax.ShapeDtypeStruct
    return pl.pallas_call(
        mlp_kernel,
        out_shape=(
            shape((tokens, width), F32),
            shape((tokens, width), F32),
            shape((owners, rows, width), F32),
        ),
        in_specs=whole(7),
        out_specs=tuple(whole(3)),
        scratch_shapes=[
            pltpu.VMEM((tokens, width), BF16),
            pltpu.VMEM((tokens, hidden_width), BF16),
            pltpu.VMEM((tokens, hidden_width), BF16),
        ],
        compiler_params=PARAMS,
        cost_estimate=pl.CostEstimate(
            flops=12 * tokens * width * hidden_width,
            bytes_accessed=8 * tokens * width * 4,
            transcendentals=2 * tokens * hidden_width,
        ),
    )(xg, w_up, w_down, vectors, bias, out_part, dx_part)


def rotary(tokens, heads):
    ladder = np.arange(ROT // 2, dtype=np.float32)
    frequency = np.exp(ladder * np.float32(-2.0 * math.log(10000.0) / ROT)).astype(np.float32)
    angles = np.arange(tokens, dtype=np.float32)[:, None] * frequency[None, :]
    cosine = np.ones((tokens, HD), np.float32)
    sine = np.zeros((tokens, HD), np.float32)
    half = ROT // 2
    cosine[:, :half] = cosine[:, half:ROT] = np.cos(angles)
    sine[:, half:ROT] = np.sin(angles)
    sine[:, :half] = -sine[:, half:ROT]
    return np.tile(cosine, (1, heads)), np.tile(sine, (1, heads))


def shards(
    owners, groups,
    inputs, cotangent, w_qkv, b_qkv, w_out, b_out, w_up, b_up, w_down, b_down,
    gain_one, shift_one, gain_two, shift_two,
):
    rows, width = w_qkv.shape[0], w_qkv.shape[1] // 3
    hidden = w_up.shape[1]
    down_rows = w_down.shape[0]
    local = inputs.shape[1]
    tokens = local * groups
    part = width // groups
    slice_width = hidden // groups
    dp_rows = rows * groups
    group = lax.axis_index("seq")
    owner = lax.axis_index("dp")

    xg = jnp.concatenate([inputs[0], cotangent[0]], axis=1)
    xg = gather_bits(xg, "seq", groups).reshape(tokens, 2 * width)

    devices = owners * groups
    place = [(f % owners) * groups + f // owners for f in range(devices)]
    out_rows = lax.ppermute(w_out, ("dp", "seq"), [(f, place[f]) for f in range(devices)])

    small = jnp.concatenate(
        [b_qkv.reshape(rows, -1), b_up.reshape(rows, -1)]
        + [v[:, None] for v in (b_out, b_down, gain_one, shift_one, gain_two, shift_two)],
        axis=1,
    )
    n_small = small.shape[1]
    n_up = b_up.shape[0] // rows
    small = jnp.pad(small, ((0, 0), (0, width - 3 * part - n_small)))
    blocks = jnp.concatenate(
        [
            w_qkv.reshape(rows, 3, groups, part).transpose(2, 0, 1, 3).reshape(groups, rows, 3 * part),
            jnp.broadcast_to(small[None], (groups,) + small.shape),
            w_up.reshape(rows, owners, groups, -1).transpose(2, 0, 1, 3).reshape(groups, rows, slice_width),
        ],
        axis=2,
    )
    blocks = swap_bits(blocks, "seq", groups).reshape(dp_rows, width + slice_width)
    first = gather_bits(jnp.concatenate([blocks[:, :width], out_rows], axis=0), "dp", owners)
    second = gather_bits(jnp.concatenate([blocks[:, width:], w_down], axis=0), "dp", owners)

    full_qkv = first[:, :dp_rows, : 3 * part].reshape(width, 3 * part)
    full_out = first[:, dp_rows:, :].reshape(part, width)
    small = first[:, :dp_rows, 3 * part : 3 * part + n_small].reshape(width, n_small).astype(F32)
    bias_qkv = lax.dynamic_index_in_dim(
        small[:, :3].reshape(3, groups, part), group, 1, keepdims=False
    ).reshape(1, 3 * part)
    bias_up = lax.dynamic_index_in_dim(
        small[:, 3 : 3 + n_up].reshape(owners, groups, -1), group, 1, keepdims=False
    ).reshape(1, slice_width)
    vectors = small[:, 3 + n_up :].T
    biases = vectors[0] + vectors[1]
    vectors = jnp.concatenate([vectors[2:], jnp.zeros((4, width), F32)], 0)
    full_up = second[:, :dp_rows, :].reshape(width, slice_width)
    full_down = second[:, dp_rows:, :].reshape(slice_width, width)

    cosine, sine = rotary(tokens, part // HD)
    out_part, dx_part, grad_a = attention(
        xg, full_qkv, full_out, vectors, bias_qkv, jnp.asarray(cosine), jnp.asarray(sine), owners
    )
    out_part, dx_part, grad_b = feed_forward(
        xg, full_up, full_down, vectors, bias_up, out_part, dx_part, owners
    )

    grad_a = scatter_bits(grad_a, "dp", owners)
    grad_b = scatter_bits(grad_b, "dp", owners)
    both = jnp.concatenate([out_part, dx_part], axis=1).reshape(groups, local, 2 * width)
    both = scatter_bits(both, "seq", groups)
    outputs = (inputs[0].astype(F32) + both[:, :width] + biases[None]).astype(BF16)[None]
    grad_inputs = (cotangent[0].astype(F32) + both[:, width:]).astype(BF16)[None]

    own_wout = lax.ppermute(
        grad_a[dp_rows : dp_rows + rows, :], ("dp", "seq"), [(place[f], f) for f in range(devices)]
    )
    tail_a = grad_a[dp_rows + rows :, :]
    tail_b = grad_b[dp_rows + down_rows :, :]
    small = jnp.concatenate([tail_a[:4], tail_b[1:3], jnp.zeros((2, width), F32)], 0)
    send = jnp.concatenate(
        [
            grad_a[:dp_rows, : 3 * part].reshape(groups, rows, 3 * part),
            grad_b[:dp_rows, :].reshape(groups, rows, slice_width),
        ],
        axis=2,
    )
    small = jnp.pad(small, ((0, 0), (0, send.shape[2] - width)))
    send = jnp.concatenate([send, jnp.broadcast_to(small[None], (groups,) + small.shape)], axis=1)
    send = swap_bits(send, "seq", groups)
    own_wqkv = send[:, :rows, : 3 * part].reshape(groups, rows, 3, part).transpose(1, 2, 0, 3).reshape(rows, -1)
    own_wup = (
        send[:, :rows, 3 * part :].reshape(groups, rows, owners, -1).transpose(1, 2, 0, 3).reshape(rows, -1)
    )
    small = send[:, rows:, :width]
    index = owner * groups + group
    own_bqkv = lax.dynamic_slice_in_dim(
        small[:, 0, : 3 * part].reshape(groups, 3, part).transpose(1, 0, 2).reshape(-1),
        index * b_qkv.shape[0],
        b_qkv.shape[0],
    )
    sums = jnp.sum(small, axis=0)
    own = lax.dynamic_slice_in_dim(sums, index * rows, rows, axis=1)
    own_bias = lax.dynamic_slice_in_dim(small[0, 3], index * rows, rows)
    own_bup = lax.dynamic_slice_in_dim(tail_b[0], owner * b_up.shape[0], b_up.shape[0])
    return (
        outputs,
        grad_inputs,
        own_wqkv,
        own_bqkv,
        own_wout,
        own_bias,
        own_wup,
        own_bup,
        grad_b[dp_rows : dp_rows + down_rows, :],
        own_bias,
        own[1],
        own[2],
        own[4],
        own[5],
    )


def solution(mesh):
    rows = P("dp", "seq", None)
    matrix, vector = P(("dp", "seq"), None), P(("dp", "seq"))
    weights = (matrix, vector) * 4
    return jax.shard_map(
        functools.partial(shards, mesh.shape["dp"], mesh.shape["seq"]),
        mesh=mesh,
        in_specs=(rows, rows) + weights + (vector,) * 4,
        out_specs=(rows, rows) + weights + (vector,) * 4,
        check_vma=False,
    )
```

```python
import functools
import math

import jax
import jax.numpy as jnp
import numpy as np
from jax import lax
from jax.experimental import pallas as pl
from jax.experimental.pallas import tpu as pltpu
from jax.sharding import PartitionSpec as P

HD = 64
ROT = 16
EPS = 1e-05
BLOCK = 256
F32 = jnp.float32
BF16 = jnp.bfloat16
PARAMS = pltpu.CompilerParams(vmem_limit_bytes=48 * 1024 * 1024)


def log2(count):
    assert count & (count - 1) == 0
    return count.bit_length() - 1


def exchange(value, axis, size, bit):
    return lax.ppermute(value, axis, [(i, i ^ (1 << bit)) for i in range(size)])


def flag_of(axis, bit):
    return (lax.axis_index(axis) >> bit) & 1 == 1


def gather_bits(value, axis, size):
    shape = value.shape
    for done, bit in enumerate(reversed(range(log2(size)))):
        other = exchange(value, axis, size, bit)
        upper = flag_of(axis, bit)
        value = jnp.where(
            upper,
            jnp.stack([other, value], done),
            jnp.stack([value, other], done),
        )
    return value.reshape((size,) + shape)


def swap_bits(blocks, axis, size):
    count = log2(size)
    rest = blocks.shape[1:]
    value = blocks.reshape((2,) * count + rest)
    for bit in range(count):
        place = count - 1 - bit
        low = lax.index_in_dim(value, 0, place, keepdims=False)
        high = lax.index_in_dim(value, 1, place, keepdims=False)
        upper = flag_of(axis, bit)
        other = exchange(jnp.where(upper, low, high), axis, size, bit)
        value = jnp.stack([jnp.where(upper, other, low), jnp.where(upper, high, other)], place)
    return value.reshape((size,) + rest)


def scatter_bits(blocks, axis, size):
    count = log2(size)
    rest = blocks.shape[1:]
    value = blocks.reshape((2,) * count + rest)
    for bit in range(count):
        place = count - 1 - bit
        low = lax.index_in_dim(value, 0, place, keepdims=False)
        high = lax.index_in_dim(value, 1, place, keepdims=False)
        upper = flag_of(axis, bit)
        sent = jnp.where(upper, low, high).astype(BF16)
        value = jnp.where(upper, high, low).astype(F32) + exchange(sent, axis, size, bit).astype(F32)
    return value


def dot(left, right):
    return lax.dot_general(left, right, (((1,), (0,)), ((), ())), preferred_element_type=F32)


def dot_rows(left, right):
    return lax.dot_general(left, right, (((0,), (0,)), ((), ())), preferred_element_type=F32)


def dot_last(left, right):
    return lax.dot_general(left, right, (((1,), (1,)), ((), ())), preferred_element_type=F32)


def standardize(rows):
    average = jnp.mean(rows, axis=-1, keepdims=True)
    centered = rows - average
    variance = jnp.mean(centered * centered, axis=-1, keepdims=True)
    scale = lax.rsqrt(variance + EPS)
    return centered * scale, scale


def norm_back(normal, scale, inner):
    first = jnp.mean(inner, axis=-1, keepdims=True)
    second = jnp.mean(inner * normal, axis=-1, keepdims=True)
    return scale * (inner - first - normal * second)


def attention_kernel(
    xg_ref, wq_ref, wo_ref, vec_ref, bias_ref, cos_ref, sin_ref,
    out_ref, dx_ref, grad_ref,
    na_ref, q_ref, k_ref, v_ref, da_ref, qt_ref, dat_ref, att_ref, dq_ref, dkt_ref, dvt_ref, dp_ref,
):
    tokens = xg_ref.shape[0]
    width = xg_ref.shape[1] // 2
    part = wo_ref.shape[0]
    heads = part // HD
    owners, _, _ = grad_ref.shape
    own_rows = width // owners
    out_rows = part // owners
    gain = vec_ref[0:1, :]
    shift = vec_ref[1:2, :]
    lane = lax.broadcasted_iota(jnp.int32, (BLOCK, part), 1)
    turn = lane % HD < ROT // 2

    def partner(value):
        return jnp.where(
            turn, pltpu.roll(value, part - ROT // 2, 1), pltpu.roll(value, ROT // 2, 1)
        )

    for block in range(tokens // BLOCK):
        rows = pl.ds(block * BLOCK, BLOCK)
        normal, _ = standardize(xg_ref[rows, :width].astype(F32))
        normed = (normal * gain + shift).astype(BF16)
        na_ref[rows, :] = normed
        projected = dot(normed, wq_ref[...]) + bias_ref[...]
        cosine, sine = cos_ref[rows, :], sin_ref[rows, :]
        query = projected[:, :part]
        query = query * cosine + partner(query) * sine
        key = projected[:, part : 2 * part]
        key = key * cosine + partner(key) * sine
        query = query.astype(BF16).astype(F32) * HD**-0.5
        q_ref[rows, :] = query.astype(BF16)
        qt_ref[:, rows] = query.T.astype(BF16)
        k_ref[rows, :] = key.astype(BF16)
        v_ref[rows, :] = projected[:, 2 * part :].astype(BF16)
        grad_att = dot_last(xg_ref[rows, width:], wo_ref[...]).astype(BF16)
        da_ref[rows, :] = grad_att
        dat_ref[:, rows] = grad_att.astype(F32).T.astype(BF16)

    dkt_ref[...] = jnp.zeros_like(dkt_ref)
    dvt_ref[...] = jnp.zeros_like(dvt_ref)
    below = lax.broadcasted_iota(jnp.int32, (BLOCK, BLOCK), 0) >= lax.broadcasted_iota(
        jnp.int32, (BLOCK, BLOCK), 1
    )
    zero = jnp.zeros((), BF16)
    for block in range(tokens // BLOCK):
        rows = pl.ds(block * BLOCK, BLOCK)
        seen = (block + 1) * BLOCK
        attended = jnp.zeros((BLOCK, part), F32)
        grad_query = jnp.zeros((BLOCK, part), F32)
        for head in range(heads):
            mine = lane // HD == head
            mine_t = lax.broadcasted_iota(jnp.int32, (part, BLOCK), 0) // HD == head
            query = jnp.where(mine, q_ref[rows, :], zero)
            grad_att = jnp.where(mine, da_ref[rows, :], zero)
            scores = dot_last(query, k_ref[:seen, :])
            last = jnp.where(below, scores[:, seen - BLOCK :], -1e30)
            scores = last if block == 0 else jnp.concatenate([scores[:, : seen - BLOCK], last], 1)
            raised = jnp.exp(scores - jnp.max(scores, axis=-1, keepdims=True))
            probs = raised * (1.0 / jnp.sum(raised, axis=-1, keepdims=True))
            probs_low = probs.astype(BF16)
            attended = jnp.where(mine, dot(probs_low, v_ref[:seen, :]), attended)
            grad_probs = dot_last(grad_att, v_ref[:seen, :])
            inner = jnp.sum(probs * grad_probs, axis=-1, keepdims=True)
            grad_scores = (probs * (grad_probs - inner)).astype(BF16)
            grad_query = jnp.where(mine, dot(grad_scores, k_ref[:seen, :]), grad_query)
            query_t = jnp.where(mine_t, qt_ref[:, rows], zero)
            grad_att_t = jnp.where(mine_t, dat_ref[:, rows], zero)
            dkt_ref[:, :seen] += dot(query_t, grad_scores)
            dvt_ref[:, :seen] += dot(grad_att_t, probs_low)
        att_ref[rows, :] = attended.astype(BF16)
        dq_ref[rows, :] = grad_query * HD**-0.5

    vectors = [jnp.zeros((1, width), F32) for _ in range(3)]
    grad_bias = jnp.zeros((1, 3 * part), F32)
    for block in range(tokens // BLOCK):
        rows = pl.ds(block * BLOCK, BLOCK)
        cosine, sine = cos_ref[rows, :], sin_ref[rows, :]
        grad_query = dq_ref[rows, :]
        grad_query = grad_query * cosine - partner(grad_query) * sine
        grad_key = dkt_ref[:, rows].T
        grad_key = grad_key * cosine - partner(grad_key) * sine
        grad_value = dvt_ref[:, rows].T
        grad_proj = jnp.concatenate([grad_query, grad_key, grad_value], 1).astype(BF16)
        dp_ref[rows, :] = grad_proj
        grad_bias += jnp.sum(grad_proj.astype(F32), axis=0, keepdims=True)
        out_ref[rows, :] = dot(att_ref[rows, :], wo_ref[...])
        upstream = dot_last(grad_proj, wq_ref[...])
        normal, scale = standardize(xg_ref[rows, :width].astype(F32))
        vectors[0] += jnp.sum(normal * upstream, axis=0, keepdims=True)
        vectors[1] += jnp.sum(upstream, axis=0, keepdims=True)
        vectors[2] += jnp.sum(xg_ref[rows, width:].astype(F32), axis=0, keepdims=True)
        dx_ref[rows, :] = norm_back(normal, scale, gain * upstream)

    grad_qkv = dot_rows(na_ref[...], dp_ref[...])
    grad_out = dot_rows(att_ref[...], xg_ref[:, width:])
    rest = grad_ref.shape[1] - own_rows - out_rows
    tail = jnp.concatenate(
        [jnp.concatenate([grad_bias, jnp.zeros((1, width - 3 * part), F32)], 1)]
        + vectors
        + [jnp.zeros((rest - 4, width), F32)],
        0,
    )
    for owner in range(owners):
        grad_ref[owner, :own_rows, : 3 * part] = grad_qkv[owner * own_rows : (owner + 1) * own_rows, :]
        grad_ref[owner, :own_rows, 3 * part :] = jnp.zeros((own_rows, width - 3 * part), F32)
        grad_ref[owner, own_rows : own_rows + out_rows, :] = grad_out[
            owner * out_rows : (owner + 1) * out_rows, :
        ]
        grad_ref[owner, own_rows + out_rows :, :] = tail


def mlp_kernel(
    xg_ref, up_ref, down_ref, vec_ref, bias_ref, out_part_ref, dx_part_ref,
    out_ref, dx_ref, grad_ref,
    nb_ref, act_ref, dh_ref,
):
    tokens = xg_ref.shape[0]
    width = xg_ref.shape[1] // 2
    hidden_width = up_ref.shape[1]
    owners = grad_ref.shape[0]
    up_rows = width // owners
    down_rows = hidden_width // owners
    gain = vec_ref[2:3, :]
    shift = vec_ref[3:4, :]
    vectors = [jnp.zeros((1, width), F32) for _ in range(2)]
    grad_bias = jnp.zeros((1, hidden_width), F32)
    for block in range(tokens // BLOCK):
        rows = pl.ds(block * BLOCK, BLOCK)
        grad_rows = xg_ref[rows, width:]
        normal, scale = standardize(xg_ref[rows, :width].astype(F32))
        normed = (normal * gain + shift).astype(BF16)
        nb_ref[rows, :] = normed
        hidden = dot(normed, up_ref[...]) + bias_ref[...]
        half = 0.5 * (1.0 + lax.erf(hidden * math.sqrt(0.5)))
        active = (hidden * half).astype(BF16)
        act_ref[rows, :] = active
        slope = half + hidden * jnp.exp(-0.5 * hidden * hidden) * (1.0 / math.sqrt(2.0 * math.pi))
        grad_hidden = (dot_last(grad_rows, down_ref[...]) * slope).astype(BF16)
        dh_ref[rows, :] = grad_hidden
        grad_bias += jnp.sum(grad_hidden.astype(F32), axis=0, keepdims=True)
        out_ref[rows, :] = (out_part_ref[rows, :] + dot(active, down_ref[...])).astype(out_ref.dtype)
        upstream = dot_last(grad_hidden, up_ref[...])
        vectors[0] += jnp.sum(normal * upstream, axis=0, keepdims=True)
        vectors[1] += jnp.sum(upstream, axis=0, keepdims=True)
        dx_ref[rows, :] = (dx_part_ref[rows, :] + norm_back(normal, scale, gain * upstream)).astype(dx_ref.dtype)
    grad_up = dot_rows(nb_ref[...], dh_ref[...])
    grad_down = dot_rows(act_ref[...], xg_ref[:, width:])
    rest = grad_ref.shape[1] - up_rows - down_rows
    tail = jnp.concatenate([grad_bias] + vectors + [jnp.zeros((rest - 3, width), F32)], 0)
    for owner in range(owners):
        grad_ref[owner, :up_rows, :] = grad_up[owner * up_rows : (owner + 1) * up_rows, :]
        grad_ref[owner, up_rows : up_rows + down_rows, :] = grad_down[
            owner * down_rows : (owner + 1) * down_rows, :
        ]
        grad_ref[owner, up_rows + down_rows :, :] = tail


def whole(count):
    return [pl.BlockSpec(memory_space=pltpu.VMEM)] * count


def attention(xg, w_qkv, w_out, vectors, bias, cosine, sine, owners):
    tokens, width = xg.shape[0], xg.shape[1] // 2
    part = w_out.shape[0]
    rows = width // owners + part // owners + 16
    shape = jax.ShapeDtypeStruct
    flops = 2 * tokens * width * part * 12 + 2 * 5 * tokens * tokens * part
    return pl.pallas_call(
        attention_kernel,
        out_shape=(
            shape((tokens, width), F32),
            shape((tokens, width), F32),
            shape((owners, rows, width), F32),
        ),
        in_specs=whole(7),
        out_specs=tuple(whole(3)),
        scratch_shapes=[
            pltpu.VMEM((tokens, width), BF16),
            pltpu.VMEM((tokens, part), BF16),
            pltpu.VMEM((tokens, part), BF16),
            pltpu.VMEM((tokens, part), BF16),
            pltpu.VMEM((tokens, part), BF16),
            pltpu.VMEM((part, tokens), BF16),
            pltpu.VMEM((part, tokens), BF16),
            pltpu.VMEM((tokens, part), BF16),
            pltpu.VMEM((tokens, part), F32),
            pltpu.VMEM((part, tokens), F32),
            pltpu.VMEM((part, tokens), F32),
            pltpu.VMEM((tokens, 3 * part), BF16),
        ],
        compiler_params=PARAMS,
        cost_estimate=pl.CostEstimate(
            flops=4 * flops, bytes_accessed=8 * tokens * width * 4, transcendentals=tokens * tokens * 2
        ),
    )(xg, w_qkv, w_out, vectors, bias, cosine, sine)


def feed_forward(xg, w_up, w_down, vectors, bias, out_part, dx_part, owners):
    tokens, width = xg.shape[0], xg.shape[1] // 2
    hidden_width = w_up.shape[1]
    rows = width // owners + hidden_width // owners + 16
    shape = jax.ShapeDtypeStruct
    return pl.pallas_call(
        mlp_kernel,
        out_shape=(
            shape((tokens, width), F32),
            shape((tokens, width), F32),
            shape((owners, rows, width), F32),
        ),
        in_specs=whole(7),
        out_specs=tuple(whole(3)),
        scratch_shapes=[
            pltpu.VMEM((tokens, width), BF16),
            pltpu.VMEM((tokens, hidden_width), BF16),
            pltpu.VMEM((tokens, hidden_width), BF16),
        ],
        compiler_params=PARAMS,
        cost_estimate=pl.CostEstimate(
            flops=12 * tokens * width * hidden_width,
            bytes_accessed=8 * tokens * width * 4,
            transcendentals=2 * tokens * hidden_width,
        ),
    )(xg, w_up, w_down, vectors, bias, out_part, dx_part)


def rotary(tokens, heads):
    ladder = np.arange(ROT // 2, dtype=np.float32)
    frequency = np.exp(ladder * np.float32(-2.0 * math.log(10000.0) / ROT)).astype(np.float32)
    angles = np.arange(tokens, dtype=np.float32)[:, None] * frequency[None, :]
    cosine = np.ones((tokens, HD), np.float32)
    sine = np.zeros((tokens, HD), np.float32)
    half = ROT // 2
    cosine[:, :half] = cosine[:, half:ROT] = np.cos(angles)
    sine[:, half:ROT] = np.sin(angles)
    sine[:, :half] = -sine[:, half:ROT]
    return np.tile(cosine, (1, heads)), np.tile(sine, (1, heads))


def shards_any(
    owners, groups,
    inputs, cotangent, w_qkv, b_qkv, w_out, b_out, w_up, b_up, w_down, b_down,
    gain_one, shift_one, gain_two, shift_two,
):
    rows, width = w_qkv.shape[0], w_qkv.shape[1] // 3
    hidden = w_up.shape[1]
    down_rows = w_down.shape[0]
    local = inputs.shape[1]
    tokens = local * groups
    part = width // groups
    slice_width = hidden // groups
    dp_rows = rows * groups
    group = lax.axis_index("seq")
    owner = lax.axis_index("dp")

    xg = jnp.concatenate([inputs[0], cotangent[0]], axis=1)
    xg = gather_bits(xg, "seq", groups).reshape(tokens, 2 * width)

    devices = owners * groups
    place = [(f % owners) * groups + f // owners for f in range(devices)]
    out_rows = lax.ppermute(w_out, ("dp", "seq"), [(f, place[f]) for f in range(devices)])

    small = jnp.concatenate(
        [b_qkv.reshape(rows, -1), b_up.reshape(rows, -1)]
        + [v[:, None] for v in (b_out, b_down, gain_one, shift_one, gain_two, shift_two)],
        axis=1,
    )
    n_small = small.shape[1]
    n_up = b_up.shape[0] // rows
    small = jnp.pad(small, ((0, 0), (0, width - 3 * part - n_small)))
    blocks = jnp.concatenate(
        [
            w_qkv.reshape(rows, 3, groups, part).transpose(2, 0, 1, 3).reshape(groups, rows, 3 * part),
            jnp.broadcast_to(small[None], (groups,) + small.shape),
            w_up.reshape(rows, owners, groups, -1).transpose(2, 0, 1, 3).reshape(groups, rows, slice_width),
        ],
        axis=2,
    )
    blocks = swap_bits(blocks, "seq", groups).reshape(dp_rows, width + slice_width)
    first = gather_bits(jnp.concatenate([blocks[:, :width], out_rows], axis=0), "dp", owners)
    second = gather_bits(jnp.concatenate([blocks[:, width:], w_down], axis=0), "dp", owners)

    full_qkv = first[:, :dp_rows, : 3 * part].reshape(width, 3 * part)
    full_out = first[:, dp_rows:, :].reshape(part, width)
    small = first[:, :dp_rows, 3 * part : 3 * part + n_small].reshape(width, n_small).astype(F32)
    bias_qkv = lax.dynamic_index_in_dim(
        small[:, :3].reshape(3, groups, part), group, 1, keepdims=False
    ).reshape(1, 3 * part)
    bias_up = lax.dynamic_index_in_dim(
        small[:, 3 : 3 + n_up].reshape(owners, groups, -1), group, 1, keepdims=False
    ).reshape(1, slice_width)
    vectors = small[:, 3 + n_up :].T
    biases = vectors[0] + vectors[1]
    vectors = jnp.concatenate([vectors[2:], jnp.zeros((4, width), F32)], 0)
    full_up = second[:, :dp_rows, :].reshape(width, slice_width)
    full_down = second[:, dp_rows:, :].reshape(slice_width, width)

    cosine, sine = rotary(tokens, part // HD)
    out_part, dx_part, grad_a = attention(
        xg, full_qkv, full_out, vectors, bias_qkv, jnp.asarray(cosine), jnp.asarray(sine), owners
    )
    out_part, dx_part, grad_b = feed_forward(
        xg, full_up, full_down, vectors, bias_up, out_part, dx_part, owners
    )

    grad_a = scatter_bits(grad_a, "dp", owners)
    grad_b = scatter_bits(grad_b, "dp", owners)
    both = jnp.concatenate([out_part, dx_part], axis=1).reshape(groups, local, 2 * width)
    both = scatter_bits(both, "seq", groups)
    outputs = (inputs[0].astype(F32) + both[:, :width] + biases[None]).astype(BF16)[None]
    grad_inputs = (cotangent[0].astype(F32) + both[:, width:]).astype(BF16)[None]

    own_wout = lax.ppermute(
        grad_a[dp_rows : dp_rows + rows, :], ("dp", "seq"), [(place[f], f) for f in range(devices)]
    )
    tail_a = grad_a[dp_rows + rows :, :]
    tail_b = grad_b[dp_rows + down_rows :, :]
    small = jnp.concatenate([tail_a[:4], tail_b[1:3], jnp.zeros((2, width), F32)], 0)
    send = jnp.concatenate(
        [
            grad_a[:dp_rows, : 3 * part].reshape(groups, rows, 3 * part),
            grad_b[:dp_rows, :].reshape(groups, rows, slice_width),
        ],
        axis=2,
    )
    small = jnp.pad(small, ((0, 0), (0, send.shape[2] - width)))
    send = jnp.concatenate([send, jnp.broadcast_to(small[None], (groups,) + small.shape)], axis=1)
    send = swap_bits(send, "seq", groups)
    own_wqkv = send[:, :rows, : 3 * part].reshape(groups, rows, 3, part).transpose(1, 2, 0, 3).reshape(rows, -1)
    own_wup = (
        send[:, :rows, 3 * part :].reshape(groups, rows, owners, -1).transpose(1, 2, 0, 3).reshape(rows, -1)
    )
    small = send[:, rows:, :width]
    index = owner * groups + group
    own_bqkv = lax.dynamic_slice_in_dim(
        small[:, 0, : 3 * part].reshape(groups, 3, part).transpose(1, 0, 2).reshape(-1),
        index * b_qkv.shape[0],
        b_qkv.shape[0],
    )
    sums = jnp.sum(small, axis=0)
    own = lax.dynamic_slice_in_dim(sums, index * rows, rows, axis=1)
    own_bias = lax.dynamic_slice_in_dim(small[0, 3], index * rows, rows)
    own_bup = lax.dynamic_slice_in_dim(tail_b[0], owner * b_up.shape[0], b_up.shape[0])
    return (
        outputs,
        grad_inputs,
        own_wqkv,
        own_bqkv,
        own_wout,
        own_bias,
        own_wup,
        own_bup,
        grad_b[dp_rows : dp_rows + down_rows, :],
        own_bias,
        own[1],
        own[2],
        own[4],
        own[5],
    )


def reversed_bits(value, count):
    result = 0
    for bit in range(count):
        result = result | (((value >> bit) & 1) << (count - 1 - bit))
    return result


def after(value, *others):
    return lax.optimization_barrier((value,) + others)[0]


def spread(value, axis, size, gates=()):
    value, seen = value[None], []
    for step, bit in enumerate(reversed(range(log2(size)))):
        seen.append(exchange(value, axis, size, bit))
        if bit:
            other = after(seen[-1], *gates[step]) if step < len(gates) else seen[-1]
            value = jnp.concatenate([value, other], 0)
    return (value, seen[-1]), seen


def fold(kept, other):
    total = kept + other.astype(F32)
    half = total.shape[0] // 2
    return total[half:].astype(BF16), total[:half]


def finish(kept, other):
    return kept[0] + other[0].astype(F32)


def call(kernel, outs, scratch, flops, transcendentals, *operands, mib=8, far=0):
    return pl.pallas_call(
        kernel,
        out_shape=tuple(outs),
        in_specs=whole(len(operands) - far)
        + [pl.BlockSpec(memory_space=pltpu.HBM)] * far,
        out_specs=tuple(whole(len(outs))),
        scratch_shapes=scratch,
        compiler_params=pltpu.CompilerParams(vmem_limit_bytes=mib * 1024 * 1024),
        cost_estimate=pl.CostEstimate(flops=1, bytes_accessed=1, transcendentals=0),
    )(*operands)


def fetch(pairs, sems):
    copies = [pltpu.make_async_copy(source, to, sems.at[i]) for i, (source, to) in enumerate(pairs)]
    for copy in copies:
        copy.start()
    for copy in copies:
        copy.wait()


def pack_kernel(*refs):
    count = (len(refs) - 4) // 2
    (sent_ref, kept_ref, block_ref, sems), held = refs[count : count + 4], refs[count + 4 :]
    fetch(tuple(zip(refs[:count], held)), sems)
    qkv_ref, up_ref, out_ref, small = held[0], held[1], held[2], held[3:]
    me = lax.axis_index("seq")
    groups, rows, _ = block_ref.shape
    width = qkv_ref.shape[1] // 3
    part = width // groups
    piece = rows * groups
    owners = up_ref.shape[1] // (groups * piece)
    lines = []
    for line in (small[:2], small[2:]):
        values = [ref[...].reshape(1, ref.shape[0]).astype(F32) for ref in line]
        used = sum(ref.shape[0] for ref in line)
        lines.append(jnp.concatenate(values + [jnp.zeros((1, part - used), F32)], 1))
    lines = jnp.concatenate(lines + [jnp.zeros((rows - 2, part), F32)], 0).astype(BF16)
    for group in range(groups):
        for c in range(3):
            start = c * width + group * part
            block_ref[group, :, c * part : (c + 1) * part] = qkv_ref[:, start : start + part]
        block_ref[group, :, 3 * part : width] = lines
        block_ref[group, :, width + up_ref.shape[1] // groups :] = out_ref[...]
        block_ref[group, :, width : width + up_ref.shape[1] // groups] = jnp.concatenate(
            [
                up_ref[:, (k * groups + group) * piece : (k * groups + group + 1) * piece]
                for k in range(owners)
            ],
            1,
        )
    for half in range(groups // 2):
        kept_ref[half] = block_ref[me ^ (2 * half)]
        sent_ref[half] = block_ref[me ^ (2 * half + 1)]


def payload_kernel(kept_ref, near_ref, far_ref, down_ref, first_ref, second_ref, sem):
    me = lax.axis_index("seq")
    width = down_ref.shape[1]
    part, rows = width // 4, first_ref.shape[0] // 8
    copy = pltpu.make_async_copy(down_ref, second_ref.at[pl.ds(4 * rows, down_ref.shape[0])], sem)
    copy.start()
    hidden = kept_ref.shape[2] - 2 * width
    for step, block in enumerate((kept_ref.at[0], near_ref.at[0], far_ref.at[0], far_ref.at[1])):
        group = me ^ step
        lanes = pl.ds(pl.multiple_of(group * part, part), part)
        second_ref[pl.ds(pl.multiple_of(group * rows, rows), rows), :] = block[:, width : width + hidden]
        for c in range(3):
            first_ref[c * rows : (c + 1) * rows, lanes] = block[:, c * part : (c + 1) * part]
        first_ref[3 * rows : 4 * rows, lanes] = block[:, 3 * part : width]
        first_ref[pl.ds(pl.multiple_of((4 + group) * rows, rows), rows), :] = block[:, width + hidden :]
    copy.wait()


def merge_kernel(bit, mine_ref, other_ref, out_ref):
    last = mine_ref.shape[0] * 2 - out_ref.shape[0]
    part = mine_ref.shape[0] - last
    out_ref[:part, :] = mine_ref[:part, :]
    out_ref[part : 2 * part, :] = other_ref[:part, :]
    same = (lax.axis_index("dp") >> bit) & 1 == (lax.axis_index("seq") >> (bit - 1)) & 1

    @pl.when(same)
    def _():
        out_ref[2 * part :, :] = mine_ref[part:, :]

    @pl.when(jnp.logical_not(same))
    def _():
        out_ref[2 * part :, :] = other_ref[part:, :]


def sources(pair, me):
    half = pair[0].shape[0]
    count = log2(2 * half)
    for slot in range(2 * half):
        ref = pair[slot // half]
        yield ref.at[slot % half], me ^ reversed_bits(slot, count)


def project_kernel(
    first_ref, other_ref, x_ref, y_ref, cos_ref, sin_ref, table_ref,
    xg_ref, na_ref, q_ref, qt_ref, k_ref, v_ref, da_ref, dat_ref, wq_ref, wo_ref, vec_ref,
):
    owner, group = lax.axis_index("dp"), lax.axis_index("seq")
    width = first_ref.shape[1]
    groups = 2 * x_ref.shape[0]
    part = width // groups
    rows = first_ref.shape[0] // 20
    owners = width // (rows * groups)
    local = x_ref.shape[1]
    lines = []
    for slot in range(owners):
        block = (first_ref, other_ref)[slot // 4].at[pl.ds(slot % 4 * 4 * rows, 4 * rows)]
        rank = owner ^ reversed_bits(slot, log2(owners))
        for g in range(groups):
            lanes = slice(g * part, (g + 1) * part)
            to = pl.ds(pl.multiple_of((rank * groups + g) * rows, rows), rows)
            for c in range(3):
                wq_ref[to, c * part : (c + 1) * part] = block[c * rows : (c + 1) * rows, lanes]
            lines.append(block[3 * rows : 4 * rows, lanes].astype(F32)[:8, :])
    for slot, ref in enumerate((first_ref, other_ref)):
        x = (owner & 1) ^ slot
        wo_ref[pl.ds(pl.multiple_of(x * 4 * rows, 4 * rows), 4 * rows), :] = ref[16 * rows :, :]
    devices = owners * groups
    line_one = jnp.concatenate([line[0:1] for line in lines], 0).astype(BF16)
    line_two = jnp.concatenate([line[1:2] for line in lines], 0).astype(BF16)

    def device_of(shape):
        slot = lax.broadcasted_iota(jnp.int32, shape, 0)
        rank = owner ^ reversed_bits(slot // groups, log2(owners))
        return rank * groups + slot % groups

    def place_values(line, lane_of, device_of_column):
        columns = lane_of.shape[1]
        pick = lax.broadcasted_iota(jnp.int32, (line.shape[1], columns), 0) == lane_of
        values = dot(line, jnp.where(pick, 1.0, 0.0).astype(BF16))
        held = device_of((devices, columns)) == device_of_column
        return jnp.sum(jnp.where(held, values, 0.0), axis=0, keepdims=True)

    column = lax.broadcasted_iota(jnp.int32, (1, width), 1)
    own = [place_values(line_two, column % rows + v * rows, column // rows) for v in range(6)]
    piece = rows * groups
    start = 3 * width // devices
    bias_up = place_values(line_one, column % piece + start, column // piece * groups + group)
    lane_of = jnp.concatenate(
        [table_ref[0:1, pl.ds(pl.multiple_of(c * width + group * part, part), part)] for c in range(3)], 1
    )
    owner_of = jnp.concatenate(
        [table_ref[1:2, pl.ds(pl.multiple_of(c * width + group * part, part), part)] for c in range(3)], 1
    )
    bias = place_values(line_one, lane_of, owner_of)
    gain, shift = own[2], own[3]
    vec_ref[...] = jnp.concatenate(
        own[2:] + [own[0] + own[1], bias_up, jnp.zeros((2, width), F32)], 0
    )

    lane = lax.broadcasted_iota(jnp.int32, (local, part), 1)
    turn = lane % HD < ROT // 2

    def partner(value):
        return jnp.where(
            turn, pltpu.roll(value, part - ROT // 2, 1), pltpu.roll(value, ROT // 2, 1)
        )

    for block, rank in sources((x_ref, y_ref), group):
        start = pl.multiple_of(rank * local, local)
        to = pl.ds(start, local)
        both = block[...]
        xg_ref[to, :] = both
        normal, _ = standardize(both[:, :width].astype(F32))
        normed = (normal * gain + shift).astype(BF16)
        na_ref[to, :] = normed
        projected = dot(normed, wq_ref[...]) + bias
        cosine, sine = cos_ref[to, :], sin_ref[to, :]
        query = projected[:, :part]
        query = query * cosine + partner(query) * sine
        key = projected[:, part : 2 * part]
        key = key * cosine + partner(key) * sine
        query = query.astype(BF16).astype(F32) * HD**-0.5
        q_ref[to, :] = query.astype(BF16)
        qt_ref[:, to] = query.T.astype(BF16)
        k_ref[to, :] = key.astype(BF16)
        v_ref[to, :] = projected[:, 2 * part :].astype(BF16)
        grad_att = dot_last(both[:, width:], wo_ref[...]).astype(BF16)
        da_ref[to, :] = grad_att
        dat_ref[:, to] = grad_att.astype(F32).T.astype(BF16)


def attend_kernel(
    xg_ref, na_ref, q_ref, qt_ref, k_ref, v_ref, da_ref, dat_ref, wq_ref, cos_ref, sin_ref,
    att_ref, dp_ref, sent_ref, kept_ref,
    dq_ref, dkt_ref, dvt_ref, gq_ref, go_ref,
):
    owner = lax.axis_index("dp")
    tokens, part = q_ref.shape
    width = na_ref.shape[1]
    groups = width // part
    owners = 2 * sent_ref.shape[0]
    rows = part // owners
    lane = lax.broadcasted_iota(jnp.int32, (BLOCK, part), 1)
    turn = lane % HD < ROT // 2

    def partner(value):
        return jnp.where(
            turn, pltpu.roll(value, part - ROT // 2, 1), pltpu.roll(value, ROT // 2, 1)
        )

    dkt_ref[...] = jnp.zeros_like(dkt_ref)
    dvt_ref[...] = jnp.zeros_like(dvt_ref)
    below = lax.broadcasted_iota(jnp.int32, (BLOCK, BLOCK), 0) >= lax.broadcasted_iota(
        jnp.int32, (BLOCK, BLOCK), 1
    )
    zero = jnp.zeros((), BF16)
    for block in range(tokens // BLOCK):
        at = pl.ds(block * BLOCK, BLOCK)
        seen = (block + 1) * BLOCK
        attended = jnp.zeros((BLOCK, part), F32)
        grad_query = jnp.zeros((BLOCK, part), F32)
        for head in range(part // HD):
            mine = lane // HD == head
            mine_t = lax.broadcasted_iota(jnp.int32, (part, BLOCK), 0) // HD == head
            query = jnp.where(mine, q_ref[at, :], zero)
            grad_att = jnp.where(mine, da_ref[at, :], zero)
            scores = dot_last(query, k_ref[:seen, :])
            last = jnp.where(below, scores[:, seen - BLOCK :], -1e30)
            scores = last if block == 0 else jnp.concatenate([scores[:, : seen - BLOCK], last], 1)
            raised = jnp.exp(scores - jnp.max(scores, axis=-1, keepdims=True))
            probs = raised * (1.0 / jnp.sum(raised, axis=-1, keepdims=True))
            probs_low = probs.astype(BF16)
            attended = jnp.where(mine, dot(probs_low, v_ref[:seen, :]), attended)
            grad_probs = dot_last(grad_att, v_ref[:seen, :])
            inner = jnp.sum(probs * grad_probs, axis=-1, keepdims=True)
            grad_scores = (probs * (grad_probs - inner)).astype(BF16)
            grad_query = jnp.where(mine, dot(grad_scores, k_ref[:seen, :]), grad_query)
            query_t = jnp.where(mine_t, qt_ref[:, at], zero)
            grad_att_t = jnp.where(mine_t, dat_ref[:, at], zero)
            dkt_ref[:, :seen] += dot(query_t, grad_scores)
            dvt_ref[:, :seen] += dot(grad_att_t, probs_low)
        att_ref[at, :] = attended.astype(BF16)
        dq_ref[at, :] = grad_query * HD**-0.5

    vectors = [jnp.zeros((1, width), F32) for _ in range(3)]
    grad_bias = jnp.zeros((1, 3 * part), F32)
    for block in range(tokens // BLOCK):
        at = pl.ds(block * BLOCK, BLOCK)
        cosine, sine = cos_ref[at, :], sin_ref[at, :]
        grad_query = dq_ref[at, :]
        grad_query = grad_query * cosine - partner(grad_query) * sine
        grad_key = dkt_ref[:, at].T
        grad_key = grad_key * cosine - partner(grad_key) * sine
        grad_proj = jnp.concatenate([grad_query, grad_key, dvt_ref[:, at].T], 1).astype(BF16)
        dp_ref[at, :] = grad_proj
        grad_bias += jnp.sum(grad_proj.astype(F32), axis=0, keepdims=True)
        upstream = dot_last(grad_proj, wq_ref[...])
        normal, _ = standardize(xg_ref[at, :width].astype(F32))
        vectors[0] += jnp.sum(normal * upstream, axis=0, keepdims=True)
        vectors[1] += jnp.sum(upstream, axis=0, keepdims=True)
        vectors[2] += jnp.sum(xg_ref[at, width:].astype(F32), axis=0, keepdims=True)

    gq_ref[...] = dot_rows(na_ref[...], dp_ref[...])
    go_ref[...] = dot_rows(att_ref[...], xg_ref[:, width:])
    tail = jnp.concatenate(
        [jnp.concatenate([grad_bias, jnp.zeros((1, width - 3 * part), F32)], 1)]
        + vectors
        + [jnp.zeros((rows - 4, width), F32)],
        0,
    )
    for ref, rank in sources((kept_ref, sent_ref), owner):
        kind = ref.dtype
        for g in range(groups):
            at = pl.ds(pl.multiple_of((rank * groups + g) * rows, rows), rows)
            for c in range(3):
                ref[c * rows : (c + 1) * rows, g * part : (g + 1) * part] = gq_ref[
                    at, c * part : (c + 1) * part
                ].astype(kind)
        ref[3 * rows : 4 * rows, :] = go_ref[pl.ds(pl.multiple_of(rank * rows, rows), rows), :].astype(kind)
        ref[4 * rows :, :] = tail.astype(kind)


def hidden_kernel(
    second_ref, other_ref, xg_ref, vec_ref,
    act_ref, dh_ref, up_ref, down_ref, sent_ref, kept_ref,
    nb_ref, gu_ref,
):
    owner = lax.axis_index("dp")
    tokens, hidden_width = act_ref.shape
    width = vec_ref.shape[1]
    rows = second_ref.shape[1] // 2
    for block, rank in sources((second_ref, other_ref), owner):
        at = pl.ds(pl.multiple_of(rank * rows, rows), rows)
        up_ref[at, :] = block[:rows, :]
        down_ref[at, :] = block[rows:, :]
    gain, shift, bias = vec_ref[2:3, :], vec_ref[3:4, :], vec_ref[5:6, :]
    vectors = [jnp.zeros((1, width), F32) for _ in range(2)]
    grad_bias = jnp.zeros((1, hidden_width), F32)
    for block in range(tokens // BLOCK):
        at = pl.ds(block * BLOCK, BLOCK)
        normal, _ = standardize(xg_ref[at, :width].astype(F32))
        normed = (normal * gain + shift).astype(BF16)
        nb_ref[at, :] = normed
        hidden = dot(normed, up_ref[...]) + bias
        half = 0.5 * (1.0 + lax.erf(hidden * math.sqrt(0.5)))
        act_ref[at, :] = (hidden * half).astype(BF16)
        slope = half + hidden * jnp.exp(-0.5 * hidden * hidden) * (1.0 / math.sqrt(2.0 * math.pi))
        grad_hidden = (dot_last(xg_ref[at, width:], down_ref[...]) * slope).astype(BF16)
        dh_ref[at, :] = grad_hidden
        grad_bias += jnp.sum(grad_hidden.astype(F32), axis=0, keepdims=True)
        upstream = dot_last(grad_hidden, up_ref[...])
        vectors[0] += jnp.sum(normal * upstream, axis=0, keepdims=True)
        vectors[1] += jnp.sum(upstream, axis=0, keepdims=True)
    gu_ref[...] = dot_rows(nb_ref[...], dh_ref[...])
    extra = sent_ref.shape[1] - rows
    tail = jnp.concatenate([grad_bias] + vectors + [jnp.zeros((extra - 3, width), F32)], 0)
    for ref, rank in sources((kept_ref, sent_ref), owner):
        ref[:rows, :] = gu_ref[pl.ds(pl.multiple_of(rank * rows, rows), rows), :].astype(ref.dtype)
        ref[rows:, :] = tail.astype(ref.dtype)


def down_kernel(act_ref, xg_ref, sent_ref, kept_ref, gd_ref):
    width = sent_ref.shape[2]
    rows = sent_ref.shape[1]
    gd_ref[...] = dot_rows(act_ref[...], xg_ref[:, width:])
    for ref, rank in sources((kept_ref, sent_ref), lax.axis_index("dp")):
        ref[...] = gd_ref[pl.ds(pl.multiple_of(rank * rows, rows), rows), :].astype(ref.dtype)


def join_kernel(
    xg_ref, att_ref, wo_ref, act_ref, down_ref, vec_ref, dp_ref, wq_ref, dh_ref, up_ref,
    sent_ref, kept_ref,
):
    group = lax.axis_index("seq")
    local = sent_ref.shape[1]
    width = wo_ref.shape[1]
    gain_one, gain_two, bias = vec_ref[0:1, :], vec_ref[2:3, :], vec_ref[4:5, :]
    for step in range(2 * sent_ref.shape[0]):
        at = pl.ds(pl.multiple_of((group ^ step) * local, local), local)
        ref = (kept_ref, sent_ref)[step % 2].at[step // 2]
        out = dot(att_ref[at, :], wo_ref[...]) + dot(act_ref[at, :], down_ref[...])
        rows_in = xg_ref[at, :width].astype(F32)
        normal, scale = standardize(rows_in)
        inner = gain_one * dot_last(dp_ref[at, :], wq_ref[...]) + gain_two * dot_last(dh_ref[at, :], up_ref[...])
        grad = norm_back(normal, scale, inner)
        if step == 0:
            out = out + rows_in + bias
            grad = grad + xg_ref[at, width:].astype(F32)
        ref[:, :width] = out.astype(ref.dtype)
        ref[:, width:] = grad.astype(ref.dtype)


def deal_kernel(a_ref, b_ref, sent_ref, kept_ref):
    me = lax.axis_index("seq")
    width = a_ref.shape[1]
    part = width // 4
    rows = a_ref.shape[0] // 5
    kind = sent_ref.dtype
    small = jnp.concatenate(
        [a_ref[4 * rows : 4 * rows + 3, :], b_ref[4 * rows + 1 : 4 * rows + 3, :], jnp.zeros((rows - 5, width), F32)], 0
    )
    for step in range(4):
        group = me ^ step
        ref = (kept_ref, sent_ref)[step % 2].at[step // 2]
        lanes = pl.ds(pl.multiple_of(group * part, part), part)
        for c in range(3):
            ref[:rows, c * part : (c + 1) * part] = a_ref[c * rows : (c + 1) * rows, lanes].astype(kind)
        ref[:rows, 3 * part :] = b_ref[pl.ds(pl.multiple_of(group * rows, rows), rows), :].astype(kind)
        ref[rows:, :width] = small.astype(kind)
        ref[rows:, width:] = jnp.zeros((rows, 3 * part), kind)


def collect_kernel(
    kept_ref, near_ref, far_ref, a_ref, b_ref, out_ref,
    qkv_ref, up_ref, wout_ref, bqkv_ref, bias_ref, twin_ref, bup_ref, gain_one_ref, shift_one_ref, gain_two_ref, shift_two_ref,
    block_ref,
):
    me = lax.axis_index("seq")
    place = lax.axis_index("dp") * 4 + me
    rows = qkv_ref.shape[0]
    width = qkv_ref.shape[1] // 3
    part = width // 4
    piece = 4 * rows
    for step, block in enumerate((kept_ref.at[0], near_ref.at[0], far_ref.at[0], far_ref.at[1])):
        block_ref[me ^ step] = block[...].astype(F32)
    for g in range(4):
        for c in range(3):
            qkv_ref[:, c * width + g * part : c * width + (g + 1) * part] = block_ref[
                g, :rows, c * part : (c + 1) * part
            ]
    for k in range(up_ref.shape[1] // (4 * piece)):
        start = 3 * part + k * piece
        up_ref[:, 4 * k * piece : 4 * (k + 1) * piece] = jnp.concatenate(
            [block_ref[g, :rows, start : start + piece] for g in range(4)], 1
        )
    wout_ref[...] = out_ref[...]

    def own(values, ref, index):
        size, count = values.shape[1], ref.shape[0]
        values = pltpu.roll(values, (size - index * count) % size, 1)[0:1, :count]
        ref[...] = values.reshape(count)

    sums = sum(block_ref[g, rows : rows + 8, :width] for g in range(4))
    for i, ref in enumerate((gain_one_ref, shift_one_ref, gain_two_ref, shift_two_ref)):
        own(sums[i + 1 : i + 2], ref, place)
    bias = jnp.concatenate(
        [block_ref[g, rows : rows + 1, c * part : (c + 1) * part] for c in range(3) for g in range(4)], 1
    )
    own(bias, bqkv_ref, place)
    own(a_ref[4 * rows + 3 : 4 * rows + 4, :], bias_ref, place)
    twin_ref[...] = bias_ref[...]
    own(b_ref[4 * rows : 4 * rows + 1, :], bup_ref, lax.axis_index("dp"))


def shards(
    owners, groups,
    inputs, cotangent, w_qkv, b_qkv, w_out, b_out, w_up, b_up, w_down, b_down,
    gain_one, shift_one, gain_two, shift_two,
):
    rows, width = w_qkv.shape[0], w_qkv.shape[1] // 3
    hidden = w_up.shape[1] // groups
    local = inputs.shape[1]
    if rows % 16 or groups != 4 or owners != 8 or local != BLOCK or hidden != width:
        return shards_any(
            owners, groups, inputs, cotangent, w_qkv, b_qkv, w_out, b_out, w_up, b_up, w_down, b_down,
            gain_one, shift_one, gain_two, shift_two,
        )
    tokens = local * groups
    part = width // groups
    devices = owners * groups
    half = owners // 2
    heads = part // HD
    shape = jax.ShapeDtypeStruct

    target = [(f % owners) * groups + f // owners for f in range(devices)]

    block = shape((2, rows, 2 * width + hidden), BF16)
    params = (w_qkv, w_up, w_out, b_qkv, b_up, b_out, b_down, gain_one, shift_one, gain_two, shift_two)
    sent, kept = call(
        pack_kernel,
        (block, block),
        [pltpu.VMEM((groups, rows, 2 * width + hidden), BF16), pltpu.SemaphoreType.DMA((len(params),))]
        + [pltpu.VMEM(p.shape, BF16) for p in params],
        0, 0, *params, mib=63, far=len(params),
    )
    near = exchange(sent, "seq", groups, 0)
    far = exchange(jnp.stack([kept[1], near[1]]), "seq", groups, 1)
    first, second = call(
        payload_kernel,
        (shape((8 * rows, width), BF16), shape((4 * rows + w_down.shape[0], width), BF16)),
        [pltpu.SemaphoreType.DMA], 0, 0, kept, near, far, w_down, mib=4, far=1,
    )
    def merged(bit, mine, other):
        count = mine.shape[0] - 4 * rows
        out = shape((2 * count + 4 * rows, width), BF16)
        return call(functools.partial(merge_kernel, bit), (out,), [], 0, 0, mine, other, mib=4)[0]

    x = jnp.concatenate([after(inputs[0], far), cotangent[0]], axis=1)[None]
    x_other = exchange(x, "seq", groups, 1)
    other = exchange(first, "dp", owners, 2)
    second = after(second, other)[None]
    first = merged(2, first, other)
    other, second_other = exchange(first, "dp", owners, 1), exchange(second, "dp", owners, 2)
    other, second_other, x_other = lax.optimization_barrier((other, second_other, x_other))
    first, second = merged(1, first, other), jnp.concatenate([second, second_other], 0)
    x = jnp.concatenate([x, x_other], 0)
    first = (first, exchange(first, "dp", owners, 0))
    x_pair = (x, exchange(x, "seq", groups, 0))
    second_other = exchange(second, "dp", owners, 1)
    second = jnp.concatenate([second, after(second_other, first[1])], 0)
    second = (second, exchange(second, "dp", owners, 0))

    cosine, sine = (jnp.asarray(t) for t in rotary(tokens, heads))
    column = np.arange(3 * width, dtype=np.int32)
    own = 3 * width // devices
    table = np.zeros((8, 3 * width), np.int32)
    table[0], table[1] = column % own, column // own
    wide, narrow, turned = shape((tokens, width), BF16), shape((tokens, part), BF16), shape((part, tokens), BF16)
    xg, normed_a, query, query_t, key, value, grad_att, grad_att_t, full_qkv, full_out, vectors = call(
        project_kernel,
        (shape((tokens, 2 * width), BF16), wide, narrow, turned, narrow, narrow, narrow, turned)
        + (shape((width, 3 * part), BF16), shape((part, width), BF16), shape((8, width), F32)),
        [], 2 * tokens * width * 4 * part, 0,
        *first, *x_pair, cosine, sine, jnp.asarray(table),
    )
    chunk = 5 * rows
    attended, grad_proj, sent_a, kept_a = call(
        attend_kernel,
        (narrow, shape((tokens, 3 * part), BF16), shape((half, chunk, width), BF16), shape((half, chunk, width), F32)),
        [
            pltpu.VMEM((tokens, part), F32),
            pltpu.VMEM((part, tokens), F32),
            pltpu.VMEM((part, tokens), F32),
            pltpu.VMEM((width, 3 * part), F32),
            pltpu.VMEM((part, width), F32),
        ],
        8 * tokens * tokens * part * 6, 2 * tokens * tokens,
        xg, normed_a, after(query, second_other), query_t, key, value, grad_att, grad_att_t, full_qkv, cosine, sine,
        mib=16,
    )
    other_a = exchange(sent_a, "dp", owners, 0)
    active, grad_hidden, full_up, full_down, sent_u, kept_u = call(
        hidden_kernel,
        (wide, wide, shape((width, hidden), BF16), shape((hidden, width), BF16))
        + (shape((half, chunk, width), BF16), shape((half, chunk, width), F32)),
        [
            pltpu.VMEM((tokens, width), BF16),
            pltpu.VMEM((width, hidden), F32),
        ],
        8 * tokens * width * hidden, 2 * tokens * hidden,
        *second, xg, after(vectors, attended),
        mib=16,
    )
    other_u = exchange(sent_u, "dp", owners, 0)
    down_rows = w_down.shape[0]
    sent_d, kept_d = call(
        down_kernel,
        (shape((half, down_rows, width), BF16), shape((half, down_rows, width), F32)),
        [pltpu.VMEM((hidden, width), F32)],
        2 * tokens * width * hidden, 0,
        after(active, other_a), xg,
    )
    other_d = exchange(sent_d, "dp", owners, 0)
    sent_x, kept_x = call(
        join_kernel,
        (shape((2, local, 2 * width), BF16), shape((2, local, 2 * width), F32)),
        [],
        4 * tokens * width * hidden, 0,
        xg, attended, full_out, active, full_down, vectors,
        grad_proj, full_qkv, grad_hidden, full_up,
    )
    steps = log2(owners)
    for bit in range(1, steps):
        sent_a, kept_a = fold(kept_a, other_a)
        other_a = exchange(sent_a, "dp", owners, bit)
    grad_a = finish(kept_a, other_a)
    other_x = exchange(sent_x, "seq", groups, 0)
    sent_x, kept_x = fold(kept_x, other_x)
    other_out = exchange(sent_x[..., :width], "seq", groups, 1)
    other_grad = exchange(after(sent_x[..., width:], other_out), "seq", groups, 1)
    outputs = finish(kept_x[..., :width], other_out).astype(BF16)[None]
    grad_inputs = finish(kept_x[..., width:], other_grad).astype(BF16)[None]
    for bit in range(1, steps):
        sent_u, kept_u = fold(kept_u, other_u)
        sent_u = sent_u if bit == 1 else after(sent_u, other_out)
        other_u = exchange(sent_u, "dp", owners, bit)
    grad_u, near_d = finish(kept_u, other_u), None
    for bit in range(1, steps):
        sent_d, kept_d = fold(kept_d, other_d)
        other_d = exchange(sent_d, "dp", owners, bit)
        near_d = near_d if bit > 1 else other_d
    grad_d = finish(kept_d, other_d)
    own_wout = lax.ppermute(
        grad_a[3 * rows : 4 * rows, :], ("dp", "seq"), [(target[f], f) for f in range(devices)]
    )
    block = shape((2, 2 * rows, 3 * part + hidden), BF16)
    sent, kept = call(deal_kernel, (block, block), [], 0, 0, grad_a, after(grad_u, other_grad, near_d))
    near = exchange(sent, "seq", groups, 0)
    far = exchange(jnp.stack([kept[1], near[1]]), "seq", groups, 1)
    vector = shape((rows,), F32)
    own_wqkv, own_wup, own_wout, own_bqkv, own_bias, twin_bias, own_bup, *own = call(
        collect_kernel,
        (shape(w_qkv.shape, F32), shape(w_up.shape, F32), shape(w_out.shape, F32))
        + (shape(b_qkv.shape, F32), vector, vector, shape(b_up.shape, F32), vector, vector, vector, vector),
        [pltpu.VMEM((groups, 2 * rows, 3 * part + hidden), F32)],
        0, 0, kept, near, far, grad_a, grad_u, own_wout,
    )
    return (
        outputs,
        grad_inputs,
        own_wqkv,
        own_bqkv,
        own_wout,
        own_bias,
        own_wup,
        own_bup,
        grad_d,
        twin_bias,
        *own,
    )


def solution(mesh):
    rows = P("dp", "seq", None)
    matrix, vector = P(("dp", "seq"), None), P(("dp", "seq"))
    weights = (matrix, vector) * 4
    return jax.shard_map(
        functools.partial(shards, mesh.shape["dp"], mesh.shape["seq"]),
        mesh=mesh,
        in_specs=(rows, rows) + weights + (vector,) * 4,
        out_specs=(rows, rows) + weights + (vector,) * 4,
        check_vma=False,
    )
```

```python
import functools
import math

import jax
import jax.numpy as jnp
import numpy as np
from jax import lax
from jax.experimental import pallas as pl
from jax.experimental.pallas import tpu as pltpu
from jax.sharding import PartitionSpec as P

HD = 64
ROT = 16
EPS = 1e-05
BLOCK = 256
F32 = jnp.float32
BF16 = jnp.bfloat16
PARAMS = pltpu.CompilerParams(vmem_limit_bytes=48 * 1024 * 1024)


def log2(count):
    assert count & (count - 1) == 0
    return count.bit_length() - 1


def exchange(value, axis, size, bit):
    return lax.ppermute(value, axis, [(i, i ^ (1 << bit)) for i in range(size)])


def flag_of(axis, bit):
    return (lax.axis_index(axis) >> bit) & 1 == 1


def gather_bits(value, axis, size):
    shape = value.shape
    for done, bit in enumerate(reversed(range(log2(size)))):
        other = exchange(value, axis, size, bit)
        upper = flag_of(axis, bit)
        value = jnp.where(
            upper,
            jnp.stack([other, value], done),
            jnp.stack([value, other], done),
        )
    return value.reshape((size,) + shape)


def swap_bits(blocks, axis, size):
    count = log2(size)
    rest = blocks.shape[1:]
    value = blocks.reshape((2,) * count + rest)
    for bit in range(count):
        place = count - 1 - bit
        low = lax.index_in_dim(value, 0, place, keepdims=False)
        high = lax.index_in_dim(value, 1, place, keepdims=False)
        upper = flag_of(axis, bit)
        other = exchange(jnp.where(upper, low, high), axis, size, bit)
        value = jnp.stack([jnp.where(upper, other, low), jnp.where(upper, high, other)], place)
    return value.reshape((size,) + rest)


def scatter_bits(blocks, axis, size):
    count = log2(size)
    rest = blocks.shape[1:]
    value = blocks.reshape((2,) * count + rest)
    for bit in range(count):
        place = count - 1 - bit
        low = lax.index_in_dim(value, 0, place, keepdims=False)
        high = lax.index_in_dim(value, 1, place, keepdims=False)
        upper = flag_of(axis, bit)
        sent = jnp.where(upper, low, high).astype(BF16)
        value = jnp.where(upper, high, low).astype(F32) + exchange(sent, axis, size, bit).astype(F32)
    return value


def dot(left, right):
    return lax.dot_general(left, right, (((1,), (0,)), ((), ())), preferred_element_type=F32)


def dot_rows(left, right):
    return lax.dot_general(left, right, (((0,), (0,)), ((), ())), preferred_element_type=F32)


def dot_last(left, right):
    return lax.dot_general(left, right, (((1,), (1,)), ((), ())), preferred_element_type=F32)


def standardize(rows):
    average = jnp.mean(rows, axis=-1, keepdims=True)
    centered = rows - average
    variance = jnp.mean(centered * centered, axis=-1, keepdims=True)
    scale = lax.rsqrt(variance + EPS)
    return centered * scale, scale


def norm_back(normal, scale, inner):
    first = jnp.mean(inner, axis=-1, keepdims=True)
    second = jnp.mean(inner * normal, axis=-1, keepdims=True)
    return scale * (inner - first - normal * second)


def attention_kernel(
    xg_ref, wq_ref, wo_ref, vec_ref, bias_ref, cos_ref, sin_ref,
    out_ref, dx_ref, grad_ref,
    na_ref, q_ref, k_ref, v_ref, da_ref, qt_ref, dat_ref, att_ref, dq_ref, dkt_ref, dvt_ref, dp_ref,
):
    tokens = xg_ref.shape[0]
    width = xg_ref.shape[1] // 2
    part = wo_ref.shape[0]
    heads = part // HD
    owners, _, _ = grad_ref.shape
    own_rows = width // owners
    out_rows = part // owners
    gain = vec_ref[0:1, :]
    shift = vec_ref[1:2, :]
    lane = lax.broadcasted_iota(jnp.int32, (BLOCK, part), 1)
    turn = lane % HD < ROT // 2

    def partner(value):
        return jnp.where(
            turn, pltpu.roll(value, part - ROT // 2, 1), pltpu.roll(value, ROT // 2, 1)
        )

    for block in range(tokens // BLOCK):
        rows = pl.ds(block * BLOCK, BLOCK)
        normal, _ = standardize(xg_ref[rows, :width].astype(F32))
        normed = (normal * gain + shift).astype(BF16)
        na_ref[rows, :] = normed
        projected = dot(normed, wq_ref[...]) + bias_ref[...]
        cosine, sine = cos_ref[rows, :], sin_ref[rows, :]
        query = projected[:, :part]
        query = query * cosine + partner(query) * sine
        key = projected[:, part : 2 * part]
        key = key * cosine + partner(key) * sine
        query = query.astype(BF16).astype(F32) * HD**-0.5
        q_ref[rows, :] = query.astype(BF16)
        qt_ref[:, rows] = query.T.astype(BF16)
        k_ref[rows, :] = key.astype(BF16)
        v_ref[rows, :] = projected[:, 2 * part :].astype(BF16)
        grad_att = dot_last(xg_ref[rows, width:], wo_ref[...]).astype(BF16)
        da_ref[rows, :] = grad_att
        dat_ref[:, rows] = grad_att.astype(F32).T.astype(BF16)

    dkt_ref[...] = jnp.zeros_like(dkt_ref)
    dvt_ref[...] = jnp.zeros_like(dvt_ref)
    below = lax.broadcasted_iota(jnp.int32, (BLOCK, BLOCK), 0) >= lax.broadcasted_iota(
        jnp.int32, (BLOCK, BLOCK), 1
    )
    zero = jnp.zeros((), BF16)
    for block in range(tokens // BLOCK):
        rows = pl.ds(block * BLOCK, BLOCK)
        seen = (block + 1) * BLOCK
        attended = jnp.zeros((BLOCK, part), F32)
        grad_query = jnp.zeros((BLOCK, part), F32)
        for head in range(heads):
            mine = lane // HD == head
            mine_t = lax.broadcasted_iota(jnp.int32, (part, BLOCK), 0) // HD == head
            query = jnp.where(mine, q_ref[rows, :], zero)
            grad_att = jnp.where(mine, da_ref[rows, :], zero)
            scores = dot_last(query, k_ref[:seen, :])
            last = jnp.where(below, scores[:, seen - BLOCK :], -1e30)
            scores = last if block == 0 else jnp.concatenate([scores[:, : seen - BLOCK], last], 1)
            raised = jnp.exp(scores - jnp.max(scores, axis=-1, keepdims=True))
            probs = raised * (1.0 / jnp.sum(raised, axis=-1, keepdims=True))
            probs_low = probs.astype(BF16)
            attended = jnp.where(mine, dot(probs_low, v_ref[:seen, :]), attended)
            grad_probs = dot_last(grad_att, v_ref[:seen, :])
            inner = jnp.sum(probs * grad_probs, axis=-1, keepdims=True)
            grad_scores = (probs * (grad_probs - inner)).astype(BF16)
            grad_query = jnp.where(mine, dot(grad_scores, k_ref[:seen, :]), grad_query)
            query_t = jnp.where(mine_t, qt_ref[:, rows], zero)
            grad_att_t = jnp.where(mine_t, dat_ref[:, rows], zero)
            dkt_ref[:, :seen] += dot(query_t, grad_scores)
            dvt_ref[:, :seen] += dot(grad_att_t, probs_low)
        att_ref[rows, :] = attended.astype(BF16)
        dq_ref[rows, :] = grad_query * HD**-0.5

    vectors = [jnp.zeros((1, width), F32) for _ in range(3)]
    grad_bias = jnp.zeros((1, 3 * part), F32)
    for block in range(tokens // BLOCK):
        rows = pl.ds(block * BLOCK, BLOCK)
        cosine, sine = cos_ref[rows, :], sin_ref[rows, :]
        grad_query = dq_ref[rows, :]
        grad_query = grad_query * cosine - partner(grad_query) * sine
        grad_key = dkt_ref[:, rows].T
        grad_key = grad_key * cosine - partner(grad_key) * sine
        grad_value = dvt_ref[:, rows].T
        grad_proj = jnp.concatenate([grad_query, grad_key, grad_value], 1).astype(BF16)
        dp_ref[rows, :] = grad_proj
        grad_bias += jnp.sum(grad_proj.astype(F32), axis=0, keepdims=True)
        out_ref[rows, :] = dot(att_ref[rows, :], wo_ref[...])
        upstream = dot_last(grad_proj, wq_ref[...])
        normal, scale = standardize(xg_ref[rows, :width].astype(F32))
        vectors[0] += jnp.sum(normal * upstream, axis=0, keepdims=True)
        vectors[1] += jnp.sum(upstream, axis=0, keepdims=True)
        vectors[2] += jnp.sum(xg_ref[rows, width:].astype(F32), axis=0, keepdims=True)
        dx_ref[rows, :] = norm_back(normal, scale, gain * upstream)

    grad_qkv = dot_rows(na_ref[...], dp_ref[...])
    grad_out = dot_rows(att_ref[...], xg_ref[:, width:])
    rest = grad_ref.shape[1] - own_rows - out_rows
    tail = jnp.concatenate(
        [jnp.concatenate([grad_bias, jnp.zeros((1, width - 3 * part), F32)], 1)]
        + vectors
        + [jnp.zeros((rest - 4, width), F32)],
        0,
    )
    for owner in range(owners):
        grad_ref[owner, :own_rows, : 3 * part] = grad_qkv[owner * own_rows : (owner + 1) * own_rows, :]
        grad_ref[owner, :own_rows, 3 * part :] = jnp.zeros((own_rows, width - 3 * part), F32)
        grad_ref[owner, own_rows : own_rows + out_rows, :] = grad_out[
            owner * out_rows : (owner + 1) * out_rows, :
        ]
        grad_ref[owner, own_rows + out_rows :, :] = tail


def mlp_kernel(
    xg_ref, up_ref, down_ref, vec_ref, bias_ref, out_part_ref, dx_part_ref,
    out_ref, dx_ref, grad_ref,
    nb_ref, act_ref, dh_ref,
):
    tokens = xg_ref.shape[0]
    width = xg_ref.shape[1] // 2
    hidden_width = up_ref.shape[1]
    owners = grad_ref.shape[0]
    up_rows = width // owners
    down_rows = hidden_width // owners
    gain = vec_ref[2:3, :]
    shift = vec_ref[3:4, :]
    vectors = [jnp.zeros((1, width), F32) for _ in range(2)]
    grad_bias = jnp.zeros((1, hidden_width), F32)
    for block in range(tokens // BLOCK):
        rows = pl.ds(block * BLOCK, BLOCK)
        grad_rows = xg_ref[rows, width:]
        normal, scale = standardize(xg_ref[rows, :width].astype(F32))
        normed = (normal * gain + shift).astype(BF16)
        nb_ref[rows, :] = normed
        hidden = dot(normed, up_ref[...]) + bias_ref[...]
        half = 0.5 * (1.0 + lax.erf(hidden * math.sqrt(0.5)))
        active = (hidden * half).astype(BF16)
        act_ref[rows, :] = active
        slope = half + hidden * jnp.exp(-0.5 * hidden * hidden) * (1.0 / math.sqrt(2.0 * math.pi))
        grad_hidden = (dot_last(grad_rows, down_ref[...]) * slope).astype(BF16)
        dh_ref[rows, :] = grad_hidden
        grad_bias += jnp.sum(grad_hidden.astype(F32), axis=0, keepdims=True)
        out_ref[rows, :] = (out_part_ref[rows, :] + dot(active, down_ref[...])).astype(out_ref.dtype)
        upstream = dot_last(grad_hidden, up_ref[...])
        vectors[0] += jnp.sum(normal * upstream, axis=0, keepdims=True)
        vectors[1] += jnp.sum(upstream, axis=0, keepdims=True)
        dx_ref[rows, :] = (dx_part_ref[rows, :] + norm_back(normal, scale, gain * upstream)).astype(dx_ref.dtype)
    grad_up = dot_rows(nb_ref[...], dh_ref[...])
    grad_down = dot_rows(act_ref[...], xg_ref[:, width:])
    rest = grad_ref.shape[1] - up_rows - down_rows
    tail = jnp.concatenate([grad_bias] + vectors + [jnp.zeros((rest - 3, width), F32)], 0)
    for owner in range(owners):
        grad_ref[owner, :up_rows, :] = grad_up[owner * up_rows : (owner + 1) * up_rows, :]
        grad_ref[owner, up_rows : up_rows + down_rows, :] = grad_down[
            owner * down_rows : (owner + 1) * down_rows, :
        ]
        grad_ref[owner, up_rows + down_rows :, :] = tail


def whole(count):
    return [pl.BlockSpec(memory_space=pltpu.VMEM)] * count


def attention(xg, w_qkv, w_out, vectors, bias, cosine, sine, owners):
    tokens, width = xg.shape[0], xg.shape[1] // 2
    part = w_out.shape[0]
    rows = width // owners + part // owners + 16
    shape = jax.ShapeDtypeStruct
    flops = 2 * tokens * width * part * 12 + 2 * 5 * tokens * tokens * part
    return pl.pallas_call(
        attention_kernel,
        out_shape=(
            shape((tokens, width), F32),
            shape((tokens, width), F32),
            shape((owners, rows, width), F32),
        ),
        in_specs=whole(7),
        out_specs=tuple(whole(3)),
        scratch_shapes=[
            pltpu.VMEM((tokens, width), BF16),
            pltpu.VMEM((tokens, part), BF16),
            pltpu.VMEM((tokens, part), BF16),
            pltpu.VMEM((tokens, part), BF16),
            pltpu.VMEM((tokens, part), BF16),
            pltpu.VMEM((part, tokens), BF16),
            pltpu.VMEM((part, tokens), BF16),
            pltpu.VMEM((tokens, part), BF16),
            pltpu.VMEM((tokens, part), F32),
            pltpu.VMEM((part, tokens), F32),
            pltpu.VMEM((part, tokens), F32),
            pltpu.VMEM((tokens, 3 * part), BF16),
        ],
        compiler_params=PARAMS,
        cost_estimate=pl.CostEstimate(
            flops=4 * flops, bytes_accessed=8 * tokens * width * 4, transcendentals=tokens * tokens * 2
        ),
    )(xg, w_qkv, w_out, vectors, bias, cosine, sine)


def feed_forward(xg, w_up, w_down, vectors, bias, out_part, dx_part, owners):
    tokens, width = xg.shape[0], xg.shape[1] // 2
    hidden_width = w_up.shape[1]
    rows = width // owners + hidden_width // owners + 16
    shape = jax.ShapeDtypeStruct
    return pl.pallas_call(
        mlp_kernel,
        out_shape=(
            shape((tokens, width), F32),
            shape((tokens, width), F32),
            shape((owners, rows, width), F32),
        ),
        in_specs=whole(7),
        out_specs=tuple(whole(3)),
        scratch_shapes=[
            pltpu.VMEM((tokens, width), BF16),
            pltpu.VMEM((tokens, hidden_width), BF16),
            pltpu.VMEM((tokens, hidden_width), BF16),
        ],
        compiler_params=PARAMS,
        cost_estimate=pl.CostEstimate(
            flops=12 * tokens * width * hidden_width,
            bytes_accessed=8 * tokens * width * 4,
            transcendentals=2 * tokens * hidden_width,
        ),
    )(xg, w_up, w_down, vectors, bias, out_part, dx_part)


def rotary(tokens, heads):
    ladder = np.arange(ROT // 2, dtype=np.float32)
    frequency = np.exp(ladder * np.float32(-2.0 * math.log(10000.0) / ROT)).astype(np.float32)
    angles = np.arange(tokens, dtype=np.float32)[:, None] * frequency[None, :]
    cosine = np.ones((tokens, HD), np.float32)
    sine = np.zeros((tokens, HD), np.float32)
    half = ROT // 2
    cosine[:, :half] = cosine[:, half:ROT] = np.cos(angles)
    sine[:, half:ROT] = np.sin(angles)
    sine[:, :half] = -sine[:, half:ROT]
    return np.tile(cosine, (1, heads)), np.tile(sine, (1, heads))


def shards_any(
    owners, groups,
    inputs, cotangent, w_qkv, b_qkv, w_out, b_out, w_up, b_up, w_down, b_down,
    gain_one, shift_one, gain_two, shift_two,
):
    rows, width = w_qkv.shape[0], w_qkv.shape[1] // 3
    hidden = w_up.shape[1]
    down_rows = w_down.shape[0]
    local = inputs.shape[1]
    tokens = local * groups
    part = width // groups
    slice_width = hidden // groups
    dp_rows = rows * groups
    group = lax.axis_index("seq")
    owner = lax.axis_index("dp")

    xg = jnp.concatenate([inputs[0], cotangent[0]], axis=1)
    xg = gather_bits(xg, "seq", groups).reshape(tokens, 2 * width)

    devices = owners * groups
    place = [(f % owners) * groups + f // owners for f in range(devices)]
    out_rows = lax.ppermute(w_out, ("dp", "seq"), [(f, place[f]) for f in range(devices)])

    small = jnp.concatenate(
        [b_qkv.reshape(rows, -1), b_up.reshape(rows, -1)]
        + [v[:, None] for v in (b_out, b_down, gain_one, shift_one, gain_two, shift_two)],
        axis=1,
    )
    n_small = small.shape[1]
    n_up = b_up.shape[0] // rows
    small = jnp.pad(small, ((0, 0), (0, width - 3 * part - n_small)))
    blocks = jnp.concatenate(
        [
            w_qkv.reshape(rows, 3, groups, part).transpose(2, 0, 1, 3).reshape(groups, rows, 3 * part),
            jnp.broadcast_to(small[None], (groups,) + small.shape),
            w_up.reshape(rows, owners, groups, -1).transpose(2, 0, 1, 3).reshape(groups, rows, slice_width),
        ],
        axis=2,
    )
    blocks = swap_bits(blocks, "seq", groups).reshape(dp_rows, width + slice_width)
    first = gather_bits(jnp.concatenate([blocks[:, :width], out_rows], axis=0), "dp", owners)
    second = gather_bits(jnp.concatenate([blocks[:, width:], w_down], axis=0), "dp", owners)

    full_qkv = first[:, :dp_rows, : 3 * part].reshape(width, 3 * part)
    full_out = first[:, dp_rows:, :].reshape(part, width)
    small = first[:, :dp_rows, 3 * part : 3 * part + n_small].reshape(width, n_small).astype(F32)
    bias_qkv = lax.dynamic_index_in_dim(
        small[:, :3].reshape(3, groups, part), group, 1, keepdims=False
    ).reshape(1, 3 * part)
    bias_up = lax.dynamic_index_in_dim(
        small[:, 3 : 3 + n_up].reshape(owners, groups, -1), group, 1, keepdims=False
    ).reshape(1, slice_width)
    vectors = small[:, 3 + n_up :].T
    biases = vectors[0] + vectors[1]
    vectors = jnp.concatenate([vectors[2:], jnp.zeros((4, width), F32)], 0)
    full_up = second[:, :dp_rows, :].reshape(width, slice_width)
    full_down = second[:, dp_rows:, :].reshape(slice_width, width)

    cosine, sine = rotary(tokens, part // HD)
    out_part, dx_part, grad_a = attention(
        xg, full_qkv, full_out, vectors, bias_qkv, jnp.asarray(cosine), jnp.asarray(sine), owners
    )
    out_part, dx_part, grad_b = feed_forward(
        xg, full_up, full_down, vectors, bias_up, out_part, dx_part, owners
    )

    grad_a = scatter_bits(grad_a, "dp", owners)
    grad_b = scatter_bits(grad_b, "dp", owners)
    both = jnp.concatenate([out_part, dx_part], axis=1).reshape(groups, local, 2 * width)
    both = scatter_bits(both, "seq", groups)
    outputs = (inputs[0].astype(F32) + both[:, :width] + biases[None]).astype(BF16)[None]
    grad_inputs = (cotangent[0].astype(F32) + both[:, width:]).astype(BF16)[None]

    own_wout = lax.ppermute(
        grad_a[dp_rows : dp_rows + rows, :], ("dp", "seq"), [(place[f], f) for f in range(devices)]
    )
    tail_a = grad_a[dp_rows + rows :, :]
    tail_b = grad_b[dp_rows + down_rows :, :]
    small = jnp.concatenate([tail_a[:4], tail_b[1:3], jnp.zeros((2, width), F32)], 0)
    send = jnp.concatenate(
        [
            grad_a[:dp_rows, : 3 * part].reshape(groups, rows, 3 * part),
            grad_b[:dp_rows, :].reshape(groups, rows, slice_width),
        ],
        axis=2,
    )
    small = jnp.pad(small, ((0, 0), (0, send.shape[2] - width)))
    send = jnp.concatenate([send, jnp.broadcast_to(small[None], (groups,) + small.shape)], axis=1)
    send = swap_bits(send, "seq", groups)
    own_wqkv = send[:, :rows, : 3 * part].reshape(groups, rows, 3, part).transpose(1, 2, 0, 3).reshape(rows, -1)
    own_wup = (
        send[:, :rows, 3 * part :].reshape(groups, rows, owners, -1).transpose(1, 2, 0, 3).reshape(rows, -1)
    )
    small = send[:, rows:, :width]
    index = owner * groups + group
    own_bqkv = lax.dynamic_slice_in_dim(
        small[:, 0, : 3 * part].reshape(groups, 3, part).transpose(1, 0, 2).reshape(-1),
        index * b_qkv.shape[0],
        b_qkv.shape[0],
    )
    sums = jnp.sum(small, axis=0)
    own = lax.dynamic_slice_in_dim(sums, index * rows, rows, axis=1)
    own_bias = lax.dynamic_slice_in_dim(small[0, 3], index * rows, rows)
    own_bup = lax.dynamic_slice_in_dim(tail_b[0], owner * b_up.shape[0], b_up.shape[0])
    return (
        outputs,
        grad_inputs,
        own_wqkv,
        own_bqkv,
        own_wout,
        own_bias,
        own_wup,
        own_bup,
        grad_b[dp_rows : dp_rows + down_rows, :],
        own_bias,
        own[1],
        own[2],
        own[4],
        own[5],
    )


def reversed_bits(value, count):
    result = 0
    for bit in range(count):
        result = result | (((value >> bit) & 1) << (count - 1 - bit))
    return result


def after(value, *others):
    return lax.optimization_barrier((value,) + others)[0]


def spread(value, axis, size, gates=()):
    value, seen = value[None], []
    for step, bit in enumerate(reversed(range(log2(size)))):
        seen.append(exchange(value, axis, size, bit))
        if bit:
            other = after(seen[-1], *gates[step]) if step < len(gates) else seen[-1]
            value = jnp.concatenate([value, other], 0)
    return (value, seen[-1]), seen


def fold(kept, other):
    total = kept + other.astype(F32)
    half = total.shape[0] // 2
    return total[half:].astype(BF16), total[:half]


def finish(kept, other):
    return kept[0] + other[0].astype(F32)


def call(kernel, outs, scratch, flops, transcendentals, *operands, mib=8, far=0):
    return pl.pallas_call(
        kernel,
        out_shape=tuple(outs),
        in_specs=whole(len(operands) - far)
        + [pl.BlockSpec(memory_space=pltpu.HBM)] * far,
        out_specs=tuple(whole(len(outs))),
        scratch_shapes=scratch,
        compiler_params=pltpu.CompilerParams(vmem_limit_bytes=mib * 1024 * 1024),
        cost_estimate=pl.CostEstimate(flops=1, bytes_accessed=1, transcendentals=0),
    )(*operands)


def fetch(pairs, sems):
    copies = [pltpu.make_async_copy(source, to, sems.at[i]) for i, (source, to) in enumerate(pairs)]
    for copy in copies:
        copy.start()
    for copy in copies:
        copy.wait()


def pack_kernel(*refs):
    x_ref, g_ref, refs = refs[0], refs[1], refs[2:]
    count = (len(refs) - 5) // 2
    (sent_ref, kept_ref, both_ref, block_ref, sems), held = refs[count : count + 5], refs[count + 5 :]
    joined = [
        pltpu.make_async_copy(ref, both_ref.at[:, :, pl.ds(i * ref.shape[2], ref.shape[2])], sems.at[count + i])
        for i, ref in enumerate((x_ref, g_ref))
    ]
    for copy in joined:
        copy.start()
    fetch(tuple(zip(refs[:count], held)), sems)
    qkv_ref, up_ref, out_ref, small = held[0], held[1], held[2], held[3:]
    me = lax.axis_index("seq")
    groups, rows, _ = block_ref.shape
    width = qkv_ref.shape[1] // 3
    part = width // groups
    piece = rows * groups
    owners = up_ref.shape[1] // (groups * piece)
    lines = []
    for line in (small[:2], small[2:]):
        values = [ref[...].reshape(1, ref.shape[0]).astype(F32) for ref in line]
        used = sum(ref.shape[0] for ref in line)
        lines.append(jnp.concatenate(values + [jnp.zeros((1, part - used), F32)], 1))
    lines = jnp.concatenate(lines + [jnp.zeros((rows - 2, part), F32)], 0).astype(BF16)
    for group in range(groups):
        for c in range(3):
            start = c * width + group * part
            block_ref[group, :, c * part : (c + 1) * part] = qkv_ref[:, start : start + part]
        block_ref[group, :, 3 * part : width] = lines
        block_ref[group, :, width + up_ref.shape[1] // groups :] = out_ref[...]
        block_ref[group, :, width : width + up_ref.shape[1] // groups] = jnp.concatenate(
            [
                up_ref[:, (k * groups + group) * piece : (k * groups + group + 1) * piece]
                for k in range(owners)
            ],
            1,
        )
    for half in range(groups // 2):
        kept_ref[half] = block_ref[me ^ (2 * half)]
        sent_ref[half] = block_ref[me ^ (2 * half + 1)]
    for copy in joined:
        copy.wait()


def payload_kernel(kept_ref, near_ref, far_ref, down_ref, first_ref, second_ref, sem):
    me = lax.axis_index("seq")
    width = down_ref.shape[1]
    part, rows = width // 4, first_ref.shape[0] // 8
    copy = pltpu.make_async_copy(down_ref, second_ref.at[pl.ds(4 * rows, down_ref.shape[0])], sem)
    copy.start()
    hidden = kept_ref.shape[2] - 2 * width
    index = lax.broadcasted_iota(jnp.int32, (rows, part), 0)
    mine = index // 2 == lax.axis_index("dp")
    for step, block in enumerate((kept_ref.at[0], near_ref.at[0], far_ref.at[0], far_ref.at[1])):
        group = me ^ step
        lanes = pl.ds(pl.multiple_of(group * part, part), part)
        second_ref[pl.ds(pl.multiple_of(group * rows, rows), rows), :] = block[:, width : width + hidden]
        for c in range(3):
            first_ref[c * rows : (c + 1) * rows, lanes] = block[:, c * part : (c + 1) * part]
        line = block[:, 3 * part : width].astype(F32)
        line = jnp.where(index % 2 == 0, line[0:1], line[1:2])
        first_ref[3 * rows : 4 * rows, lanes] = jnp.where(mine, line, 0.0).astype(BF16)
        first_ref[pl.ds(pl.multiple_of((4 + group) * rows, rows), rows), :] = block[:, width + hidden :]
    copy.wait()


def merge_kernel(bit, rows, mine_ref, other_ref, out_ref):
    part = mine_ref.shape[0] - 5 * rows
    small, last = slice(part, part + rows), slice(part + rows, part + 5 * rows)
    out_ref[:part, :] = mine_ref[:part, :]
    out_ref[part : 2 * part, :] = other_ref[:part, :]
    out_ref[2 * part : 2 * part + rows, :] = mine_ref[small, :] + other_ref[small, :]
    same = (lax.axis_index("dp") >> bit) & 1 == (lax.axis_index("seq") >> (bit - 1)) & 1

    @pl.when(same)
    def _():
        out_ref[2 * part + rows :, :] = mine_ref[last, :]

    @pl.when(jnp.logical_not(same))
    def _():
        out_ref[2 * part + rows :, :] = other_ref[last, :]


def sources(pair, me):
    half = pair[0].shape[0]
    count = log2(2 * half)
    for slot in range(2 * half):
        ref = pair[slot // half]
        yield ref.at[slot % half], me ^ reversed_bits(slot, count)


def project_kernel(
    first_ref, other_ref, x_ref, y_ref, cos_ref, sin_ref, table_ref,
    xg_ref, na_ref, q_ref, qt_ref, k_ref, v_ref, da_ref, dat_ref, wq_ref, wo_ref, vec_ref,
):
    owner, group = lax.axis_index("dp"), lax.axis_index("seq")
    width = first_ref.shape[1]
    groups = 2 * x_ref.shape[0]
    part = width // groups
    rows = first_ref.shape[0] // 17
    owners = width // (rows * groups)
    local = x_ref.shape[1]
    for slot in range(owners):
        block = (first_ref, other_ref)[slot // 4].at[pl.ds(slot % 4 * 3 * rows, 3 * rows)]
        rank = owner ^ reversed_bits(slot, log2(owners))
        for g in range(groups):
            lanes = slice(g * part, (g + 1) * part)
            to = pl.ds(pl.multiple_of((rank * groups + g) * rows, rows), rows)
            for c in range(3):
                wq_ref[to, c * part : (c + 1) * part] = block[c * rows : (c + 1) * rows, lanes]
    for slot, ref in enumerate((first_ref, other_ref)):
        x = (owner & 1) ^ slot
        wo_ref[pl.ds(pl.multiple_of(x * 4 * rows, 4 * rows), 4 * rows), :] = ref[13 * rows :, :]
    devices = owners * groups
    small = first_ref[12 * rows : 13 * rows, :].astype(F32) + other_ref[12 * rows : 13 * rows, :].astype(F32)
    line_one, line_two = (
        jnp.concatenate(
            [
                small[2 * rank + i : 2 * rank + i + 1, g * part : (g + 1) * part]
                for rank in range(owners)
                for g in range(groups)
            ],
            0,
        ).astype(BF16)
        for i in range(2)
    )

    def place_values(line, lane_of, device_of_column):
        columns = lane_of.shape[1]
        pick = lax.broadcasted_iota(jnp.int32, (line.shape[1], columns), 0) == lane_of
        values = dot(line, jnp.where(pick, 1.0, 0.0).astype(BF16))
        held = lax.broadcasted_iota(jnp.int32, (devices, columns), 0) == device_of_column
        return jnp.sum(jnp.where(held, values, 0.0), axis=0, keepdims=True)

    column = lax.broadcasted_iota(jnp.int32, (1, width), 1)
    own = [place_values(line_two, column % rows + v * rows, column // rows) for v in range(6)]
    piece = rows * groups
    start = 3 * width // devices
    bias_up = place_values(line_one, column % piece + start, column // piece * groups + group)
    lane_of = jnp.concatenate(
        [table_ref[0:1, pl.ds(pl.multiple_of(c * width + group * part, part), part)] for c in range(3)], 1
    )
    owner_of = jnp.concatenate(
        [table_ref[1:2, pl.ds(pl.multiple_of(c * width + group * part, part), part)] for c in range(3)], 1
    )
    bias = place_values(line_one, lane_of, owner_of)
    gain, shift = own[2], own[3]
    vec_ref[...] = jnp.concatenate(
        own[2:] + [own[0] + own[1], bias_up, jnp.zeros((2, width), F32)], 0
    )

    lane = lax.broadcasted_iota(jnp.int32, (local, part), 1)
    turn = lane % HD < ROT // 2

    def partner(value):
        return jnp.where(
            turn, pltpu.roll(value, part - ROT // 2, 1), pltpu.roll(value, ROT // 2, 1)
        )

    for block, rank in sources((x_ref, y_ref), group):
        start = pl.multiple_of(rank * local, local)
        to = pl.ds(start, local)
        both = block[...]
        xg_ref[to, :] = both
        normal, _ = standardize(both[:, :width].astype(F32))
        normed = (normal * gain + shift).astype(BF16)
        na_ref[to, :] = normed
        projected = dot(normed, wq_ref[...]) + bias
        cosine, sine = cos_ref[to, :], sin_ref[to, :]
        query = projected[:, :part]
        query = query * cosine + partner(query) * sine
        key = projected[:, part : 2 * part]
        key = key * cosine + partner(key) * sine
        query = query.astype(BF16).astype(F32) * HD**-0.5
        q_ref[to, :] = query.astype(BF16)
        qt_ref[:, to] = query.T.astype(BF16)
        k_ref[to, :] = key.astype(BF16)
        v_ref[to, :] = projected[:, 2 * part :].astype(BF16)
        grad_att = dot_last(both[:, width:], wo_ref[...]).astype(BF16)
        da_ref[to, :] = grad_att
        dat_ref[:, to] = grad_att.astype(F32).T.astype(BF16)


def attend_kernel(
    xg_ref, na_ref, q_ref, qt_ref, k_ref, v_ref, da_ref, dat_ref, wq_ref, cos_ref, sin_ref,
    att_ref, dp_ref, small_ref, sent_ref, kept_ref,
    dq_ref, dkt_ref, dvt_ref, gq_ref, go_ref,
):
    owner = lax.axis_index("dp")
    tokens, part = q_ref.shape
    width = na_ref.shape[1]
    groups = width // part
    owners = 2 * sent_ref.shape[0]
    rows = part // owners
    lane = lax.broadcasted_iota(jnp.int32, (BLOCK, part), 1)
    turn = lane % HD < ROT // 2

    def partner(value):
        return jnp.where(
            turn, pltpu.roll(value, part - ROT // 2, 1), pltpu.roll(value, ROT // 2, 1)
        )

    dkt_ref[...] = jnp.zeros_like(dkt_ref)
    dvt_ref[...] = jnp.zeros_like(dvt_ref)
    below = lax.broadcasted_iota(jnp.int32, (BLOCK, BLOCK), 0) >= lax.broadcasted_iota(
        jnp.int32, (BLOCK, BLOCK), 1
    )
    zero = jnp.zeros((), BF16)
    for block in range(tokens // BLOCK):
        at = pl.ds(block * BLOCK, BLOCK)
        seen = (block + 1) * BLOCK
        attended = jnp.zeros((BLOCK, part), F32)
        grad_query = jnp.zeros((BLOCK, part), F32)
        for head in range(part // HD):
            mine = lane // HD == head
            mine_t = lax.broadcasted_iota(jnp.int32, (part, BLOCK), 0) // HD == head
            query = jnp.where(mine, q_ref[at, :], zero)
            grad_att = jnp.where(mine, da_ref[at, :], zero)
            scores = dot_last(query, k_ref[:seen, :])
            last = jnp.where(below, scores[:, seen - BLOCK :], -1e30)
            scores = last if block == 0 else jnp.concatenate([scores[:, : seen - BLOCK], last], 1)
            raised = jnp.exp(scores - jnp.max(scores, axis=-1, keepdims=True))
            probs = raised * (1.0 / jnp.sum(raised, axis=-1, keepdims=True))
            probs_low = probs.astype(BF16)
            attended = jnp.where(mine, dot(probs_low, v_ref[:seen, :]), attended)
            grad_probs = dot_last(grad_att, v_ref[:seen, :])
            inner = jnp.sum(probs * grad_probs, axis=-1, keepdims=True)
            grad_scores = (probs * (grad_probs - inner)).astype(BF16)
            grad_query = jnp.where(mine, dot(grad_scores, k_ref[:seen, :]), grad_query)
            query_t = jnp.where(mine_t, qt_ref[:, at], zero)
            grad_att_t = jnp.where(mine_t, dat_ref[:, at], zero)
            dkt_ref[:, :seen] += dot(query_t, grad_scores)
            dvt_ref[:, :seen] += dot(grad_att_t, probs_low)
        att_ref[at, :] = attended.astype(BF16)
        dq_ref[at, :] = grad_query * HD**-0.5

    vectors = [jnp.zeros((1, width), F32) for _ in range(3)]
    grad_bias = jnp.zeros((1, 3 * part), F32)
    for block in range(tokens // BLOCK):
        at = pl.ds(block * BLOCK, BLOCK)
        cosine, sine = cos_ref[at, :], sin_ref[at, :]
        grad_query = dq_ref[at, :]
        grad_query = grad_query * cosine - partner(grad_query) * sine
        grad_key = dkt_ref[:, at].T
        grad_key = grad_key * cosine - partner(grad_key) * sine
        grad_proj = jnp.concatenate([grad_query, grad_key, dvt_ref[:, at].T], 1).astype(BF16)
        dp_ref[at, :] = grad_proj
        grad_bias += jnp.sum(grad_proj.astype(F32), axis=0, keepdims=True)
        upstream = dot_last(grad_proj, wq_ref[...])
        normal, _ = standardize(xg_ref[at, :width].astype(F32))
        vectors[0] += jnp.sum(normal * upstream, axis=0, keepdims=True)
        vectors[1] += jnp.sum(upstream, axis=0, keepdims=True)
        vectors[2] += jnp.sum(xg_ref[at, width:].astype(F32), axis=0, keepdims=True)

    gq_ref[...] = dot_rows(na_ref[...], dp_ref[...])
    go_ref[...] = dot_rows(att_ref[...], xg_ref[:, width:])
    small_ref[...] = jnp.concatenate(
        [jnp.concatenate([grad_bias, jnp.zeros((1, width - 3 * part), F32)], 1)]
        + vectors
        + [jnp.zeros((4, width), F32)],
        0,
    )
    for ref, rank in sources((kept_ref, sent_ref), owner):
        kind = ref.dtype
        for g in range(groups):
            at = pl.ds(pl.multiple_of((rank * groups + g) * rows, rows), rows)
            for c in range(3):
                ref[c * rows : (c + 1) * rows, g * part : (g + 1) * part] = gq_ref[
                    at, c * part : (c + 1) * part
                ].astype(kind)
        ref[3 * rows : 4 * rows, :] = go_ref[pl.ds(pl.multiple_of((rank % 2 * 4 + rank // 2) * rows, rows), rows), :].astype(kind)


def hidden_kernel(
    second_ref, other_ref, xg_ref, vec_ref, small_ref,
    act_ref, dh_ref, up_ref, down_ref, sent_ref, kept_ref,
    nb_ref, gu_ref,
):
    owner = lax.axis_index("dp")
    tokens, hidden_width = act_ref.shape
    width = vec_ref.shape[1]
    rows = second_ref.shape[1] // 2
    for block, rank in sources((second_ref, other_ref), owner):
        at = pl.ds(pl.multiple_of(rank * rows, rows), rows)
        up_ref[at, :] = block[:rows, :]
        down_ref[at, :] = block[rows:, :]
    gain, shift, bias = vec_ref[2:3, :], vec_ref[3:4, :], vec_ref[5:6, :]
    vectors = [jnp.zeros((1, width), F32) for _ in range(2)]
    grad_bias = jnp.zeros((1, hidden_width), F32)
    for block in range(tokens // BLOCK):
        at = pl.ds(block * BLOCK, BLOCK)
        normal, _ = standardize(xg_ref[at, :width].astype(F32))
        normed = (normal * gain + shift).astype(BF16)
        nb_ref[at, :] = normed
        hidden = dot(normed, up_ref[...]) + bias
        half = 0.5 * (1.0 + lax.erf(hidden * math.sqrt(0.5)))
        act_ref[at, :] = (hidden * half).astype(BF16)
        slope = half + hidden * jnp.exp(-0.5 * hidden * hidden) * (1.0 / math.sqrt(2.0 * math.pi))
        grad_hidden = (dot_last(xg_ref[at, width:], down_ref[...]) * slope).astype(BF16)
        dh_ref[at, :] = grad_hidden
        grad_bias += jnp.sum(grad_hidden.astype(F32), axis=0, keepdims=True)
        upstream = dot_last(grad_hidden, up_ref[...])
        vectors[0] += jnp.sum(normal * upstream, axis=0, keepdims=True)
        vectors[1] += jnp.sum(upstream, axis=0, keepdims=True)
    gu_ref[...] = dot_rows(nb_ref[...], dh_ref[...])
    extra = sent_ref.shape[1] - rows
    tail = jnp.concatenate([grad_bias] + vectors + [small_ref[:4, :], jnp.zeros((extra - 7, width), F32)], 0)
    for ref, rank in sources((kept_ref, sent_ref), owner):
        ref[:rows, :] = gu_ref[pl.ds(pl.multiple_of(rank * rows, rows), rows), :].astype(ref.dtype)
        ref[rows:, :] = tail.astype(ref.dtype)


def down_kernel(act_ref, xg_ref, sent_ref, kept_ref, gd_ref):
    width = sent_ref.shape[2]
    rows = sent_ref.shape[1]
    gd_ref[...] = dot_rows(act_ref[...], xg_ref[:, width:])
    for ref, rank in sources((kept_ref, sent_ref), lax.axis_index("dp")):
        ref[...] = gd_ref[pl.ds(pl.multiple_of(rank * rows, rows), rows), :].astype(ref.dtype)


def join_kernel(
    xg_ref, att_ref, wo_ref, act_ref, down_ref, vec_ref, dp_ref, wq_ref, dh_ref, up_ref,
    sent_ref, kept_ref,
):
    group = lax.axis_index("seq")
    local = sent_ref.shape[1]
    width = wo_ref.shape[1]
    gain_one, gain_two, bias = vec_ref[0:1, :], vec_ref[2:3, :], vec_ref[4:5, :]
    for step in range(2 * sent_ref.shape[0]):
        at = pl.ds(pl.multiple_of((group ^ step) * local, local), local)
        ref = (kept_ref, sent_ref)[step % 2].at[step // 2]
        out = dot(att_ref[at, :], wo_ref[...]) + dot(act_ref[at, :], down_ref[...])
        rows_in = xg_ref[at, :width].astype(F32)
        normal, scale = standardize(rows_in)
        inner = gain_one * dot_last(dp_ref[at, :], wq_ref[...]) + gain_two * dot_last(dh_ref[at, :], up_ref[...])
        grad = norm_back(normal, scale, inner)
        if step == 0:
            out = out + rows_in + bias
            grad = grad + xg_ref[at, width:].astype(F32)
        ref[:, :width] = out.astype(ref.dtype)
        ref[:, width:] = grad.astype(ref.dtype)


def deal_kernel(a_ref, b_ref, sent_ref, kept_ref):
    me = lax.axis_index("seq")
    width = a_ref.shape[1]
    part = width // 4
    rows = a_ref.shape[0] // 4
    kind = sent_ref.dtype
    small = jnp.concatenate(
        [b_ref[4 * rows + 3 : 4 * rows + 6, :], b_ref[4 * rows + 1 : 4 * rows + 3, :], jnp.zeros((rows - 5, width), F32)], 0
    )
    for step in range(4):
        group = me ^ step
        ref = (kept_ref, sent_ref)[step % 2].at[step // 2]
        lanes = pl.ds(pl.multiple_of(group * part, part), part)
        for c in range(3):
            ref[:rows, c * part : (c + 1) * part] = a_ref[c * rows : (c + 1) * rows, lanes].astype(kind)
        ref[:rows, 3 * part :] = b_ref[pl.ds(pl.multiple_of(group * rows, rows), rows), :].astype(kind)
        ref[rows:, :width] = small.astype(kind)
        ref[rows:, width:] = jnp.zeros((rows, 3 * part), kind)


def collect_kernel(
    kept_ref, near_ref, far_ref, b_ref, out_ref, down_kept_ref, down_other_ref,
    qkv_ref, up_ref, wout_ref, bqkv_ref, bias_ref, twin_ref, bup_ref, gain_one_ref, shift_one_ref, gain_two_ref, shift_two_ref, down_ref,
    block_ref,
):
    me = lax.axis_index("seq")
    place = lax.axis_index("dp") * 4 + me
    rows = qkv_ref.shape[0]
    width = qkv_ref.shape[1] // 3
    part = width // 4
    piece = 4 * rows
    for step, block in enumerate((kept_ref.at[0], near_ref.at[0], far_ref.at[0], far_ref.at[1])):
        block_ref[me ^ step] = block[...].astype(F32)
    for g in range(4):
        for c in range(3):
            qkv_ref[:, c * width + g * part : c * width + (g + 1) * part] = block_ref[
                g, :rows, c * part : (c + 1) * part
            ]
    for k in range(up_ref.shape[1] // (4 * piece)):
        start = 3 * part + k * piece
        up_ref[:, 4 * k * piece : 4 * (k + 1) * piece] = jnp.concatenate(
            [block_ref[g, :rows, start : start + piece] for g in range(4)], 1
        )
    wout_ref[...] = out_ref[...]
    down_ref[...] = down_kept_ref[0] + down_other_ref[0].astype(F32)

    def own(values, ref, index):
        size, count = values.shape[1], ref.shape[0]
        values = pltpu.roll(values, (size - index * count) % size, 1)[0:1, :count]
        ref[...] = values.reshape(count)

    sums = sum(block_ref[g, rows : rows + 8, :width] for g in range(4))
    for i, ref in enumerate((gain_one_ref, shift_one_ref, gain_two_ref, shift_two_ref)):
        own(sums[i + 1 : i + 2], ref, place)
    bias = jnp.concatenate(
        [block_ref[g, rows : rows + 1, c * part : (c + 1) * part] for c in range(3) for g in range(4)], 1
    )
    own(bias, bqkv_ref, place)
    own(b_ref[4 * rows + 6 : 4 * rows + 7, :], bias_ref, place)
    twin_ref[...] = bias_ref[...]
    own(b_ref[4 * rows : 4 * rows + 1, :], bup_ref, lax.axis_index("dp"))


def shards(
    owners, groups,
    inputs, cotangent, w_qkv, b_qkv, w_out, b_out, w_up, b_up, w_down, b_down,
    gain_one, shift_one, gain_two, shift_two,
):
    rows, width = w_qkv.shape[0], w_qkv.shape[1] // 3
    hidden = w_up.shape[1] // groups
    local = inputs.shape[1]
    if rows % 16 or groups != 4 or owners != 8 or local != BLOCK or hidden != width:
        return shards_any(
            owners, groups, inputs, cotangent, w_qkv, b_qkv, w_out, b_out, w_up, b_up, w_down, b_down,
            gain_one, shift_one, gain_two, shift_two,
        )
    tokens = local * groups
    part = width // groups
    devices = owners * groups
    half = owners // 2
    heads = part // HD
    shape = jax.ShapeDtypeStruct

    target = [(f % 4 * 2 + f // 4 % 2) * groups + f // owners for f in range(devices)]

    block = shape((2, rows, 2 * width + hidden), BF16)
    params = (w_qkv, w_up, w_out, b_qkv, b_up, b_out, b_down, gain_one, shift_one, gain_two, shift_two)
    sent, kept, x = call(
        pack_kernel,
        (block, block, shape((1, local, 2 * width), BF16)),
        [pltpu.VMEM((groups, rows, 2 * width + hidden), BF16), pltpu.SemaphoreType.DMA((len(params) + 2,))]
        + [pltpu.VMEM(p.shape, BF16) for p in params],
        0, 0, inputs, cotangent, *params, mib=63, far=len(params) + 2,
    )
    near = exchange(sent, "seq", groups, 0)
    far = exchange(jnp.stack([kept[1], near[1]]), "seq", groups, 1)
    first, second = call(
        payload_kernel,
        (shape((8 * rows, width), BF16), shape((4 * rows + w_down.shape[0], width), BF16)),
        [pltpu.SemaphoreType.DMA], 0, 0, kept, near, far, w_down, mib=4, far=1,
    )
    def merged(bit, mine, other):
        out = shape((2 * mine.shape[0] - 5 * rows, width), BF16)
        return call(functools.partial(merge_kernel, bit, rows), (out,), [], 0, 0, mine, other, mib=4)[0]

    x = after(x, far)
    x_other = exchange(x, "seq", groups, 1)
    other = exchange(first, "dp", owners, 2)
    second = after(second, other)[None]
    first = merged(2, first, other)
    other, second_other = exchange(first, "dp", owners, 1), exchange(second, "dp", owners, 2)
    other, second_other, x_other = lax.optimization_barrier((other, second_other, x_other))
    first, second = merged(1, first, other), jnp.concatenate([second, second_other], 0)
    x = jnp.concatenate([x, x_other], 0)
    first = (first, exchange(first, "dp", owners, 0))
    x_pair = (x, exchange(x, "seq", groups, 0))
    second_other = exchange(second, "dp", owners, 1)

    cosine, sine = (jnp.asarray(t) for t in rotary(tokens, heads))
    column = np.arange(3 * width, dtype=np.int32)
    own = 3 * width // devices
    table = np.zeros((8, 3 * width), np.int32)
    table[0], table[1] = column % own, column // own
    wide, narrow, turned = shape((tokens, width), BF16), shape((tokens, part), BF16), shape((part, tokens), BF16)
    xg, normed_a, query, query_t, key, value, grad_att, grad_att_t, full_qkv, full_out, vectors = call(
        project_kernel,
        (shape((tokens, 2 * width), BF16), wide, narrow, turned, narrow, narrow, narrow, turned)
        + (shape((width, 3 * part), BF16), shape((part, width), BF16), shape((8, width), F32)),
        [], 2 * tokens * width * 4 * part, 0,
        *first, *x_pair, cosine, sine, jnp.asarray(table),
    )
    second = jnp.concatenate([second, after(second_other, normed_a)], 0)
    second = (second, exchange(second, "dp", owners, 0))
    chunk = 5 * rows
    attended, grad_proj, small, sent_a, kept_a = call(
        attend_kernel,
        (narrow, shape((tokens, 3 * part), BF16), shape((8, width), F32))
        + (shape((half, 4 * rows, width), BF16), shape((half, 4 * rows, width), F32)),
        [
            pltpu.VMEM((tokens, part), F32),
            pltpu.VMEM((part, tokens), F32),
            pltpu.VMEM((part, tokens), F32),
            pltpu.VMEM((width, 3 * part), F32),
            pltpu.VMEM((part, width), F32),
        ],
        8 * tokens * tokens * part * 6, 2 * tokens * tokens,
        xg, normed_a, after(query, second_other), query_t, key, value, grad_att, grad_att_t, full_qkv, cosine, sine,
        mib=16,
    )
    other_a = exchange(sent_a, "dp", owners, 0)
    active, grad_hidden, full_up, full_down, sent_u, kept_u = call(
        hidden_kernel,
        (wide, wide, shape((width, hidden), BF16), shape((hidden, width), BF16))
        + (shape((half, chunk, width), BF16), shape((half, chunk, width), F32)),
        [
            pltpu.VMEM((tokens, width), BF16),
            pltpu.VMEM((width, hidden), F32),
        ],
        8 * tokens * width * hidden, 2 * tokens * hidden,
        *second, xg, vectors, small,
        mib=16,
    )
    other_u = exchange(sent_u, "dp", owners, 0)
    sent_a, kept_a = fold(kept_a, other_a)
    other_a = exchange(sent_a, "dp", owners, 1)
    sent_x, kept_x = call(
        join_kernel,
        (shape((2, local, 2 * width), BF16), shape((2, local, 2 * width), F32)),
        [],
        4 * tokens * width * hidden, 0,
        xg, attended, full_out, active, full_down, vectors,
        grad_proj, full_qkv, grad_hidden, full_up,
    )
    down_rows = w_down.shape[0]
    sent_d, kept_d = call(
        down_kernel,
        (shape((half, down_rows, width), BF16), shape((half, down_rows, width), F32)),
        [pltpu.VMEM((hidden, width), F32)],
        2 * tokens * width * hidden, 0,
        active, xg,
    )
    other_x = exchange(after(sent_x, other_u, other_a), "seq", groups, 0)
    other_u, other_x, sent_d, = lax.optimization_barrier((other_u, other_x, sent_d,))
    other_d = exchange(sent_d, "dp", owners, 0)
    sent_u, kept_u = fold(kept_u, other_u)
    other_u = exchange(sent_u, "dp", owners, 1)
    sent_a, kept_a = fold(kept_a, other_a)
    other_a = exchange(sent_a, "dp", owners, 2)
    sent_x, kept_x = fold(kept_x, other_x)
    other_x = exchange(sent_x, "seq", groups, 1)
    sent_d, kept_d = fold(kept_d, other_d)
    other_u, other_a, sent_d, kept_d, = lax.optimization_barrier((other_u, other_a, sent_d, kept_d,))
    sent_u, kept_u = fold(kept_u, other_u)
    other_u = exchange(sent_u, "dp", owners, 2)
    grad_a = finish(kept_a, other_a)
    own_wout = lax.ppermute(grad_a[3 * rows :, :], ("dp", "seq"), [(target[f], f) for f in range(devices)])
    other_d = exchange(sent_d, "dp", owners, 1)
    other_u, other_d, other_x, = lax.optimization_barrier((other_u, other_d, other_x,))
    grad_u = finish(kept_u, other_u)
    sent_d, kept_d = fold(kept_d, other_d)
    block = shape((2, 2 * rows, 3 * part + hidden), BF16)
    sent, kept = call(deal_kernel, (block, block), [], 0, 0, grad_a, grad_u)
    near = exchange(sent, "seq", groups, 0)
    other_d = exchange(sent_d, "dp", owners, 2)
    both = finish(kept_x, after(other_x, near))
    outputs, grad_inputs = (v.astype(BF16)[None] for v in (both[:, :width], both[:, width:]))
    far = exchange(jnp.stack([kept[1], near[1]]), "seq", groups, 1)
    vector = shape((rows,), F32)
    own_wqkv, own_wup, own_wout, own_bqkv, own_bias, twin_bias, own_bup, *own, grad_d = call(
        collect_kernel,
        (shape(w_qkv.shape, F32), shape(w_up.shape, F32), shape(w_out.shape, F32))
        + (shape(b_qkv.shape, F32), vector, vector, shape(b_up.shape, F32), vector, vector, vector, vector, shape(w_down.shape, F32)),
        [pltpu.VMEM((groups, 2 * rows, 3 * part + hidden), F32)],
        0, 0, kept, near, far, grad_u, own_wout, kept_d, other_d,
    )
    return (
        outputs,
        grad_inputs,
        own_wqkv,
        own_bqkv,
        own_wout,
        own_bias,
        own_wup,
        own_bup,
        grad_d,
        twin_bias,
        *own,
    )


def solution(mesh):
    rows = P("dp", "seq", None)
    matrix, vector = P(("dp", "seq"), None), P(("dp", "seq"))
    weights = (matrix, vector) * 4
    return jax.shard_map(
        functools.partial(shards, mesh.shape["dp"], mesh.shape["seq"]),
        mesh=mesh,
        in_specs=(rows, rows) + weights + (vector,) * 4,
        out_specs=(rows, rows) + weights + (vector,) * 4,
        check_vma=False,
    )
```

```python
import functools
import math

import jax
import jax.numpy as jnp
import numpy as np
from jax import lax
from jax.experimental import pallas as pl
from jax.experimental.pallas import tpu as pltpu
from jax.sharding import PartitionSpec as P

HD = 64
ROT = 16
EPS = 1e-05
BLOCK = 256
F32 = jnp.float32
BF16 = jnp.bfloat16
PARAMS = pltpu.CompilerParams(vmem_limit_bytes=48 * 1024 * 1024)


def log2(count):
    assert count & (count - 1) == 0
    return count.bit_length() - 1


def exchange(value, axis, size, bit):
    return lax.ppermute(value, axis, [(i, i ^ (1 << bit)) for i in range(size)])


def flag_of(axis, bit):
    return (lax.axis_index(axis) >> bit) & 1 == 1


def gather_bits(value, axis, size):
    shape = value.shape
    for done, bit in enumerate(reversed(range(log2(size)))):
        other = exchange(value, axis, size, bit)
        upper = flag_of(axis, bit)
        value = jnp.where(
            upper,
            jnp.stack([other, value], done),
            jnp.stack([value, other], done),
        )
    return value.reshape((size,) + shape)


def swap_bits(blocks, axis, size):
    count = log2(size)
    rest = blocks.shape[1:]
    value = blocks.reshape((2,) * count + rest)
    for bit in range(count):
        place = count - 1 - bit
        low = lax.index_in_dim(value, 0, place, keepdims=False)
        high = lax.index_in_dim(value, 1, place, keepdims=False)
        upper = flag_of(axis, bit)
        other = exchange(jnp.where(upper, low, high), axis, size, bit)
        value = jnp.stack([jnp.where(upper, other, low), jnp.where(upper, high, other)], place)
    return value.reshape((size,) + rest)


def scatter_bits(blocks, axis, size):
    count = log2(size)
    rest = blocks.shape[1:]
    value = blocks.reshape((2,) * count + rest)
    for bit in range(count):
        place = count - 1 - bit
        low = lax.index_in_dim(value, 0, place, keepdims=False)
        high = lax.index_in_dim(value, 1, place, keepdims=False)
        upper = flag_of(axis, bit)
        sent = jnp.where(upper, low, high).astype(BF16)
        value = jnp.where(upper, high, low).astype(F32) + exchange(sent, axis, size, bit).astype(F32)
    return value


def dot(left, right):
    return lax.dot_general(left, right, (((1,), (0,)), ((), ())), preferred_element_type=F32)


def dot_rows(left, right):
    return lax.dot_general(left, right, (((0,), (0,)), ((), ())), preferred_element_type=F32)


def dot_last(left, right):
    return lax.dot_general(left, right, (((1,), (1,)), ((), ())), preferred_element_type=F32)


def standardize(rows):
    average = jnp.mean(rows, axis=-1, keepdims=True)
    centered = rows - average
    variance = jnp.mean(centered * centered, axis=-1, keepdims=True)
    scale = lax.rsqrt(variance + EPS)
    return centered * scale, scale


def norm_back(normal, scale, inner):
    first = jnp.mean(inner, axis=-1, keepdims=True)
    second = jnp.mean(inner * normal, axis=-1, keepdims=True)
    return scale * (inner - first - normal * second)


def attention_kernel(
    xg_ref, wq_ref, wo_ref, vec_ref, bias_ref, cos_ref, sin_ref,
    out_ref, dx_ref, grad_ref,
    na_ref, q_ref, k_ref, v_ref, da_ref, qt_ref, dat_ref, att_ref, dq_ref, dkt_ref, dvt_ref, dp_ref,
):
    tokens = xg_ref.shape[0]
    width = xg_ref.shape[1] // 2
    part = wo_ref.shape[0]
    heads = part // HD
    owners, _, _ = grad_ref.shape
    own_rows = width // owners
    out_rows = part // owners
    gain = vec_ref[0:1, :]
    shift = vec_ref[1:2, :]
    lane = lax.broadcasted_iota(jnp.int32, (BLOCK, part), 1)
    turn = lane % HD < ROT // 2

    def partner(value):
        return jnp.where(
            turn, pltpu.roll(value, part - ROT // 2, 1), pltpu.roll(value, ROT // 2, 1)
        )

    for block in range(tokens // BLOCK):
        rows = pl.ds(block * BLOCK, BLOCK)
        normal, _ = standardize(xg_ref[rows, :width].astype(F32))
        normed = (normal * gain + shift).astype(BF16)
        na_ref[rows, :] = normed
        projected = dot(normed, wq_ref[...]) + bias_ref[...]
        cosine, sine = cos_ref[rows, :], sin_ref[rows, :]
        query = projected[:, :part]
        query = query * cosine + partner(query) * sine
        key = projected[:, part : 2 * part]
        key = key * cosine + partner(key) * sine
        query = query.astype(BF16).astype(F32) * HD**-0.5
        q_ref[rows, :] = query.astype(BF16)
        qt_ref[:, rows] = query.T.astype(BF16)
        k_ref[rows, :] = key.astype(BF16)
        v_ref[rows, :] = projected[:, 2 * part :].astype(BF16)
        grad_att = dot_last(xg_ref[rows, width:], wo_ref[...]).astype(BF16)
        da_ref[rows, :] = grad_att
        dat_ref[:, rows] = grad_att.astype(F32).T.astype(BF16)

    dkt_ref[...] = jnp.zeros_like(dkt_ref)
    dvt_ref[...] = jnp.zeros_like(dvt_ref)
    below = lax.broadcasted_iota(jnp.int32, (BLOCK, BLOCK), 0) >= lax.broadcasted_iota(
        jnp.int32, (BLOCK, BLOCK), 1
    )
    zero = jnp.zeros((), BF16)
    for block in range(tokens // BLOCK):
        rows = pl.ds(block * BLOCK, BLOCK)
        seen = (block + 1) * BLOCK
        attended = jnp.zeros((BLOCK, part), F32)
        grad_query = jnp.zeros((BLOCK, part), F32)
        for head in range(heads):
            mine = lane // HD == head
            mine_t = lax.broadcasted_iota(jnp.int32, (part, BLOCK), 0) // HD == head
            query = jnp.where(mine, q_ref[rows, :], zero)
            grad_att = jnp.where(mine, da_ref[rows, :], zero)
            scores = dot_last(query, k_ref[:seen, :])
            last = jnp.where(below, scores[:, seen - BLOCK :], -1e30)
            scores = last if block == 0 else jnp.concatenate([scores[:, : seen - BLOCK], last], 1)
            raised = jnp.exp(scores - jnp.max(scores, axis=-1, keepdims=True))
            probs = raised * (1.0 / jnp.sum(raised, axis=-1, keepdims=True))
            probs_low = probs.astype(BF16)
            attended = jnp.where(mine, dot(probs_low, v_ref[:seen, :]), attended)
            grad_probs = dot_last(grad_att, v_ref[:seen, :])
            inner = jnp.sum(probs * grad_probs, axis=-1, keepdims=True)
            grad_scores = (probs * (grad_probs - inner)).astype(BF16)
            grad_query = jnp.where(mine, dot(grad_scores, k_ref[:seen, :]), grad_query)
            query_t = jnp.where(mine_t, qt_ref[:, rows], zero)
            grad_att_t = jnp.where(mine_t, dat_ref[:, rows], zero)
            dkt_ref[:, :seen] += dot(query_t, grad_scores)
            dvt_ref[:, :seen] += dot(grad_att_t, probs_low)
        att_ref[rows, :] = attended.astype(BF16)
        dq_ref[rows, :] = grad_query * HD**-0.5

    vectors = [jnp.zeros((1, width), F32) for _ in range(3)]
    grad_bias = jnp.zeros((1, 3 * part), F32)
    for block in range(tokens // BLOCK):
        rows = pl.ds(block * BLOCK, BLOCK)
        cosine, sine = cos_ref[rows, :], sin_ref[rows, :]
        grad_query = dq_ref[rows, :]
        grad_query = grad_query * cosine - partner(grad_query) * sine
        grad_key = dkt_ref[:, rows].T
        grad_key = grad_key * cosine - partner(grad_key) * sine
        grad_value = dvt_ref[:, rows].T
        grad_proj = jnp.concatenate([grad_query, grad_key, grad_value], 1).astype(BF16)
        dp_ref[rows, :] = grad_proj
        grad_bias += jnp.sum(grad_proj.astype(F32), axis=0, keepdims=True)
        out_ref[rows, :] = dot(att_ref[rows, :], wo_ref[...])
        upstream = dot_last(grad_proj, wq_ref[...])
        normal, scale = standardize(xg_ref[rows, :width].astype(F32))
        vectors[0] += jnp.sum(normal * upstream, axis=0, keepdims=True)
        vectors[1] += jnp.sum(upstream, axis=0, keepdims=True)
        vectors[2] += jnp.sum(xg_ref[rows, width:].astype(F32), axis=0, keepdims=True)
        dx_ref[rows, :] = norm_back(normal, scale, gain * upstream)

    grad_qkv = dot_rows(na_ref[...], dp_ref[...])
    grad_out = dot_rows(att_ref[...], xg_ref[:, width:])
    rest = grad_ref.shape[1] - own_rows - out_rows
    tail = jnp.concatenate(
        [jnp.concatenate([grad_bias, jnp.zeros((1, width - 3 * part), F32)], 1)]
        + vectors
        + [jnp.zeros((rest - 4, width), F32)],
        0,
    )
    for owner in range(owners):
        grad_ref[owner, :own_rows, : 3 * part] = grad_qkv[owner * own_rows : (owner + 1) * own_rows, :]
        grad_ref[owner, :own_rows, 3 * part :] = jnp.zeros((own_rows, width - 3 * part), F32)
        grad_ref[owner, own_rows : own_rows + out_rows, :] = grad_out[
            owner * out_rows : (owner + 1) * out_rows, :
        ]
        grad_ref[owner, own_rows + out_rows :, :] = tail


def mlp_kernel(
    xg_ref, up_ref, down_ref, vec_ref, bias_ref, out_part_ref, dx_part_ref,
    out_ref, dx_ref, grad_ref,
    nb_ref, act_ref, dh_ref,
):
    tokens = xg_ref.shape[0]
    width = xg_ref.shape[1] // 2
    hidden_width = up_ref.shape[1]
    owners = grad_ref.shape[0]
    up_rows = width // owners
    down_rows = hidden_width // owners
    gain = vec_ref[2:3, :]
    shift = vec_ref[3:4, :]
    vectors = [jnp.zeros((1, width), F32) for _ in range(2)]
    grad_bias = jnp.zeros((1, hidden_width), F32)
    for block in range(tokens // BLOCK):
        rows = pl.ds(block * BLOCK, BLOCK)
        grad_rows = xg_ref[rows, width:]
        normal, scale = standardize(xg_ref[rows, :width].astype(F32))
        normed = (normal * gain + shift).astype(BF16)
        nb_ref[rows, :] = normed
        hidden = dot(normed, up_ref[...]) + bias_ref[...]
        half = 0.5 * (1.0 + lax.erf(hidden * math.sqrt(0.5)))
        active = (hidden * half).astype(BF16)
        act_ref[rows, :] = active
        slope = half + hidden * jnp.exp(-0.5 * hidden * hidden) * (1.0 / math.sqrt(2.0 * math.pi))
        grad_hidden = (dot_last(grad_rows, down_ref[...]) * slope).astype(BF16)
        dh_ref[rows, :] = grad_hidden
        grad_bias += jnp.sum(grad_hidden.astype(F32), axis=0, keepdims=True)
        out_ref[rows, :] = (out_part_ref[rows, :] + dot(active, down_ref[...])).astype(out_ref.dtype)
        upstream = dot_last(grad_hidden, up_ref[...])
        vectors[0] += jnp.sum(normal * upstream, axis=0, keepdims=True)
        vectors[1] += jnp.sum(upstream, axis=0, keepdims=True)
        dx_ref[rows, :] = (dx_part_ref[rows, :] + norm_back(normal, scale, gain * upstream)).astype(dx_ref.dtype)
    grad_up = dot_rows(nb_ref[...], dh_ref[...])
    grad_down = dot_rows(act_ref[...], xg_ref[:, width:])
    rest = grad_ref.shape[1] - up_rows - down_rows
    tail = jnp.concatenate([grad_bias] + vectors + [jnp.zeros((rest - 3, width), F32)], 0)
    for owner in range(owners):
        grad_ref[owner, :up_rows, :] = grad_up[owner * up_rows : (owner + 1) * up_rows, :]
        grad_ref[owner, up_rows : up_rows + down_rows, :] = grad_down[
            owner * down_rows : (owner + 1) * down_rows, :
        ]
        grad_ref[owner, up_rows + down_rows :, :] = tail


def whole(count):
    return [pl.BlockSpec(memory_space=pltpu.VMEM)] * count


def attention(xg, w_qkv, w_out, vectors, bias, cosine, sine, owners):
    tokens, width = xg.shape[0], xg.shape[1] // 2
    part = w_out.shape[0]
    rows = width // owners + part // owners + 16
    shape = jax.ShapeDtypeStruct
    flops = 2 * tokens * width * part * 12 + 2 * 5 * tokens * tokens * part
    return pl.pallas_call(
        attention_kernel,
        out_shape=(
            shape((tokens, width), F32),
            shape((tokens, width), F32),
            shape((owners, rows, width), F32),
        ),
        in_specs=whole(7),
        out_specs=tuple(whole(3)),
        scratch_shapes=[
            pltpu.VMEM((tokens, width), BF16),
            pltpu.VMEM((tokens, part), BF16),
            pltpu.VMEM((tokens, part), BF16),
            pltpu.VMEM((tokens, part), BF16),
            pltpu.VMEM((tokens, part), BF16),
            pltpu.VMEM((part, tokens), BF16),
            pltpu.VMEM((part, tokens), BF16),
            pltpu.VMEM((tokens, part), BF16),
            pltpu.VMEM((tokens, part), F32),
            pltpu.VMEM((part, tokens), F32),
            pltpu.VMEM((part, tokens), F32),
            pltpu.VMEM((tokens, 3 * part), BF16),
        ],
        compiler_params=PARAMS,
        cost_estimate=pl.CostEstimate(
            flops=4 * flops, bytes_accessed=8 * tokens * width * 4, transcendentals=tokens * tokens * 2
        ),
    )(xg, w_qkv, w_out, vectors, bias, cosine, sine)


def feed_forward(xg, w_up, w_down, vectors, bias, out_part, dx_part, owners):
    tokens, width = xg.shape[0], xg.shape[1] // 2
    hidden_width = w_up.shape[1]
    rows = width // owners + hidden_width // owners + 16
    shape = jax.ShapeDtypeStruct
    return pl.pallas_call(
        mlp_kernel,
        out_shape=(
            shape((tokens, width), F32),
            shape((tokens, width), F32),
            shape((owners, rows, width), F32),
        ),
        in_specs=whole(7),
        out_specs=tuple(whole(3)),
        scratch_shapes=[
            pltpu.VMEM((tokens, width), BF16),
            pltpu.VMEM((tokens, hidden_width), BF16),
            pltpu.VMEM((tokens, hidden_width), BF16),
        ],
        compiler_params=PARAMS,
        cost_estimate=pl.CostEstimate(
            flops=12 * tokens * width * hidden_width,
            bytes_accessed=8 * tokens * width * 4,
            transcendentals=2 * tokens * hidden_width,
        ),
    )(xg, w_up, w_down, vectors, bias, out_part, dx_part)


def rotary(tokens, heads):
    ladder = np.arange(ROT // 2, dtype=np.float32)
    frequency = np.exp(ladder * np.float32(-2.0 * math.log(10000.0) / ROT)).astype(np.float32)
    angles = np.arange(tokens, dtype=np.float32)[:, None] * frequency[None, :]
    cosine = np.ones((tokens, HD), np.float32)
    sine = np.zeros((tokens, HD), np.float32)
    half = ROT // 2
    cosine[:, :half] = cosine[:, half:ROT] = np.cos(angles)
    sine[:, half:ROT] = np.sin(angles)
    sine[:, :half] = -sine[:, half:ROT]
    return np.tile(cosine, (1, heads)), np.tile(sine, (1, heads))


def shards_any(
    owners, groups,
    inputs, cotangent, w_qkv, b_qkv, w_out, b_out, w_up, b_up, w_down, b_down,
    gain_one, shift_one, gain_two, shift_two,
):
    rows, width = w_qkv.shape[0], w_qkv.shape[1] // 3
    hidden = w_up.shape[1]
    down_rows = w_down.shape[0]
    local = inputs.shape[1]
    tokens = local * groups
    part = width // groups
    slice_width = hidden // groups
    dp_rows = rows * groups
    group = lax.axis_index("seq")
    owner = lax.axis_index("dp")

    xg = jnp.concatenate([inputs[0], cotangent[0]], axis=1)
    xg = gather_bits(xg, "seq", groups).reshape(tokens, 2 * width)

    devices = owners * groups
    place = [(f % owners) * groups + f // owners for f in range(devices)]
    out_rows = lax.ppermute(w_out, ("dp", "seq"), [(f, place[f]) for f in range(devices)])

    small = jnp.concatenate(
        [b_qkv.reshape(rows, -1), b_up.reshape(rows, -1)]
        + [v[:, None] for v in (b_out, b_down, gain_one, shift_one, gain_two, shift_two)],
        axis=1,
    )
    n_small = small.shape[1]
    n_up = b_up.shape[0] // rows
    small = jnp.pad(small, ((0, 0), (0, width - 3 * part - n_small)))
    blocks = jnp.concatenate(
        [
            w_qkv.reshape(rows, 3, groups, part).transpose(2, 0, 1, 3).reshape(groups, rows, 3 * part),
            jnp.broadcast_to(small[None], (groups,) + small.shape),
            w_up.reshape(rows, owners, groups, -1).transpose(2, 0, 1, 3).reshape(groups, rows, slice_width),
        ],
        axis=2,
    )
    blocks = swap_bits(blocks, "seq", groups).reshape(dp_rows, width + slice_width)
    first = gather_bits(jnp.concatenate([blocks[:, :width], out_rows], axis=0), "dp", owners)
    second = gather_bits(jnp.concatenate([blocks[:, width:], w_down], axis=0), "dp", owners)

    full_qkv = first[:, :dp_rows, : 3 * part].reshape(width, 3 * part)
    full_out = first[:, dp_rows:, :].reshape(part, width)
    small = first[:, :dp_rows, 3 * part : 3 * part + n_small].reshape(width, n_small).astype(F32)
    bias_qkv = lax.dynamic_index_in_dim(
        small[:, :3].reshape(3, groups, part), group, 1, keepdims=False
    ).reshape(1, 3 * part)
    bias_up = lax.dynamic_index_in_dim(
        small[:, 3 : 3 + n_up].reshape(owners, groups, -1), group, 1, keepdims=False
    ).reshape(1, slice_width)
    vectors = small[:, 3 + n_up :].T
    biases = vectors[0] + vectors[1]
    vectors = jnp.concatenate([vectors[2:], jnp.zeros((4, width), F32)], 0)
    full_up = second[:, :dp_rows, :].reshape(width, slice_width)
    full_down = second[:, dp_rows:, :].reshape(slice_width, width)

    cosine, sine = rotary(tokens, part // HD)
    out_part, dx_part, grad_a = attention(
        xg, full_qkv, full_out, vectors, bias_qkv, jnp.asarray(cosine), jnp.asarray(sine), owners
    )
    out_part, dx_part, grad_b = feed_forward(
        xg, full_up, full_down, vectors, bias_up, out_part, dx_part, owners
    )

    grad_a = scatter_bits(grad_a, "dp", owners)
    grad_b = scatter_bits(grad_b, "dp", owners)
    both = jnp.concatenate([out_part, dx_part], axis=1).reshape(groups, local, 2 * width)
    both = scatter_bits(both, "seq", groups)
    outputs = (inputs[0].astype(F32) + both[:, :width] + biases[None]).astype(BF16)[None]
    grad_inputs = (cotangent[0].astype(F32) + both[:, width:]).astype(BF16)[None]

    own_wout = lax.ppermute(
        grad_a[dp_rows : dp_rows + rows, :], ("dp", "seq"), [(place[f], f) for f in range(devices)]
    )
    tail_a = grad_a[dp_rows + rows :, :]
    tail_b = grad_b[dp_rows + down_rows :, :]
    small = jnp.concatenate([tail_a[:4], tail_b[1:3], jnp.zeros((2, width), F32)], 0)
    send = jnp.concatenate(
        [
            grad_a[:dp_rows, : 3 * part].reshape(groups, rows, 3 * part),
            grad_b[:dp_rows, :].reshape(groups, rows, slice_width),
        ],
        axis=2,
    )
    small = jnp.pad(small, ((0, 0), (0, send.shape[2] - width)))
    send = jnp.concatenate([send, jnp.broadcast_to(small[None], (groups,) + small.shape)], axis=1)
    send = swap_bits(send, "seq", groups)
    own_wqkv = send[:, :rows, : 3 * part].reshape(groups, rows, 3, part).transpose(1, 2, 0, 3).reshape(rows, -1)
    own_wup = (
        send[:, :rows, 3 * part :].reshape(groups, rows, owners, -1).transpose(1, 2, 0, 3).reshape(rows, -1)
    )
    small = send[:, rows:, :width]
    index = owner * groups + group
    own_bqkv = lax.dynamic_slice_in_dim(
        small[:, 0, : 3 * part].reshape(groups, 3, part).transpose(1, 0, 2).reshape(-1),
        index * b_qkv.shape[0],
        b_qkv.shape[0],
    )
    sums = jnp.sum(small, axis=0)
    own = lax.dynamic_slice_in_dim(sums, index * rows, rows, axis=1)
    own_bias = lax.dynamic_slice_in_dim(small[0, 3], index * rows, rows)
    own_bup = lax.dynamic_slice_in_dim(tail_b[0], owner * b_up.shape[0], b_up.shape[0])
    return (
        outputs,
        grad_inputs,
        own_wqkv,
        own_bqkv,
        own_wout,
        own_bias,
        own_wup,
        own_bup,
        grad_b[dp_rows : dp_rows + down_rows, :],
        own_bias,
        own[1],
        own[2],
        own[4],
        own[5],
    )


def reversed_bits(value, count):
    result = 0
    for bit in range(count):
        result = result | (((value >> bit) & 1) << (count - 1 - bit))
    return result


def after(value, *others):
    return lax.optimization_barrier((value,) + others)[0]


def spread(value, axis, size, gates=()):
    value, seen = value[None], []
    for step, bit in enumerate(reversed(range(log2(size)))):
        seen.append(exchange(value, axis, size, bit))
        if bit:
            other = after(seen[-1], *gates[step]) if step < len(gates) else seen[-1]
            value = jnp.concatenate([value, other], 0)
    return (value, seen[-1]), seen


def fold(kept, other):
    total = kept + other.astype(F32)
    half = total.shape[0] // 2
    return total[half:].astype(BF16), total[:half]


def finish(kept, other):
    return kept[0] + other[0].astype(F32)


def call(kernel, outs, scratch, flops, transcendentals, *operands, mib=8, far=0):
    return pl.pallas_call(
        kernel,
        out_shape=tuple(outs),
        in_specs=whole(len(operands) - far)
        + [pl.BlockSpec(memory_space=pltpu.HBM)] * far,
        out_specs=tuple(whole(len(outs))),
        scratch_shapes=scratch,
        compiler_params=pltpu.CompilerParams(vmem_limit_bytes=mib * 1024 * 1024),
        cost_estimate=pl.CostEstimate(flops=1, bytes_accessed=1, transcendentals=0),
    )(*operands)


def fetch(pairs, sems):
    copies = [pltpu.make_async_copy(source, to, sems.at[i]) for i, (source, to) in enumerate(pairs)]
    for copy in copies:
        copy.start()
    for copy in copies:
        copy.wait()


def pack_kernel(*refs):
    x_ref, g_ref, refs = refs[0], refs[1], refs[2:]
    count = (len(refs) - 5) // 2
    (sent_ref, kept_ref, both_ref, block_ref, sems), held = refs[count : count + 5], refs[count + 5 :]
    joined = [
        pltpu.make_async_copy(ref, both_ref.at[:, :, pl.ds(i * ref.shape[2], ref.shape[2])], sems.at[count + i])
        for i, ref in enumerate((x_ref, g_ref))
    ]
    for copy in joined:
        copy.start()
    fetch(tuple(zip(refs[:count], held)), sems)
    qkv_ref, up_ref, out_ref, small = held[0], held[1], held[2], held[3:]
    me = lax.axis_index("seq")
    groups, rows, _ = block_ref.shape
    width = qkv_ref.shape[1] // 3
    part = width // groups
    piece = rows * groups
    owners = up_ref.shape[1] // (groups * piece)
    lines = []
    for line in (small[:2], small[2:]):
        values = [ref[...].reshape(1, ref.shape[0]).astype(F32) for ref in line]
        used = sum(ref.shape[0] for ref in line)
        lines.append(jnp.concatenate(values + [jnp.zeros((1, part - used), F32)], 1))
    lines = jnp.concatenate(lines + [jnp.zeros((rows - 2, part), F32)], 0).astype(BF16)
    for group in range(groups):
        for c in range(3):
            start = c * width + group * part
            block_ref[group, :, c * part : (c + 1) * part] = qkv_ref[:, start : start + part]
        block_ref[group, :, 3 * part : width] = lines
        block_ref[group, :, width + up_ref.shape[1] // groups :] = out_ref[...]
        block_ref[group, :, width : width + up_ref.shape[1] // groups] = jnp.concatenate(
            [
                up_ref[:, (k * groups + group) * piece : (k * groups + group + 1) * piece]
                for k in range(owners)
            ],
            1,
        )
    for half in range(groups // 2):
        kept_ref[half] = block_ref[me ^ (2 * half)]
        sent_ref[half] = block_ref[me ^ (2 * half + 1)]
    for copy in joined:
        copy.wait()


def payload_kernel(kept_ref, near_ref, far_ref, down_ref, first_ref, second_ref, sem):
    me = lax.axis_index("seq")
    width = down_ref.shape[1]
    part, rows = width // 4, first_ref.shape[0] // 8
    copy = pltpu.make_async_copy(down_ref, second_ref.at[pl.ds(4 * rows, down_ref.shape[0])], sem)
    copy.start()
    hidden = kept_ref.shape[2] - 2 * width
    index = lax.broadcasted_iota(jnp.int32, (rows, part), 0)
    mine = index // 2 == lax.axis_index("dp")
    for step, block in enumerate((kept_ref.at[0], near_ref.at[0], far_ref.at[0], far_ref.at[1])):
        group = me ^ step
        lanes = pl.ds(pl.multiple_of(group * part, part), part)
        second_ref[pl.ds(pl.multiple_of(group * rows, rows), rows), :] = block[:, width : width + hidden]
        for c in range(3):
            first_ref[c * rows : (c + 1) * rows, lanes] = block[:, c * part : (c + 1) * part]
        line = block[:, 3 * part : width].astype(F32)
        line = jnp.where(index % 2 == 0, line[0:1], line[1:2])
        first_ref[3 * rows : 4 * rows, lanes] = jnp.where(mine, line, 0.0).astype(BF16)
        first_ref[pl.ds(pl.multiple_of((4 + group) * rows, rows), rows), :] = block[:, width + hidden :]
    copy.wait()


def merge_kernel(bit, rows, mine_ref, other_ref, out_ref):
    part = mine_ref.shape[0] - 5 * rows
    small, last = slice(part, part + rows), slice(part + rows, part + 5 * rows)
    out_ref[:part, :] = mine_ref[:part, :]
    out_ref[part : 2 * part, :] = other_ref[:part, :]
    out_ref[2 * part : 2 * part + rows, :] = mine_ref[small, :] + other_ref[small, :]
    same = (lax.axis_index("dp") >> bit) & 1 == (lax.axis_index("seq") >> (bit - 1)) & 1

    @pl.when(same)
    def _():
        out_ref[2 * part + rows :, :] = mine_ref[last, :]

    @pl.when(jnp.logical_not(same))
    def _():
        out_ref[2 * part + rows :, :] = other_ref[last, :]


def sources(pair, me):
    half = pair[0].shape[0]
    count = log2(2 * half)
    for slot in range(2 * half):
        ref = pair[slot // half]
        yield ref.at[slot % half], me ^ reversed_bits(slot, count)


def project_kernel(
    first_ref, other_ref, x_ref, y_ref, cos_ref, sin_ref, table_ref,
    xg_ref, na_ref, q_ref, qt_ref, k_ref, v_ref, da_ref, dat_ref, wq_ref, wo_ref, vec_ref,
):
    owner, group = lax.axis_index("dp"), lax.axis_index("seq")
    width = first_ref.shape[1]
    groups = 2 * x_ref.shape[0]
    part = width // groups
    rows = first_ref.shape[0] // 17
    owners = width // (rows * groups)
    local = x_ref.shape[1]
    for slot in range(owners):
        block = (first_ref, other_ref)[slot // 4].at[pl.ds(slot % 4 * 3 * rows, 3 * rows)]
        rank = owner ^ reversed_bits(slot, log2(owners))
        for g in range(groups):
            lanes = slice(g * part, (g + 1) * part)
            to = pl.ds(pl.multiple_of((rank * groups + g) * rows, rows), rows)
            for c in range(3):
                wq_ref[to, c * part : (c + 1) * part] = block[c * rows : (c + 1) * rows, lanes]
    for slot, ref in enumerate((first_ref, other_ref)):
        x = (owner & 1) ^ slot
        wo_ref[pl.ds(pl.multiple_of(x * 4 * rows, 4 * rows), 4 * rows), :] = ref[13 * rows :, :]
    devices = owners * groups
    small = first_ref[12 * rows : 13 * rows, :].astype(F32) + other_ref[12 * rows : 13 * rows, :].astype(F32)
    line_one, line_two = (
        jnp.concatenate(
            [
                small[2 * rank + i : 2 * rank + i + 1, g * part : (g + 1) * part]
                for rank in range(owners)
                for g in range(groups)
            ],
            0,
        ).astype(BF16)
        for i in range(2)
    )

    def place_values(line, lane_of, device_of_column):
        columns = lane_of.shape[1]
        pick = lax.broadcasted_iota(jnp.int32, (line.shape[1], columns), 0) == lane_of
        values = dot(line, jnp.where(pick, 1.0, 0.0).astype(BF16))
        held = lax.broadcasted_iota(jnp.int32, (devices, columns), 0) == device_of_column
        return jnp.sum(jnp.where(held, values, 0.0), axis=0, keepdims=True)

    column = lax.broadcasted_iota(jnp.int32, (1, width), 1)
    own = [place_values(line_two, column % rows + v * rows, column // rows) for v in range(6)]
    piece = rows * groups
    start = 3 * width // devices
    bias_up = place_values(line_one, column % piece + start, column // piece * groups + group)
    lane_of = jnp.concatenate(
        [table_ref[0:1, pl.ds(pl.multiple_of(c * width + group * part, part), part)] for c in range(3)], 1
    )
    owner_of = jnp.concatenate(
        [table_ref[1:2, pl.ds(pl.multiple_of(c * width + group * part, part), part)] for c in range(3)], 1
    )
    bias = place_values(line_one, lane_of, owner_of)
    gain, shift = own[2], own[3]
    vec_ref[...] = jnp.concatenate(
        own[2:] + [own[0] + own[1], bias_up, jnp.zeros((2, width), F32)], 0
    )

    lane = lax.broadcasted_iota(jnp.int32, (local, part), 1)
    turn = lane % HD < ROT // 2

    def partner(value):
        return jnp.where(
            turn, pltpu.roll(value, part - ROT // 2, 1), pltpu.roll(value, ROT // 2, 1)
        )

    for block, rank in sources((x_ref, y_ref), group):
        start = pl.multiple_of(rank * local, local)
        to = pl.ds(start, local)
        both = block[...]
        xg_ref[to, :] = both
        normal, _ = standardize(both[:, :width].astype(F32))
        normed = (normal * gain + shift).astype(BF16)
        na_ref[to, :] = normed
        projected = dot(normed, wq_ref[...]) + bias
        cosine, sine = cos_ref[to, :], sin_ref[to, :]
        query = projected[:, :part]
        query = query * cosine + partner(query) * sine
        key = projected[:, part : 2 * part]
        key = key * cosine + partner(key) * sine
        query = query.astype(BF16).astype(F32) * HD**-0.5
        q_ref[to, :] = query.astype(BF16)
        qt_ref[:, to] = query.T.astype(BF16)
        k_ref[to, :] = key.astype(BF16)
        v_ref[to, :] = projected[:, 2 * part :].astype(BF16)
        grad_att = dot_last(both[:, width:], wo_ref[...]).astype(BF16)
        da_ref[to, :] = grad_att
        dat_ref[:, to] = grad_att.astype(F32).T.astype(BF16)


def attend_kernel(
    xg_ref, na_ref, q_ref, qt_ref, k_ref, v_ref, da_ref, dat_ref, wq_ref, cos_ref, sin_ref,
    att_ref, dp_ref, small_ref, sent_ref, kept_ref,
    dq_ref, dkt_ref, dvt_ref, gq_ref, go_ref,
):
    owner = lax.axis_index("dp")
    tokens, part = q_ref.shape
    width = na_ref.shape[1]
    groups = width // part
    owners = 2 * sent_ref.shape[0]
    rows = part // owners
    lane = lax.broadcasted_iota(jnp.int32, (BLOCK, part), 1)
    turn = lane % HD < ROT // 2

    def partner(value):
        return jnp.where(
            turn, pltpu.roll(value, part - ROT // 2, 1), pltpu.roll(value, ROT // 2, 1)
        )

    dkt_ref[...] = jnp.zeros_like(dkt_ref)
    dvt_ref[...] = jnp.zeros_like(dvt_ref)
    below = lax.broadcasted_iota(jnp.int32, (BLOCK, BLOCK), 0) >= lax.broadcasted_iota(
        jnp.int32, (BLOCK, BLOCK), 1
    )
    zero = jnp.zeros((), BF16)
    for block in range(tokens // BLOCK):
        at = pl.ds(block * BLOCK, BLOCK)
        seen = (block + 1) * BLOCK
        attended = jnp.zeros((BLOCK, part), F32)
        grad_query = jnp.zeros((BLOCK, part), F32)
        for head in range(part // HD):
            mine = lane // HD == head
            mine_t = lax.broadcasted_iota(jnp.int32, (part, BLOCK), 0) // HD == head
            query = jnp.where(mine, q_ref[at, :], zero)
            grad_att = jnp.where(mine, da_ref[at, :], zero)
            scores = dot_last(query, k_ref[:seen, :])
            last = jnp.where(below, scores[:, seen - BLOCK :], -1e30)
            scores = last if block == 0 else jnp.concatenate([scores[:, : seen - BLOCK], last], 1)
            raised = jnp.exp(scores - jnp.max(scores, axis=-1, keepdims=True))
            probs = raised * (1.0 / jnp.sum(raised, axis=-1, keepdims=True))
            probs_low = probs.astype(BF16)
            attended = jnp.where(mine, dot(probs_low, v_ref[:seen, :]), attended)
            grad_probs = dot_last(grad_att, v_ref[:seen, :])
            inner = jnp.sum(probs * grad_probs, axis=-1, keepdims=True)
            grad_scores = (probs * (grad_probs - inner)).astype(BF16)
            grad_query = jnp.where(mine, dot(grad_scores, k_ref[:seen, :]), grad_query)
            query_t = jnp.where(mine_t, qt_ref[:, at], zero)
            grad_att_t = jnp.where(mine_t, dat_ref[:, at], zero)
            dkt_ref[:, :seen] += dot(query_t, grad_scores)
            dvt_ref[:, :seen] += dot(grad_att_t, probs_low)
        att_ref[at, :] = attended.astype(BF16)
        dq_ref[at, :] = grad_query * HD**-0.5

    vectors = [jnp.zeros((1, width), F32) for _ in range(3)]
    grad_bias = jnp.zeros((1, 3 * part), F32)
    for block in range(tokens // BLOCK):
        at = pl.ds(block * BLOCK, BLOCK)
        cosine, sine = cos_ref[at, :], sin_ref[at, :]
        grad_query = dq_ref[at, :]
        grad_query = grad_query * cosine - partner(grad_query) * sine
        grad_key = dkt_ref[:, at].T
        grad_key = grad_key * cosine - partner(grad_key) * sine
        grad_proj = jnp.concatenate([grad_query, grad_key, dvt_ref[:, at].T], 1).astype(BF16)
        dp_ref[at, :] = grad_proj
        grad_bias += jnp.sum(grad_proj.astype(F32), axis=0, keepdims=True)
        upstream = dot_last(grad_proj, wq_ref[...])
        normal, _ = standardize(xg_ref[at, :width].astype(F32))
        vectors[0] += jnp.sum(normal * upstream, axis=0, keepdims=True)
        vectors[1] += jnp.sum(upstream, axis=0, keepdims=True)
        vectors[2] += jnp.sum(xg_ref[at, width:].astype(F32), axis=0, keepdims=True)

    gq_ref[...] = dot_rows(na_ref[...], dp_ref[...])
    go_ref[...] = dot_rows(att_ref[...], xg_ref[:, width:])
    small_ref[...] = jnp.concatenate(
        [jnp.concatenate([grad_bias, jnp.zeros((1, width - 3 * part), F32)], 1)]
        + vectors
        + [jnp.zeros((4, width), F32)],
        0,
    )
    for ref, rank in sources((kept_ref, sent_ref), owner):
        kind = ref.dtype
        for g in range(groups):
            at = pl.ds(pl.multiple_of((rank * groups + g) * rows, rows), rows)
            for c in range(3):
                ref[c * rows : (c + 1) * rows, g * part : (g + 1) * part] = gq_ref[
                    at, c * part : (c + 1) * part
                ].astype(kind)
        ref[3 * rows : 4 * rows, :] = go_ref[pl.ds(pl.multiple_of((rank % 2 * 4 + rank // 2) * rows, rows), rows), :].astype(kind)


def hidden_kernel(
    second_ref, other_ref, xg_ref, vec_ref, small_ref,
    act_ref, dh_ref, up_ref, down_ref, sent_ref, kept_ref,
    nb_ref, gu_ref,
):
    owner = lax.axis_index("dp")
    tokens, hidden_width = act_ref.shape
    width = vec_ref.shape[1]
    rows = second_ref.shape[1] // 2
    for block, rank in sources((second_ref, other_ref), owner):
        at = pl.ds(pl.multiple_of(rank * rows, rows), rows)
        up_ref[at, :] = block[:rows, :]
        down_ref[at, :] = block[rows:, :]
    gain, shift, bias = vec_ref[2:3, :], vec_ref[3:4, :], vec_ref[5:6, :]
    vectors = [jnp.zeros((1, width), F32) for _ in range(2)]
    grad_bias = jnp.zeros((1, hidden_width), F32)
    for block in range(tokens // BLOCK):
        at = pl.ds(block * BLOCK, BLOCK)
        normal, _ = standardize(xg_ref[at, :width].astype(F32))
        normed = (normal * gain + shift).astype(BF16)
        nb_ref[at, :] = normed
        hidden = dot(normed, up_ref[...]) + bias
        half = 0.5 * (1.0 + lax.erf(hidden * math.sqrt(0.5)))
        act_ref[at, :] = (hidden * half).astype(BF16)
        slope = half + hidden * jnp.exp(-0.5 * hidden * hidden) * (1.0 / math.sqrt(2.0 * math.pi))
        grad_hidden = (dot_last(xg_ref[at, width:], down_ref[...]) * slope).astype(BF16)
        dh_ref[at, :] = grad_hidden
        grad_bias += jnp.sum(grad_hidden.astype(F32), axis=0, keepdims=True)
        upstream = dot_last(grad_hidden, up_ref[...])
        vectors[0] += jnp.sum(normal * upstream, axis=0, keepdims=True)
        vectors[1] += jnp.sum(upstream, axis=0, keepdims=True)
    gu_ref[...] = dot_rows(nb_ref[...], dh_ref[...])
    extra = sent_ref.shape[1] - rows
    tail = jnp.concatenate([grad_bias] + vectors + [small_ref[:4, :], jnp.zeros((extra - 7, width), F32)], 0)
    for ref, rank in sources((kept_ref, sent_ref), owner):
        ref[:rows, :] = gu_ref[pl.ds(pl.multiple_of(rank * rows, rows), rows), :].astype(ref.dtype)
        ref[rows:, :] = tail.astype(ref.dtype)


def down_kernel(act_ref, xg_ref, sent_ref, kept_ref, gd_ref):
    width = sent_ref.shape[2]
    rows = sent_ref.shape[1]
    gd_ref[...] = dot_rows(act_ref[...], xg_ref[:, width:])
    for ref, rank in sources((kept_ref, sent_ref), lax.axis_index("dp")):
        ref[...] = gd_ref[pl.ds(pl.multiple_of(rank * rows, rows), rows), :].astype(ref.dtype)


def join_kernel(
    xg_ref, att_ref, wo_ref, act_ref, down_ref, vec_ref, dp_ref, wq_ref, dh_ref, up_ref,
    sent_ref, kept_ref,
):
    group = lax.axis_index("seq")
    local = sent_ref.shape[1]
    width = wo_ref.shape[1]
    gain_one, gain_two, bias = vec_ref[0:1, :], vec_ref[2:3, :], vec_ref[4:5, :]
    for step in range(2 * sent_ref.shape[0]):
        at = pl.ds(pl.multiple_of((group ^ step) * local, local), local)
        ref = (kept_ref, sent_ref)[step % 2].at[step // 2]
        out = dot(att_ref[at, :], wo_ref[...]) + dot(act_ref[at, :], down_ref[...])
        rows_in = xg_ref[at, :width].astype(F32)
        normal, scale = standardize(rows_in)
        inner = gain_one * dot_last(dp_ref[at, :], wq_ref[...]) + gain_two * dot_last(dh_ref[at, :], up_ref[...])
        grad = norm_back(normal, scale, inner)
        if step == 0:
            out = out + rows_in + bias
            grad = grad + xg_ref[at, width:].astype(F32)
        ref[:, :width] = out.astype(ref.dtype)
        ref[:, width:] = grad.astype(ref.dtype)


def deal_kernel(a_ref, b_ref, sent_ref, kept_ref):
    me = lax.axis_index("seq")
    width = a_ref.shape[1]
    part = width // 4
    rows = a_ref.shape[0] // 4
    kind = sent_ref.dtype
    small = jnp.concatenate(
        [b_ref[4 * rows + 3 : 4 * rows + 6, :], b_ref[4 * rows + 1 : 4 * rows + 3, :], jnp.zeros((rows - 5, width), F32)], 0
    )
    for step in range(4):
        group = me ^ step
        ref = (kept_ref, sent_ref)[step // 2].at[step % 2]
        lanes = pl.ds(pl.multiple_of(group * part, part), part)
        for c in range(3):
            ref[:rows, c * part : (c + 1) * part] = a_ref[c * rows : (c + 1) * rows, lanes].astype(kind)
        ref[:rows, 3 * part :] = b_ref[pl.ds(pl.multiple_of(group * rows, rows), rows), :].astype(kind)
        ref[rows:, :width] = small.astype(kind)
        ref[rows:, width:] = jnp.zeros((rows, 3 * part), kind)


def collect_kernel(
    kept_ref, near_ref, far_ref, b_ref, out_ref, down_kept_ref, down_other_ref,
    qkv_ref, up_ref, wout_ref, bqkv_ref, bias_ref, twin_ref, bup_ref, gain_one_ref, shift_one_ref, gain_two_ref, shift_two_ref, down_ref,
    block_ref,
):
    me = lax.axis_index("seq")
    place = lax.axis_index("dp") * 4 + me
    rows = qkv_ref.shape[0]
    width = qkv_ref.shape[1] // 3
    part = width // 4
    piece = 4 * rows
    for step, block in enumerate((kept_ref.at[0], far_ref.at[0], near_ref.at[0], far_ref.at[1])):
        block_ref[me ^ step] = block[...].astype(F32)
    for g in range(4):
        for c in range(3):
            qkv_ref[:, c * width + g * part : c * width + (g + 1) * part] = block_ref[
                g, :rows, c * part : (c + 1) * part
            ]
    for k in range(up_ref.shape[1] // (4 * piece)):
        start = 3 * part + k * piece
        up_ref[:, 4 * k * piece : 4 * (k + 1) * piece] = jnp.concatenate(
            [block_ref[g, :rows, start : start + piece] for g in range(4)], 1
        )
    wout_ref[...] = out_ref[...]
    down_ref[...] = down_kept_ref[0] + down_other_ref[0].astype(F32)

    def own(values, ref, index):
        size, count = values.shape[1], ref.shape[0]
        values = pltpu.roll(values, (size - index * count) % size, 1)[0:1, :count]
        ref[...] = values.reshape(count)

    sums = sum(block_ref[g, rows : rows + 8, :width] for g in range(4))
    for i, ref in enumerate((gain_one_ref, shift_one_ref, gain_two_ref, shift_two_ref)):
        own(sums[i + 1 : i + 2], ref, place)
    bias = jnp.concatenate(
        [block_ref[g, rows : rows + 1, c * part : (c + 1) * part] for c in range(3) for g in range(4)], 1
    )
    own(bias, bqkv_ref, place)
    own(b_ref[4 * rows + 6 : 4 * rows + 7, :], bias_ref, place)
    twin_ref[...] = bias_ref[...]
    own(b_ref[4 * rows : 4 * rows + 1, :], bup_ref, lax.axis_index("dp"))


def shards(
    owners, groups,
    inputs, cotangent, w_qkv, b_qkv, w_out, b_out, w_up, b_up, w_down, b_down,
    gain_one, shift_one, gain_two, shift_two,
):
    rows, width = w_qkv.shape[0], w_qkv.shape[1] // 3
    hidden = w_up.shape[1] // groups
    local = inputs.shape[1]
    if rows % 16 or groups != 4 or owners != 8 or local != BLOCK or hidden != width:
        return shards_any(
            owners, groups, inputs, cotangent, w_qkv, b_qkv, w_out, b_out, w_up, b_up, w_down, b_down,
            gain_one, shift_one, gain_two, shift_two,
        )
    tokens = local * groups
    part = width // groups
    devices = owners * groups
    half = owners // 2
    heads = part // HD
    shape = jax.ShapeDtypeStruct

    target = [(f % 4 * 2 + f // 4 % 2) * groups + f // owners for f in range(devices)]

    block = shape((2, rows, 2 * width + hidden), BF16)
    params = (w_qkv, w_up, w_out, b_qkv, b_up, b_out, b_down, gain_one, shift_one, gain_two, shift_two)
    sent, kept, x = call(
        pack_kernel,
        (block, block, shape((1, local, 2 * width), BF16)),
        [pltpu.VMEM((groups, rows, 2 * width + hidden), BF16), pltpu.SemaphoreType.DMA((len(params) + 2,))]
        + [pltpu.VMEM(p.shape, BF16) for p in params],
        0, 0, inputs, cotangent, *params, mib=63, far=len(params) + 2,
    )
    near = exchange(sent, "seq", groups, 0)
    far = exchange(jnp.stack([kept[1], near[1]]), "seq", groups, 1)
    first, second = call(
        payload_kernel,
        (shape((8 * rows, width), BF16), shape((4 * rows + w_down.shape[0], width), BF16)),
        [pltpu.SemaphoreType.DMA], 0, 0, kept, near, far, w_down, mib=4, far=1,
    )
    def merged(bit, mine, other):
        out = shape((2 * mine.shape[0] - 5 * rows, width), BF16)
        return call(functools.partial(merge_kernel, bit, rows), (out,), [], 0, 0, mine, other, mib=4)[0]

    x = after(x, far)
    x_other = exchange(x, "seq", groups, 1)
    other = exchange(first, "dp", owners, 2)
    second = after(second, other)[None]
    first = merged(2, first, other)
    other, second_other = exchange(first, "dp", owners, 1), exchange(second, "dp", owners, 2)
    other, second_other, x_other = lax.optimization_barrier((other, second_other, x_other))
    first, second = merged(1, first, other), jnp.concatenate([second, second_other], 0)
    x = jnp.concatenate([x, x_other], 0)
    first = (first, exchange(first, "dp", owners, 0))
    x_pair = (x, exchange(x, "seq", groups, 0))
    second_other = exchange(second, "dp", owners, 1)

    cosine, sine = (jnp.asarray(t) for t in rotary(tokens, heads))
    column = np.arange(3 * width, dtype=np.int32)
    own = 3 * width // devices
    table = np.zeros((8, 3 * width), np.int32)
    table[0], table[1] = column % own, column // own
    wide, narrow, turned = shape((tokens, width), BF16), shape((tokens, part), BF16), shape((part, tokens), BF16)
    xg, normed_a, query, query_t, key, value, grad_att, grad_att_t, full_qkv, full_out, vectors = call(
        project_kernel,
        (shape((tokens, 2 * width), BF16), wide, narrow, turned, narrow, narrow, narrow, turned)
        + (shape((width, 3 * part), BF16), shape((part, width), BF16), shape((8, width), F32)),
        [], 2 * tokens * width * 4 * part, 0,
        *first, *x_pair, cosine, sine, jnp.asarray(table),
    )
    second = jnp.concatenate([second, after(second_other, normed_a)], 0)
    second = (second, exchange(second, "dp", owners, 0))
    chunk = 5 * rows
    attended, grad_proj, small, sent_a, kept_a = call(
        attend_kernel,
        (narrow, shape((tokens, 3 * part), BF16), shape((8, width), F32))
        + (shape((half, 4 * rows, width), BF16), shape((half, 4 * rows, width), F32)),
        [
            pltpu.VMEM((tokens, part), F32),
            pltpu.VMEM((part, tokens), F32),
            pltpu.VMEM((part, tokens), F32),
            pltpu.VMEM((width, 3 * part), F32),
            pltpu.VMEM((part, width), F32),
        ],
        8 * tokens * tokens * part * 6, 2 * tokens * tokens,
        xg, normed_a, after(query, second_other), query_t, key, value, grad_att, grad_att_t, full_qkv, cosine, sine,
        mib=16,
    )
    other_a = exchange(sent_a, "dp", owners, 0)
    active, grad_hidden, full_up, full_down, sent_u, kept_u = call(
        hidden_kernel,
        (wide, wide, shape((width, hidden), BF16), shape((hidden, width), BF16))
        + (shape((half, chunk, width), BF16), shape((half, chunk, width), F32)),
        [
            pltpu.VMEM((tokens, width), BF16),
            pltpu.VMEM((width, hidden), F32),
        ],
        8 * tokens * width * hidden, 2 * tokens * hidden,
        *second, xg, vectors, small,
        mib=16,
    )
    other_u = exchange(sent_u, "dp", owners, 0)
    sent_a, kept_a = fold(kept_a, other_a)
    other_a = exchange(sent_a, "dp", owners, 1)
    sent_x, kept_x = call(
        join_kernel,
        (shape((2, local, 2 * width), BF16), shape((2, local, 2 * width), F32)),
        [],
        4 * tokens * width * hidden, 0,
        xg, attended, full_out, active, full_down, vectors,
        grad_proj, full_qkv, grad_hidden, full_up,
    )
    down_rows = w_down.shape[0]
    sent_d, kept_d = call(
        down_kernel,
        (shape((half, down_rows, width), BF16), shape((half, down_rows, width), F32)),
        [pltpu.VMEM((hidden, width), F32)],
        2 * tokens * width * hidden, 0,
        active, xg,
    )
    other_x = exchange(after(sent_x, other_u, other_a), "seq", groups, 0)
    other_u, other_x, sent_d, = lax.optimization_barrier((other_u, other_x, sent_d,))
    other_d = exchange(sent_d, "dp", owners, 0)
    sent_u, kept_u = fold(kept_u, other_u)
    other_u = exchange(sent_u, "dp", owners, 1)
    sent_a, kept_a = fold(kept_a, other_a)
    other_a = exchange(sent_a, "dp", owners, 2)
    sent_x, kept_x = fold(kept_x, other_x)
    other_x = exchange(sent_x, "seq", groups, 1)
    sent_d, kept_d = fold(kept_d, other_d)
    other_u, other_a, sent_d, kept_d, = lax.optimization_barrier((other_u, other_a, sent_d, kept_d,))
    sent_u, kept_u = fold(kept_u, other_u)
    other_u = exchange(sent_u, "dp", owners, 2)
    grad_a = finish(kept_a, other_a)
    own_wout = lax.ppermute(grad_a[3 * rows :, :], ("dp", "seq"), [(target[f], f) for f in range(devices)])
    other_d = exchange(sent_d, "dp", owners, 1)
    other_u, other_d, other_x, = lax.optimization_barrier((other_u, other_d, other_x,))
    grad_u = finish(kept_u, other_u)
    sent_d, kept_d = fold(kept_d, other_d)
    block = shape((2, 2 * rows, 3 * part + hidden), BF16)
    sent, kept = call(deal_kernel, (block, block), [], 0, 0, grad_a, grad_u)
    near = exchange(sent, "seq", groups, 1)
    other_d = exchange(sent_d, "dp", owners, 2)
    both = finish(kept_x, other_x)
    outputs, grad_inputs = (v.astype(BF16)[None] for v in (both[:, :width], both[:, width:]))
    far = exchange(jnp.stack([kept[1], near[1]]), "seq", groups, 0)
    vector = shape((rows,), F32)
    own_wqkv, own_wup, own_wout, own_bqkv, own_bias, twin_bias, own_bup, *own, grad_d = call(
        collect_kernel,
        (shape(w_qkv.shape, F32), shape(w_up.shape, F32), shape(w_out.shape, F32))
        + (shape(b_qkv.shape, F32), vector, vector, shape(b_up.shape, F32), vector, vector, vector, vector, shape(w_down.shape, F32)),
        [pltpu.VMEM((groups, 2 * rows, 3 * part + hidden), F32)],
        0, 0, kept, near, far, grad_u, own_wout, kept_d, other_d,
    )
    return (
        outputs,
        grad_inputs,
        own_wqkv,
        own_bqkv,
        own_wout,
        own_bias,
        own_wup,
        own_bup,
        grad_d,
        twin_bias,
        *own,
    )


def solution(mesh):
    rows = P("dp", "seq", None)
    matrix, vector = P(("dp", "seq"), None), P(("dp", "seq"))
    weights = (matrix, vector) * 4
    return jax.shard_map(
        functools.partial(shards, mesh.shape["dp"], mesh.shape["seq"]),
        mesh=mesh,
        in_specs=(rows, rows) + weights + (vector,) * 4,
        out_specs=(rows, rows) + weights + (vector,) * 4,
        check_vma=False,
    )
```

```python
import functools
import math

import jax
import jax.numpy as jnp
import numpy as np
from jax import lax
from jax.experimental import pallas as pl
from jax.experimental.pallas import tpu as pltpu
from jax.sharding import PartitionSpec as P

HD = 64
ROT = 16
EPS = 1e-05
BLOCK = 256
F32 = jnp.float32
BF16 = jnp.bfloat16
PARAMS = pltpu.CompilerParams(vmem_limit_bytes=48 * 1024 * 1024)


def log2(count):
    assert count & (count - 1) == 0
    return count.bit_length() - 1


def exchange(value, axis, size, bit):
    return lax.ppermute(value, axis, [(i, i ^ (1 << bit)) for i in range(size)])


def flag_of(axis, bit):
    return (lax.axis_index(axis) >> bit) & 1 == 1


def gather_bits(value, axis, size):
    shape = value.shape
    for done, bit in enumerate(reversed(range(log2(size)))):
        other = exchange(value, axis, size, bit)
        upper = flag_of(axis, bit)
        value = jnp.where(
            upper,
            jnp.stack([other, value], done),
            jnp.stack([value, other], done),
        )
    return value.reshape((size,) + shape)


def swap_bits(blocks, axis, size):
    count = log2(size)
    rest = blocks.shape[1:]
    value = blocks.reshape((2,) * count + rest)
    for bit in range(count):
        place = count - 1 - bit
        low = lax.index_in_dim(value, 0, place, keepdims=False)
        high = lax.index_in_dim(value, 1, place, keepdims=False)
        upper = flag_of(axis, bit)
        other = exchange(jnp.where(upper, low, high), axis, size, bit)
        value = jnp.stack([jnp.where(upper, other, low), jnp.where(upper, high, other)], place)
    return value.reshape((size,) + rest)


def scatter_bits(blocks, axis, size):
    count = log2(size)
    rest = blocks.shape[1:]
    value = blocks.reshape((2,) * count + rest)
    for bit in range(count):
        place = count - 1 - bit
        low = lax.index_in_dim(value, 0, place, keepdims=False)
        high = lax.index_in_dim(value, 1, place, keepdims=False)
        upper = flag_of(axis, bit)
        sent = jnp.where(upper, low, high).astype(BF16)
        value = jnp.where(upper, high, low).astype(F32) + exchange(sent, axis, size, bit).astype(F32)
    return value


def dot(left, right):
    return lax.dot_general(left, right, (((1,), (0,)), ((), ())), preferred_element_type=F32)


def dot_rows(left, right):
    return lax.dot_general(left, right, (((0,), (0,)), ((), ())), preferred_element_type=F32)


def dot_last(left, right):
    return lax.dot_general(left, right, (((1,), (1,)), ((), ())), preferred_element_type=F32)


def standardize(rows):
    average = jnp.mean(rows, axis=-1, keepdims=True)
    centered = rows - average
    variance = jnp.mean(centered * centered, axis=-1, keepdims=True)
    scale = lax.rsqrt(variance + EPS)
    return centered * scale, scale


def norm_back(normal, scale, inner):
    first = jnp.mean(inner, axis=-1, keepdims=True)
    second = jnp.mean(inner * normal, axis=-1, keepdims=True)
    return scale * (inner - first - normal * second)


def attention_kernel(
    xg_ref, wq_ref, wo_ref, vec_ref, bias_ref, cos_ref, sin_ref,
    out_ref, dx_ref, grad_ref,
    na_ref, q_ref, k_ref, v_ref, da_ref, qt_ref, dat_ref, att_ref, dq_ref, dkt_ref, dvt_ref, dp_ref,
):
    tokens = xg_ref.shape[0]
    width = xg_ref.shape[1] // 2
    part = wo_ref.shape[0]
    heads = part // HD
    owners, _, _ = grad_ref.shape
    own_rows = width // owners
    out_rows = part // owners
    gain = vec_ref[0:1, :]
    shift = vec_ref[1:2, :]
    lane = lax.broadcasted_iota(jnp.int32, (BLOCK, part), 1)
    turn = lane % HD < ROT // 2

    def partner(value):
        return jnp.where(
            turn, pltpu.roll(value, part - ROT // 2, 1), pltpu.roll(value, ROT // 2, 1)
        )

    for block in range(tokens // BLOCK):
        rows = pl.ds(block * BLOCK, BLOCK)
        normal, _ = standardize(xg_ref[rows, :width].astype(F32))
        normed = (normal * gain + shift).astype(BF16)
        na_ref[rows, :] = normed
        projected = dot(normed, wq_ref[...]) + bias_ref[...]
        cosine, sine = cos_ref[rows, :], sin_ref[rows, :]
        query = projected[:, :part]
        query = query * cosine + partner(query) * sine
        key = projected[:, part : 2 * part]
        key = key * cosine + partner(key) * sine
        query = query.astype(BF16).astype(F32) * HD**-0.5
        q_ref[rows, :] = query.astype(BF16)
        qt_ref[:, rows] = query.T.astype(BF16)
        k_ref[rows, :] = key.astype(BF16)
        v_ref[rows, :] = projected[:, 2 * part :].astype(BF16)
        grad_att = dot_last(xg_ref[rows, width:], wo_ref[...]).astype(BF16)
        da_ref[rows, :] = grad_att
        dat_ref[:, rows] = grad_att.astype(F32).T.astype(BF16)

    dkt_ref[...] = jnp.zeros_like(dkt_ref)
    dvt_ref[...] = jnp.zeros_like(dvt_ref)
    below = lax.broadcasted_iota(jnp.int32, (BLOCK, BLOCK), 0) >= lax.broadcasted_iota(
        jnp.int32, (BLOCK, BLOCK), 1
    )
    zero = jnp.zeros((), BF16)
    for block in range(tokens // BLOCK):
        rows = pl.ds(block * BLOCK, BLOCK)
        seen = (block + 1) * BLOCK
        attended = jnp.zeros((BLOCK, part), F32)
        grad_query = jnp.zeros((BLOCK, part), F32)
        for head in range(heads):
            mine = lane // HD == head
            mine_t = lax.broadcasted_iota(jnp.int32, (part, BLOCK), 0) // HD == head
            query = jnp.where(mine, q_ref[rows, :], zero)
            grad_att = jnp.where(mine, da_ref[rows, :], zero)
            scores = dot_last(query, k_ref[:seen, :])
            last = jnp.where(below, scores[:, seen - BLOCK :], -1e30)
            scores = last if block == 0 else jnp.concatenate([scores[:, : seen - BLOCK], last], 1)
            raised = jnp.exp(scores - jnp.max(scores, axis=-1, keepdims=True))
            probs = raised * (1.0 / jnp.sum(raised, axis=-1, keepdims=True))
            probs_low = probs.astype(BF16)
            attended = jnp.where(mine, dot(probs_low, v_ref[:seen, :]), attended)
            grad_probs = dot_last(grad_att, v_ref[:seen, :])
            inner = jnp.sum(probs * grad_probs, axis=-1, keepdims=True)
            grad_scores = (probs * (grad_probs - inner)).astype(BF16)
            grad_query = jnp.where(mine, dot(grad_scores, k_ref[:seen, :]), grad_query)
            query_t = jnp.where(mine_t, qt_ref[:, rows], zero)
            grad_att_t = jnp.where(mine_t, dat_ref[:, rows], zero)
            dkt_ref[:, :seen] += dot(query_t, grad_scores)
            dvt_ref[:, :seen] += dot(grad_att_t, probs_low)
        att_ref[rows, :] = attended.astype(BF16)
        dq_ref[rows, :] = grad_query * HD**-0.5

    vectors = [jnp.zeros((1, width), F32) for _ in range(3)]
    grad_bias = jnp.zeros((1, 3 * part), F32)
    for block in range(tokens // BLOCK):
        rows = pl.ds(block * BLOCK, BLOCK)
        cosine, sine = cos_ref[rows, :], sin_ref[rows, :]
        grad_query = dq_ref[rows, :]
        grad_query = grad_query * cosine - partner(grad_query) * sine
        grad_key = dkt_ref[:, rows].T
        grad_key = grad_key * cosine - partner(grad_key) * sine
        grad_value = dvt_ref[:, rows].T
        grad_proj = jnp.concatenate([grad_query, grad_key, grad_value], 1).astype(BF16)
        dp_ref[rows, :] = grad_proj
        grad_bias += jnp.sum(grad_proj.astype(F32), axis=0, keepdims=True)
        out_ref[rows, :] = dot(att_ref[rows, :], wo_ref[...])
        upstream = dot_last(grad_proj, wq_ref[...])
        normal, scale = standardize(xg_ref[rows, :width].astype(F32))
        vectors[0] += jnp.sum(normal * upstream, axis=0, keepdims=True)
        vectors[1] += jnp.sum(upstream, axis=0, keepdims=True)
        vectors[2] += jnp.sum(xg_ref[rows, width:].astype(F32), axis=0, keepdims=True)
        dx_ref[rows, :] = norm_back(normal, scale, gain * upstream)

    grad_qkv = dot_rows(na_ref[...], dp_ref[...])
    grad_out = dot_rows(att_ref[...], xg_ref[:, width:])
    rest = grad_ref.shape[1] - own_rows - out_rows
    tail = jnp.concatenate(
        [jnp.concatenate([grad_bias, jnp.zeros((1, width - 3 * part), F32)], 1)]
        + vectors
        + [jnp.zeros((rest - 4, width), F32)],
        0,
    )
    for owner in range(owners):
        grad_ref[owner, :own_rows, : 3 * part] = grad_qkv[owner * own_rows : (owner + 1) * own_rows, :]
        grad_ref[owner, :own_rows, 3 * part :] = jnp.zeros((own_rows, width - 3 * part), F32)
        grad_ref[owner, own_rows : own_rows + out_rows, :] = grad_out[
            owner * out_rows : (owner + 1) * out_rows, :
        ]
        grad_ref[owner, own_rows + out_rows :, :] = tail


def mlp_kernel(
    xg_ref, up_ref, down_ref, vec_ref, bias_ref, out_part_ref, dx_part_ref,
    out_ref, dx_ref, grad_ref,
    nb_ref, act_ref, dh_ref,
):
    tokens = xg_ref.shape[0]
    width = xg_ref.shape[1] // 2
    hidden_width = up_ref.shape[1]
    owners = grad_ref.shape[0]
    up_rows = width // owners
    down_rows = hidden_width // owners
    gain = vec_ref[2:3, :]
    shift = vec_ref[3:4, :]
    vectors = [jnp.zeros((1, width), F32) for _ in range(2)]
    grad_bias = jnp.zeros((1, hidden_width), F32)
    for block in range(tokens // BLOCK):
        rows = pl.ds(block * BLOCK, BLOCK)
        grad_rows = xg_ref[rows, width:]
        normal, scale = standardize(xg_ref[rows, :width].astype(F32))
        normed = (normal * gain + shift).astype(BF16)
        nb_ref[rows, :] = normed
        hidden = dot(normed, up_ref[...]) + bias_ref[...]
        half = 0.5 * (1.0 + lax.erf(hidden * math.sqrt(0.5)))
        active = (hidden * half).astype(BF16)
        act_ref[rows, :] = active
        slope = half + hidden * jnp.exp(-0.5 * hidden * hidden) * (1.0 / math.sqrt(2.0 * math.pi))
        grad_hidden = (dot_last(grad_rows, down_ref[...]) * slope).astype(BF16)
        dh_ref[rows, :] = grad_hidden
        grad_bias += jnp.sum(grad_hidden.astype(F32), axis=0, keepdims=True)
        out_ref[rows, :] = (out_part_ref[rows, :] + dot(active, down_ref[...])).astype(out_ref.dtype)
        upstream = dot_last(grad_hidden, up_ref[...])
        vectors[0] += jnp.sum(normal * upstream, axis=0, keepdims=True)
        vectors[1] += jnp.sum(upstream, axis=0, keepdims=True)
        dx_ref[rows, :] = (dx_part_ref[rows, :] + norm_back(normal, scale, gain * upstream)).astype(dx_ref.dtype)
    grad_up = dot_rows(nb_ref[...], dh_ref[...])
    grad_down = dot_rows(act_ref[...], xg_ref[:, width:])
    rest = grad_ref.shape[1] - up_rows - down_rows
    tail = jnp.concatenate([grad_bias] + vectors + [jnp.zeros((rest - 3, width), F32)], 0)
    for owner in range(owners):
        grad_ref[owner, :up_rows, :] = grad_up[owner * up_rows : (owner + 1) * up_rows, :]
        grad_ref[owner, up_rows : up_rows + down_rows, :] = grad_down[
            owner * down_rows : (owner + 1) * down_rows, :
        ]
        grad_ref[owner, up_rows + down_rows :, :] = tail


def whole(count):
    return [pl.BlockSpec(memory_space=pltpu.VMEM)] * count


def attention(xg, w_qkv, w_out, vectors, bias, cosine, sine, owners):
    tokens, width = xg.shape[0], xg.shape[1] // 2
    part = w_out.shape[0]
    rows = width // owners + part // owners + 16
    shape = jax.ShapeDtypeStruct
    flops = 2 * tokens * width * part * 12 + 2 * 5 * tokens * tokens * part
    return pl.pallas_call(
        attention_kernel,
        out_shape=(
            shape((tokens, width), F32),
            shape((tokens, width), F32),
            shape((owners, rows, width), F32),
        ),
        in_specs=whole(7),
        out_specs=tuple(whole(3)),
        scratch_shapes=[
            pltpu.VMEM((tokens, width), BF16),
            pltpu.VMEM((tokens, part), BF16),
            pltpu.VMEM((tokens, part), BF16),
            pltpu.VMEM((tokens, part), BF16),
            pltpu.VMEM((tokens, part), BF16),
            pltpu.VMEM((part, tokens), BF16),
            pltpu.VMEM((part, tokens), BF16),
            pltpu.VMEM((tokens, part), BF16),
            pltpu.VMEM((tokens, part), F32),
            pltpu.VMEM((part, tokens), F32),
            pltpu.VMEM((part, tokens), F32),
            pltpu.VMEM((tokens, 3 * part), BF16),
        ],
        compiler_params=PARAMS,
        cost_estimate=pl.CostEstimate(
            flops=4 * flops, bytes_accessed=8 * tokens * width * 4, transcendentals=tokens * tokens * 2
        ),
    )(xg, w_qkv, w_out, vectors, bias, cosine, sine)


def feed_forward(xg, w_up, w_down, vectors, bias, out_part, dx_part, owners):
    tokens, width = xg.shape[0], xg.shape[1] // 2
    hidden_width = w_up.shape[1]
    rows = width // owners + hidden_width // owners + 16
    shape = jax.ShapeDtypeStruct
    return pl.pallas_call(
        mlp_kernel,
        out_shape=(
            shape((tokens, width), F32),
            shape((tokens, width), F32),
            shape((owners, rows, width), F32),
        ),
        in_specs=whole(7),
        out_specs=tuple(whole(3)),
        scratch_shapes=[
            pltpu.VMEM((tokens, width), BF16),
            pltpu.VMEM((tokens, hidden_width), BF16),
            pltpu.VMEM((tokens, hidden_width), BF16),
        ],
        compiler_params=PARAMS,
        cost_estimate=pl.CostEstimate(
            flops=12 * tokens * width * hidden_width,
            bytes_accessed=8 * tokens * width * 4,
            transcendentals=2 * tokens * hidden_width,
        ),
    )(xg, w_up, w_down, vectors, bias, out_part, dx_part)


def rotary(tokens, heads):
    ladder = np.arange(ROT // 2, dtype=np.float32)
    frequency = np.exp(ladder * np.float32(-2.0 * math.log(10000.0) / ROT)).astype(np.float32)
    angles = np.arange(tokens, dtype=np.float32)[:, None] * frequency[None, :]
    cosine = np.ones((tokens, HD), np.float32)
    sine = np.zeros((tokens, HD), np.float32)
    half = ROT // 2
    cosine[:, :half] = cosine[:, half:ROT] = np.cos(angles)
    sine[:, half:ROT] = np.sin(angles)
    sine[:, :half] = -sine[:, half:ROT]
    return np.tile(cosine, (1, heads)), np.tile(sine, (1, heads))


def shards_any(
    owners, groups,
    inputs, cotangent, w_qkv, b_qkv, w_out, b_out, w_up, b_up, w_down, b_down,
    gain_one, shift_one, gain_two, shift_two,
):
    rows, width = w_qkv.shape[0], w_qkv.shape[1] // 3
    hidden = w_up.shape[1]
    down_rows = w_down.shape[0]
    local = inputs.shape[1]
    tokens = local * groups
    part = width // groups
    slice_width = hidden // groups
    dp_rows = rows * groups
    group = lax.axis_index("seq")
    owner = lax.axis_index("dp")

    xg = jnp.concatenate([inputs[0], cotangent[0]], axis=1)
    xg = gather_bits(xg, "seq", groups).reshape(tokens, 2 * width)

    devices = owners * groups
    place = [(f % owners) * groups + f // owners for f in range(devices)]
    out_rows = lax.ppermute(w_out, ("dp", "seq"), [(f, place[f]) for f in range(devices)])

    small = jnp.concatenate(
        [b_qkv.reshape(rows, -1), b_up.reshape(rows, -1)]
        + [v[:, None] for v in (b_out, b_down, gain_one, shift_one, gain_two, shift_two)],
        axis=1,
    )
    n_small = small.shape[1]
    n_up = b_up.shape[0] // rows
    small = jnp.pad(small, ((0, 0), (0, width - 3 * part - n_small)))
    blocks = jnp.concatenate(
        [
            w_qkv.reshape(rows, 3, groups, part).transpose(2, 0, 1, 3).reshape(groups, rows, 3 * part),
            jnp.broadcast_to(small[None], (groups,) + small.shape),
            w_up.reshape(rows, owners, groups, -1).transpose(2, 0, 1, 3).reshape(groups, rows, slice_width),
        ],
        axis=2,
    )
    blocks = swap_bits(blocks, "seq", groups).reshape(dp_rows, width + slice_width)
    first = gather_bits(jnp.concatenate([blocks[:, :width], out_rows], axis=0), "dp", owners)
    second = gather_bits(jnp.concatenate([blocks[:, width:], w_down], axis=0), "dp", owners)

    full_qkv = first[:, :dp_rows, : 3 * part].reshape(width, 3 * part)
    full_out = first[:, dp_rows:, :].reshape(part, width)
    small = first[:, :dp_rows, 3 * part : 3 * part + n_small].reshape(width, n_small).astype(F32)
    bias_qkv = lax.dynamic_index_in_dim(
        small[:, :3].reshape(3, groups, part), group, 1, keepdims=False
    ).reshape(1, 3 * part)
    bias_up = lax.dynamic_index_in_dim(
        small[:, 3 : 3 + n_up].reshape(owners, groups, -1), group, 1, keepdims=False
    ).reshape(1, slice_width)
    vectors = small[:, 3 + n_up :].T
    biases = vectors[0] + vectors[1]
    vectors = jnp.concatenate([vectors[2:], jnp.zeros((4, width), F32)], 0)
    full_up = second[:, :dp_rows, :].reshape(width, slice_width)
    full_down = second[:, dp_rows:, :].reshape(slice_width, width)

    cosine, sine = rotary(tokens, part // HD)
    out_part, dx_part, grad_a = attention(
        xg, full_qkv, full_out, vectors, bias_qkv, jnp.asarray(cosine), jnp.asarray(sine), owners
    )
    out_part, dx_part, grad_b = feed_forward(
        xg, full_up, full_down, vectors, bias_up, out_part, dx_part, owners
    )

    grad_a = scatter_bits(grad_a, "dp", owners)
    grad_b = scatter_bits(grad_b, "dp", owners)
    both = jnp.concatenate([out_part, dx_part], axis=1).reshape(groups, local, 2 * width)
    both = scatter_bits(both, "seq", groups)
    outputs = (inputs[0].astype(F32) + both[:, :width] + biases[None]).astype(BF16)[None]
    grad_inputs = (cotangent[0].astype(F32) + both[:, width:]).astype(BF16)[None]

    own_wout = lax.ppermute(
        grad_a[dp_rows : dp_rows + rows, :], ("dp", "seq"), [(place[f], f) for f in range(devices)]
    )
    tail_a = grad_a[dp_rows + rows :, :]
    tail_b = grad_b[dp_rows + down_rows :, :]
    small = jnp.concatenate([tail_a[:4], tail_b[1:3], jnp.zeros((2, width), F32)], 0)
    send = jnp.concatenate(
        [
            grad_a[:dp_rows, : 3 * part].reshape(groups, rows, 3 * part),
            grad_b[:dp_rows, :].reshape(groups, rows, slice_width),
        ],
        axis=2,
    )
    small = jnp.pad(small, ((0, 0), (0, send.shape[2] - width)))
    send = jnp.concatenate([send, jnp.broadcast_to(small[None], (groups,) + small.shape)], axis=1)
    send = swap_bits(send, "seq", groups)
    own_wqkv = send[:, :rows, : 3 * part].reshape(groups, rows, 3, part).transpose(1, 2, 0, 3).reshape(rows, -1)
    own_wup = (
        send[:, :rows, 3 * part :].reshape(groups, rows, owners, -1).transpose(1, 2, 0, 3).reshape(rows, -1)
    )
    small = send[:, rows:, :width]
    index = owner * groups + group
    own_bqkv = lax.dynamic_slice_in_dim(
        small[:, 0, : 3 * part].reshape(groups, 3, part).transpose(1, 0, 2).reshape(-1),
        index * b_qkv.shape[0],
        b_qkv.shape[0],
    )
    sums = jnp.sum(small, axis=0)
    own = lax.dynamic_slice_in_dim(sums, index * rows, rows, axis=1)
    own_bias = lax.dynamic_slice_in_dim(small[0, 3], index * rows, rows)
    own_bup = lax.dynamic_slice_in_dim(tail_b[0], owner * b_up.shape[0], b_up.shape[0])
    return (
        outputs,
        grad_inputs,
        own_wqkv,
        own_bqkv,
        own_wout,
        own_bias,
        own_wup,
        own_bup,
        grad_b[dp_rows : dp_rows + down_rows, :],
        own_bias,
        own[1],
        own[2],
        own[4],
        own[5],
    )


def reversed_bits(value, count):
    result = 0
    for bit in range(count):
        result = result | (((value >> bit) & 1) << (count - 1 - bit))
    return result


def after(value, *others):
    return lax.optimization_barrier((value,) + others)[0]


def spread(value, axis, size, gates=()):
    value, seen = value[None], []
    for step, bit in enumerate(reversed(range(log2(size)))):
        seen.append(exchange(value, axis, size, bit))
        if bit:
            other = after(seen[-1], *gates[step]) if step < len(gates) else seen[-1]
            value = jnp.concatenate([value, other], 0)
    return (value, seen[-1]), seen


def fold(kept, other):
    total = kept + other.astype(F32)
    half = total.shape[0] // 2
    return total[half:].astype(BF16), total[:half]


def finish(kept, other):
    return kept[0] + other[0].astype(F32)


def call(kernel, outs, scratch, flops, transcendentals, *operands, mib=8, far=0):
    return pl.pallas_call(
        kernel,
        out_shape=tuple(outs),
        in_specs=whole(len(operands) - far)
        + [pl.BlockSpec(memory_space=pltpu.HBM)] * far,
        out_specs=tuple(whole(len(outs))),
        scratch_shapes=scratch,
        compiler_params=pltpu.CompilerParams(vmem_limit_bytes=mib * 1024 * 1024),
        cost_estimate=pl.CostEstimate(flops=1, bytes_accessed=1, transcendentals=0),
    )(*operands)


def fetch(pairs, sems):
    copies = [pltpu.make_async_copy(source, to, sems.at[i]) for i, (source, to) in enumerate(pairs)]
    for copy in copies:
        copy.start()
    for copy in copies:
        copy.wait()


def pack_kernel(*refs):
    x_ref, g_ref, refs = refs[0], refs[1], refs[2:]
    count = (len(refs) - 5) // 2
    (sent_ref, kept_ref, both_ref, block_ref, sems), held = refs[count : count + 5], refs[count + 5 :]
    joined = [
        pltpu.make_async_copy(ref, both_ref.at[:, :, pl.ds(i * ref.shape[2], ref.shape[2])], sems.at[count + i])
        for i, ref in enumerate((x_ref, g_ref))
    ]
    for copy in joined:
        copy.start()
    fetch(tuple(zip(refs[:count], held)), sems)
    qkv_ref, up_ref, out_ref, small = held[0], held[1], held[2], held[3:]
    me = lax.axis_index("seq")
    groups, rows, _ = block_ref.shape
    width = qkv_ref.shape[1] // 3
    part = width // groups
    piece = rows * groups
    owners = up_ref.shape[1] // (groups * piece)
    lines = []
    for line in (small[:2], small[2:]):
        values = [ref[...].reshape(1, ref.shape[0]).astype(F32) for ref in line]
        used = sum(ref.shape[0] for ref in line)
        lines.append(jnp.concatenate(values + [jnp.zeros((1, part - used), F32)], 1))
    lines = jnp.concatenate(lines + [jnp.zeros((rows - 2, part), F32)], 0).astype(BF16)
    for group in range(groups):
        for c in range(3):
            start = c * width + group * part
            block_ref[group, :, c * part : (c + 1) * part] = qkv_ref[:, start : start + part]
        block_ref[group, :, 3 * part : width] = lines
        block_ref[group, :, width + up_ref.shape[1] // groups :] = out_ref[...]
        block_ref[group, :, width : width + up_ref.shape[1] // groups] = jnp.concatenate(
            [
                up_ref[:, (k * groups + group) * piece : (k * groups + group + 1) * piece]
                for k in range(owners)
            ],
            1,
        )
    for half in range(groups // 2):
        kept_ref[half] = block_ref[me ^ (2 * half)]
        sent_ref[half] = block_ref[me ^ (2 * half + 1)]
    for copy in joined:
        copy.wait()


def payload_kernel(kept_ref, near_ref, far_ref, down_ref, first_ref, second_ref, sem):
    me = lax.axis_index("seq")
    width = down_ref.shape[1]
    part, rows = width // 4, first_ref.shape[0] // 8
    copy = pltpu.make_async_copy(down_ref, second_ref.at[pl.ds(4 * rows, down_ref.shape[0])], sem)
    copy.start()
    hidden = kept_ref.shape[2] - 2 * width
    index = lax.broadcasted_iota(jnp.int32, (rows, part), 0)
    mine = index // 2 == lax.axis_index("dp")
    for step, block in enumerate((kept_ref.at[0], near_ref.at[0], far_ref.at[0], far_ref.at[1])):
        group = me ^ step
        lanes = pl.ds(pl.multiple_of(group * part, part), part)
        second_ref[pl.ds(pl.multiple_of(group * rows, rows), rows), :] = block[:, width : width + hidden]
        for c in range(3):
            first_ref[c * rows : (c + 1) * rows, lanes] = block[:, c * part : (c + 1) * part]
        line = block[:, 3 * part : width].astype(F32)
        line = jnp.where(index % 2 == 0, line[0:1], line[1:2])
        first_ref[3 * rows : 4 * rows, lanes] = jnp.where(mine, line, 0.0).astype(BF16)
        first_ref[pl.ds(pl.multiple_of((4 + group) * rows, rows), rows), :] = block[:, width + hidden :]
    copy.wait()


def merge_kernel(bit, rows, mine_ref, other_ref, out_ref):
    part = mine_ref.shape[0] - 5 * rows
    small, last = slice(part, part + rows), slice(part + rows, part + 5 * rows)
    out_ref[:part, :] = mine_ref[:part, :]
    out_ref[part : 2 * part, :] = other_ref[:part, :]
    out_ref[2 * part : 2 * part + rows, :] = mine_ref[small, :] + other_ref[small, :]
    same = (lax.axis_index("dp") >> bit) & 1 == (lax.axis_index("seq") >> (bit - 1)) & 1

    @pl.when(same)
    def _():
        out_ref[2 * part + rows :, :] = mine_ref[last, :]

    @pl.when(jnp.logical_not(same))
    def _():
        out_ref[2 * part + rows :, :] = other_ref[last, :]


def sources(pair, me):
    half = pair[0].shape[0]
    count = log2(2 * half)
    for slot in range(2 * half):
        ref = pair[slot // half]
        yield ref.at[slot % half], me ^ reversed_bits(slot, count)


def project_kernel(
    first_ref, other_ref, x_ref, y_ref, cos_ref, sin_ref, table_ref,
    xg_ref, na_ref, q_ref, qt_ref, k_ref, v_ref, da_ref, dat_ref, wq_ref, wo_ref, vec_ref,
):
    owner, group = lax.axis_index("dp"), lax.axis_index("seq")
    width = first_ref.shape[1]
    groups = 2 * x_ref.shape[0]
    part = width // groups
    rows = first_ref.shape[0] // 17
    owners = width // (rows * groups)
    local = x_ref.shape[1]
    for slot in range(owners):
        block = (first_ref, other_ref)[slot // 4].at[pl.ds(slot % 4 * 3 * rows, 3 * rows)]
        rank = owner ^ reversed_bits(slot, log2(owners))
        for g in range(groups):
            lanes = slice(g * part, (g + 1) * part)
            to = pl.ds(pl.multiple_of((rank * groups + g) * rows, rows), rows)
            for c in range(3):
                wq_ref[to, c * part : (c + 1) * part] = block[c * rows : (c + 1) * rows, lanes]
    for slot, ref in enumerate((first_ref, other_ref)):
        x = (owner & 1) ^ slot
        wo_ref[pl.ds(pl.multiple_of(x * 4 * rows, 4 * rows), 4 * rows), :] = ref[13 * rows :, :]
    devices = owners * groups
    small = first_ref[12 * rows : 13 * rows, :].astype(F32) + other_ref[12 * rows : 13 * rows, :].astype(F32)
    line_one, line_two = (
        jnp.concatenate(
            [
                small[2 * rank + i : 2 * rank + i + 1, g * part : (g + 1) * part]
                for rank in range(owners)
                for g in range(groups)
            ],
            0,
        ).astype(BF16)
        for i in range(2)
    )

    def place_values(line, lane_of, device_of_column):
        columns = lane_of.shape[1]
        pick = lax.broadcasted_iota(jnp.int32, (line.shape[1], columns), 0) == lane_of
        values = dot(line, jnp.where(pick, 1.0, 0.0).astype(BF16))
        held = lax.broadcasted_iota(jnp.int32, (devices, columns), 0) == device_of_column
        return jnp.sum(jnp.where(held, values, 0.0), axis=0, keepdims=True)

    column = lax.broadcasted_iota(jnp.int32, (1, width), 1)
    own = [place_values(line_two, column % rows + v * rows, column // rows) for v in range(6)]
    piece = rows * groups
    start = 3 * width // devices
    bias_up = place_values(line_one, column % piece + start, column // piece * groups + group)
    lane_of = jnp.concatenate(
        [table_ref[0:1, pl.ds(pl.multiple_of(c * width + group * part, part), part)] for c in range(3)], 1
    )
    owner_of = jnp.concatenate(
        [table_ref[1:2, pl.ds(pl.multiple_of(c * width + group * part, part), part)] for c in range(3)], 1
    )
    bias = place_values(line_one, lane_of, owner_of)
    gain, shift = own[2], own[3]
    vec_ref[...] = jnp.concatenate(
        own[2:] + [own[0] + own[1], bias_up, jnp.zeros((2, width), F32)], 0
    )

    lane = lax.broadcasted_iota(jnp.int32, (local, part), 1)
    turn = lane % HD < ROT // 2

    def partner(value):
        return jnp.where(
            turn, pltpu.roll(value, part - ROT // 2, 1), pltpu.roll(value, ROT // 2, 1)
        )

    for block, rank in sources((x_ref, y_ref), group):
        start = pl.multiple_of(rank * local, local)
        to = pl.ds(start, local)
        both = block[...]
        xg_ref[to, :] = both
        normal, _ = standardize(both[:, :width].astype(F32))
        normed = (normal * gain + shift).astype(BF16)
        na_ref[to, :] = normed
        projected = dot(normed, wq_ref[...]) + bias
        cosine, sine = cos_ref[to, :], sin_ref[to, :]
        query = projected[:, :part]
        query = query * cosine + partner(query) * sine
        key = projected[:, part : 2 * part]
        key = key * cosine + partner(key) * sine
        query = query.astype(BF16).astype(F32) * HD**-0.5
        q_ref[to, :] = query.astype(BF16)
        qt_ref[:, to] = query.T.astype(BF16)
        k_ref[to, :] = key.astype(BF16)
        v_ref[to, :] = projected[:, 2 * part :].astype(BF16)
        grad_att = dot_last(both[:, width:], wo_ref[...]).astype(BF16)
        da_ref[to, :] = grad_att
        dat_ref[:, to] = grad_att.astype(F32).T.astype(BF16)


def attend_kernel(
    xg_ref, na_ref, q_ref, qt_ref, k_ref, v_ref, da_ref, dat_ref, wq_ref, cos_ref, sin_ref,
    att_ref, dp_ref, small_ref, sent_ref, kept_ref,
    dq_ref, dkt_ref, dvt_ref, gq_ref, go_ref,
):
    owner = lax.axis_index("dp")
    tokens, part = q_ref.shape
    width = na_ref.shape[1]
    groups = width // part
    owners = 2 * sent_ref.shape[0]
    rows = part // owners
    lane = lax.broadcasted_iota(jnp.int32, (BLOCK, part), 1)
    turn = lane % HD < ROT // 2

    def partner(value):
        return jnp.where(
            turn, pltpu.roll(value, part - ROT // 2, 1), pltpu.roll(value, ROT // 2, 1)
        )

    dkt_ref[...] = jnp.zeros_like(dkt_ref)
    dvt_ref[...] = jnp.zeros_like(dvt_ref)
    below = lax.broadcasted_iota(jnp.int32, (BLOCK, BLOCK), 0) >= lax.broadcasted_iota(
        jnp.int32, (BLOCK, BLOCK), 1
    )
    zero = jnp.zeros((), BF16)
    for block in range(tokens // BLOCK):
        at = pl.ds(block * BLOCK, BLOCK)
        seen = (block + 1) * BLOCK
        attended = jnp.zeros((BLOCK, part), F32)
        grad_query = jnp.zeros((BLOCK, part), F32)
        for head in range(part // HD):
            mine = lane // HD == head
            mine_t = lax.broadcasted_iota(jnp.int32, (part, BLOCK), 0) // HD == head
            query = jnp.where(mine, q_ref[at, :], zero)
            grad_att = jnp.where(mine, da_ref[at, :], zero)
            scores = dot_last(query, k_ref[:seen, :])
            last = jnp.where(below, scores[:, seen - BLOCK :], -1e30)
            scores = last if block == 0 else jnp.concatenate([scores[:, : seen - BLOCK], last], 1)
            raised = jnp.exp(scores - jnp.max(scores, axis=-1, keepdims=True))
            probs = raised * (1.0 / jnp.sum(raised, axis=-1, keepdims=True))
            probs_low = probs.astype(BF16)
            attended = jnp.where(mine, dot(probs_low, v_ref[:seen, :]), attended)
            grad_probs = dot_last(grad_att, v_ref[:seen, :])
            inner = jnp.sum(probs * grad_probs, axis=-1, keepdims=True)
            grad_scores = (probs * (grad_probs - inner)).astype(BF16)
            grad_query = jnp.where(mine, dot(grad_scores, k_ref[:seen, :]), grad_query)
            query_t = jnp.where(mine_t, qt_ref[:, at], zero)
            grad_att_t = jnp.where(mine_t, dat_ref[:, at], zero)
            dkt_ref[:, :seen] += dot(query_t, grad_scores)
            dvt_ref[:, :seen] += dot(grad_att_t, probs_low)
        att_ref[at, :] = attended.astype(BF16)
        dq_ref[at, :] = grad_query * HD**-0.5

    vectors = [jnp.zeros((1, width), F32) for _ in range(3)]
    grad_bias = jnp.zeros((1, 3 * part), F32)
    for block in range(tokens // BLOCK):
        at = pl.ds(block * BLOCK, BLOCK)
        cosine, sine = cos_ref[at, :], sin_ref[at, :]
        grad_query = dq_ref[at, :]
        grad_query = grad_query * cosine - partner(grad_query) * sine
        grad_key = dkt_ref[:, at].T
        grad_key = grad_key * cosine - partner(grad_key) * sine
        grad_proj = jnp.concatenate([grad_query, grad_key, dvt_ref[:, at].T], 1).astype(BF16)
        dp_ref[at, :] = grad_proj
        grad_bias += jnp.sum(grad_proj.astype(F32), axis=0, keepdims=True)
        upstream = dot_last(grad_proj, wq_ref[...])
        normal, _ = standardize(xg_ref[at, :width].astype(F32))
        vectors[0] += jnp.sum(normal * upstream, axis=0, keepdims=True)
        vectors[1] += jnp.sum(upstream, axis=0, keepdims=True)
        vectors[2] += jnp.sum(xg_ref[at, width:].astype(F32), axis=0, keepdims=True)

    gq_ref[...] = dot_rows(na_ref[...], dp_ref[...])
    go_ref[...] = dot_rows(att_ref[...], xg_ref[:, width:])
    small_ref[...] = jnp.concatenate(
        [jnp.concatenate([grad_bias, jnp.zeros((1, width - 3 * part), F32)], 1)]
        + vectors
        + [jnp.zeros((4, width), F32)],
        0,
    )
    for ref, rank in sources((kept_ref, sent_ref), owner):
        kind = ref.dtype
        for g in range(groups):
            at = pl.ds(pl.multiple_of((rank * groups + g) * rows, rows), rows)
            for c in range(3):
                ref[c * rows : (c + 1) * rows, g * part : (g + 1) * part] = gq_ref[
                    at, c * part : (c + 1) * part
                ].astype(kind)
        ref[3 * rows : 4 * rows, :] = go_ref[pl.ds(pl.multiple_of((rank % 2 * 4 + rank // 2) * rows, rows), rows), :].astype(kind)


def hidden_kernel(
    second_ref, other_ref, xg_ref, vec_ref, small_ref,
    act_ref, dh_ref, up_ref, down_ref, sent_ref, kept_ref,
    nb_ref, gu_ref,
):
    owner = lax.axis_index("dp")
    tokens, hidden_width = act_ref.shape
    width = vec_ref.shape[1]
    rows = second_ref.shape[1] // 2
    for block, rank in sources((second_ref, other_ref), owner):
        at = pl.ds(pl.multiple_of(rank * rows, rows), rows)
        up_ref[at, :] = block[:rows, :]
        down_ref[at, :] = block[rows:, :]
    gain, shift, bias = vec_ref[2:3, :], vec_ref[3:4, :], vec_ref[5:6, :]
    vectors = [jnp.zeros((1, width), F32) for _ in range(2)]
    grad_bias = jnp.zeros((1, hidden_width), F32)
    for block in range(tokens // BLOCK):
        at = pl.ds(block * BLOCK, BLOCK)
        normal, _ = standardize(xg_ref[at, :width].astype(F32))
        normed = (normal * gain + shift).astype(BF16)
        nb_ref[at, :] = normed
        hidden = dot(normed, up_ref[...]) + bias
        half = 0.5 * (1.0 + lax.erf(hidden * math.sqrt(0.5)))
        act_ref[at, :] = (hidden * half).astype(BF16)
        slope = half + hidden * jnp.exp(-0.5 * hidden * hidden) * (1.0 / math.sqrt(2.0 * math.pi))
        grad_hidden = (dot_last(xg_ref[at, width:], down_ref[...]) * slope).astype(BF16)
        dh_ref[at, :] = grad_hidden
        grad_bias += jnp.sum(grad_hidden.astype(F32), axis=0, keepdims=True)
        upstream = dot_last(grad_hidden, up_ref[...])
        vectors[0] += jnp.sum(normal * upstream, axis=0, keepdims=True)
        vectors[1] += jnp.sum(upstream, axis=0, keepdims=True)
    gu_ref[...] = dot_rows(nb_ref[...], dh_ref[...])
    extra = sent_ref.shape[1] - rows
    tail = jnp.concatenate([grad_bias] + vectors + [small_ref[:4, :], jnp.zeros((extra - 7, width), F32)], 0)
    for ref, rank in sources((kept_ref, sent_ref), owner):
        ref[:rows, :] = gu_ref[pl.ds(pl.multiple_of(rank * rows, rows), rows), :].astype(ref.dtype)
        ref[rows:, :] = tail.astype(ref.dtype)


def down_kernel(act_ref, xg_ref, sent_ref, kept_ref, gd_ref):
    width = sent_ref.shape[2]
    rows = sent_ref.shape[1]
    gd_ref[...] = dot_rows(act_ref[...], xg_ref[:, width:])
    for ref, rank in sources((kept_ref, sent_ref), lax.axis_index("dp")):
        ref[...] = gd_ref[pl.ds(pl.multiple_of(rank * rows, rows), rows), :].astype(ref.dtype)


def join_kernel(
    xg_ref, att_ref, wo_ref, act_ref, down_ref, vec_ref, dp_ref, wq_ref, dh_ref, up_ref,
    sent_ref, kept_ref,
):
    group = lax.axis_index("seq")
    local = sent_ref.shape[1]
    width = wo_ref.shape[1]
    gain_one, gain_two, bias = vec_ref[0:1, :], vec_ref[2:3, :], vec_ref[4:5, :]
    for step in range(2 * sent_ref.shape[0]):
        at = pl.ds(pl.multiple_of((group ^ step) * local, local), local)
        ref = (kept_ref, sent_ref)[step % 2].at[step // 2]
        out = dot(att_ref[at, :], wo_ref[...]) + dot(act_ref[at, :], down_ref[...])
        rows_in = xg_ref[at, :width].astype(F32)
        normal, scale = standardize(rows_in)
        inner = gain_one * dot_last(dp_ref[at, :], wq_ref[...]) + gain_two * dot_last(dh_ref[at, :], up_ref[...])
        grad = norm_back(normal, scale, inner)
        if step == 0:
            out = out + rows_in + bias
            grad = grad + xg_ref[at, width:].astype(F32)
        ref[:, :width] = out.astype(ref.dtype)
        ref[:, width:] = grad.astype(ref.dtype)


def deal_kernel(a_ref, b_ref, sent_ref, kept_ref):
    me = lax.axis_index("seq")
    width = a_ref.shape[1]
    part = width // 4
    rows = a_ref.shape[0] // 4
    kind = sent_ref.dtype
    small = jnp.concatenate(
        [b_ref[4 * rows + 3 : 4 * rows + 6, :], b_ref[4 * rows + 1 : 4 * rows + 3, :], jnp.zeros((rows - 5, width), F32)], 0
    )
    for step in range(4):
        group = me ^ step
        ref = (kept_ref, sent_ref)[step // 2].at[step % 2]
        lanes = pl.ds(pl.multiple_of(group * part, part), part)
        for c in range(3):
            ref[:rows, c * part : (c + 1) * part] = a_ref[c * rows : (c + 1) * rows, lanes].astype(kind)
        ref[:rows, 3 * part :] = b_ref[pl.ds(pl.multiple_of(group * rows, rows), rows), :].astype(kind)
        ref[rows:, :width] = small.astype(kind)
        ref[rows:, width:] = jnp.zeros((rows, 3 * part), kind)


def collect_kernel(
    kept_ref, near_ref, far_ref, b_ref, out_ref, down_kept_ref, down_other_ref,
    qkv_ref, up_ref, wout_ref, bqkv_ref, bias_ref, twin_ref, bup_ref, gain_one_ref, shift_one_ref, gain_two_ref, shift_two_ref, down_ref,
    block_ref,
):
    me = lax.axis_index("seq")
    place = lax.axis_index("dp") * 4 + me
    rows = qkv_ref.shape[0]
    width = qkv_ref.shape[1] // 3
    part = width // 4
    piece = 4 * rows
    for step, block in enumerate((kept_ref.at[0], far_ref.at[0], near_ref.at[0], far_ref.at[1])):
        block_ref[me ^ step] = block[...].astype(F32)
    for g in range(4):
        for c in range(3):
            qkv_ref[:, c * width + g * part : c * width + (g + 1) * part] = block_ref[
                g, :rows, c * part : (c + 1) * part
            ]
    for k in range(up_ref.shape[1] // (4 * piece)):
        start = 3 * part + k * piece
        up_ref[:, 4 * k * piece : 4 * (k + 1) * piece] = jnp.concatenate(
            [block_ref[g, :rows, start : start + piece] for g in range(4)], 1
        )
    wout_ref[...] = out_ref[...]
    down_ref[...] = down_kept_ref[0] + down_other_ref[0].astype(F32)

    def own(values, ref, index):
        size, count = values.shape[1], ref.shape[0]
        values = pltpu.roll(values, (size - index * count) % size, 1)[0:1, :count]
        ref[...] = values.reshape(count)

    sums = sum(block_ref[g, rows : rows + 8, :width] for g in range(4))
    for i, ref in enumerate((gain_one_ref, shift_one_ref, gain_two_ref, shift_two_ref)):
        own(sums[i + 1 : i + 2], ref, place)
    bias = jnp.concatenate(
        [block_ref[g, rows : rows + 1, c * part : (c + 1) * part] for c in range(3) for g in range(4)], 1
    )
    own(bias, bqkv_ref, place)
    own(b_ref[4 * rows + 6 : 4 * rows + 7, :], bias_ref, place)
    twin_ref[...] = bias_ref[...]
    own(b_ref[4 * rows : 4 * rows + 1, :], bup_ref, lax.axis_index("dp"))


def shards(
    owners, groups,
    inputs, cotangent, w_qkv, b_qkv, w_out, b_out, w_up, b_up, w_down, b_down,
    gain_one, shift_one, gain_two, shift_two,
):
    rows, width = w_qkv.shape[0], w_qkv.shape[1] // 3
    hidden = w_up.shape[1] // groups
    local = inputs.shape[1]
    if rows % 16 or groups != 4 or owners != 8 or local != BLOCK or hidden != width:
        return shards_any(
            owners, groups, inputs, cotangent, w_qkv, b_qkv, w_out, b_out, w_up, b_up, w_down, b_down,
            gain_one, shift_one, gain_two, shift_two,
        )
    tokens = local * groups
    part = width // groups
    devices = owners * groups
    half = owners // 2
    heads = part // HD
    shape = jax.ShapeDtypeStruct

    target = [(f % 4 * 2 + f // 4 % 2) * groups + f // owners for f in range(devices)]

    block = shape((2, rows, 2 * width + hidden), BF16)
    params = (w_qkv, w_up, w_out, b_qkv, b_up, b_out, b_down, gain_one, shift_one, gain_two, shift_two)
    sent, kept, x = call(
        pack_kernel,
        (block, block, shape((1, local, 2 * width), BF16)),
        [pltpu.VMEM((groups, rows, 2 * width + hidden), BF16), pltpu.SemaphoreType.DMA((len(params) + 2,))]
        + [pltpu.VMEM(p.shape, BF16) for p in params],
        0, 0, inputs, cotangent, *params, mib=63, far=len(params) + 2,
    )
    near = exchange(sent, "seq", groups, 0)
    far = exchange(jnp.stack([kept[1], near[1]]), "seq", groups, 1)
    first, second = call(
        payload_kernel,
        (shape((8 * rows, width), BF16), shape((4 * rows + w_down.shape[0], width), BF16)),
        [pltpu.SemaphoreType.DMA], 0, 0, kept, near, far, w_down, mib=4, far=1,
    )
    def merged(bit, mine, other):
        out = shape((2 * mine.shape[0] - 5 * rows, width), BF16)
        return call(functools.partial(merge_kernel, bit, rows), (out,), [], 0, 0, mine, other, mib=4)[0]

    x = after(x, far)
    x_other = exchange(x, "seq", groups, 1)
    other = exchange(first, "dp", owners, 2)
    second = after(second, other)[None]
    first = merged(2, first, other)
    other, second_other = exchange(first, "dp", owners, 1), exchange(second, "dp", owners, 2)
    other, second_other, x_other = lax.optimization_barrier((other, second_other, x_other))
    first, second = merged(1, first, other), jnp.concatenate([second, second_other], 0)
    x = jnp.concatenate([x, x_other], 0)
    first = (first, exchange(first, "dp", owners, 0))
    x_pair = (x, exchange(x, "seq", groups, 0))
    second_other = exchange(second, "dp", owners, 1)

    cosine, sine = (jnp.asarray(t) for t in rotary(tokens, heads))
    column = np.arange(3 * width, dtype=np.int32)
    own = 3 * width // devices
    table = np.zeros((8, 3 * width), np.int32)
    table[0], table[1] = column % own, column // own
    wide, narrow, turned = shape((tokens, width), BF16), shape((tokens, part), BF16), shape((part, tokens), BF16)
    xg, normed_a, query, query_t, key, value, grad_att, grad_att_t, full_qkv, full_out, vectors = call(
        project_kernel,
        (shape((tokens, 2 * width), BF16), wide, narrow, turned, narrow, narrow, narrow, turned)
        + (shape((width, 3 * part), BF16), shape((part, width), BF16), shape((8, width), F32)),
        [], 2 * tokens * width * 4 * part, 0,
        *first, *x_pair, cosine, sine, jnp.asarray(table),
    )
    second = jnp.concatenate([second, after(second_other, first[1])], 0)
    second = (second, exchange(second, "dp", owners, 0))
    chunk = 5 * rows
    attended, grad_proj, small, sent_a, kept_a = call(
        attend_kernel,
        (narrow, shape((tokens, 3 * part), BF16), shape((8, width), F32))
        + (shape((half, 4 * rows, width), BF16), shape((half, 4 * rows, width), F32)),
        [
            pltpu.VMEM((tokens, part), F32),
            pltpu.VMEM((part, tokens), F32),
            pltpu.VMEM((part, tokens), F32),
            pltpu.VMEM((width, 3 * part), F32),
            pltpu.VMEM((part, width), F32),
        ],
        8 * tokens * tokens * part * 6, 2 * tokens * tokens,
        xg, normed_a, after(query, second_other), query_t, key, value, grad_att, grad_att_t, full_qkv, cosine, sine,
        mib=16,
    )
    other_a = exchange(sent_a, "dp", owners, 0)
    active, grad_hidden, full_up, full_down, sent_u, kept_u = call(
        hidden_kernel,
        (wide, wide, shape((width, hidden), BF16), shape((hidden, width), BF16))
        + (shape((half, chunk, width), BF16), shape((half, chunk, width), F32)),
        [
            pltpu.VMEM((tokens, width), BF16),
            pltpu.VMEM((width, hidden), F32),
        ],
        8 * tokens * width * hidden, 2 * tokens * hidden,
        *second, xg, vectors, small,
        mib=16,
    )
    other_u = exchange(sent_u, "dp", owners, 0)
    sent_a, kept_a = fold(kept_a, other_a)
    other_a = exchange(sent_a, "dp", owners, 1)
    down_rows = w_down.shape[0]
    sent_d, kept_d = call(
        down_kernel,
        (shape((half, down_rows, width), BF16), shape((half, down_rows, width), F32)),
        [pltpu.VMEM((hidden, width), F32)],
        2 * tokens * width * hidden, 0,
        active, xg,
    )
    sent_x, kept_x = call(
        join_kernel,
        (shape((2, local, 2 * width), BF16), shape((2, local, 2 * width), F32)),
        [],
        4 * tokens * width * hidden, 0,
        xg, attended, full_out, active, full_down, vectors,
        grad_proj, full_qkv, grad_hidden, full_up,
    )
    other_x = exchange(after(sent_x, other_u, other_a), "seq", groups, 0)
    other_u, other_x, sent_d, = lax.optimization_barrier((other_u, other_x, sent_d,))
    other_d = exchange(sent_d, "dp", owners, 0)
    sent_u, kept_u = fold(kept_u, other_u)
    other_u = exchange(sent_u, "dp", owners, 1)
    sent_a, kept_a = fold(kept_a, other_a)
    other_a = exchange(sent_a, "dp", owners, 2)
    sent_x, kept_x = fold(kept_x, other_x)
    other_x = exchange(sent_x, "seq", groups, 1)
    sent_d, kept_d = fold(kept_d, other_d)
    other_u, other_a, sent_d, kept_d, = lax.optimization_barrier((other_u, other_a, sent_d, kept_d,))
    sent_u, kept_u = fold(kept_u, other_u)
    other_u = exchange(sent_u, "dp", owners, 2)
    grad_a = finish(kept_a, other_a)
    own_wout = lax.ppermute(grad_a[3 * rows :, :], ("dp", "seq"), [(target[f], f) for f in range(devices)])
    other_d = exchange(sent_d, "dp", owners, 1)
    other_u, other_d, other_x, = lax.optimization_barrier((other_u, other_d, other_x,))
    grad_u = finish(kept_u, other_u)
    sent_d, kept_d = fold(kept_d, other_d)
    block = shape((2, 2 * rows, 3 * part + hidden), BF16)
    sent, kept = call(deal_kernel, (block, block), [], 0, 0, grad_a, grad_u)
    near = exchange(sent, "seq", groups, 1)
    other_d = exchange(sent_d, "dp", owners, 2)
    both = finish(kept_x, other_x)
    outputs, grad_inputs = (v.astype(BF16)[None] for v in (both[:, :width], both[:, width:]))
    far = exchange(jnp.stack([kept[1], near[1]]), "seq", groups, 0)
    vector = shape((rows,), F32)
    own_wqkv, own_wup, own_wout, own_bqkv, own_bias, twin_bias, own_bup, *own, grad_d = call(
        collect_kernel,
        (shape(w_qkv.shape, F32), shape(w_up.shape, F32), shape(w_out.shape, F32))
        + (shape(b_qkv.shape, F32), vector, vector, shape(b_up.shape, F32), vector, vector, vector, vector, shape(w_down.shape, F32)),
        [pltpu.VMEM((groups, 2 * rows, 3 * part + hidden), F32)],
        0, 0, kept, near, far, grad_u, own_wout, kept_d, other_d,
    )
    return (
        outputs,
        grad_inputs,
        own_wqkv,
        own_bqkv,
        own_wout,
        own_bias,
        own_wup,
        own_bup,
        grad_d,
        twin_bias,
        *own,
    )


def solution(mesh):
    rows = P("dp", "seq", None)
    matrix, vector = P(("dp", "seq"), None), P(("dp", "seq"))
    weights = (matrix, vector) * 4
    return jax.shard_map(
        functools.partial(shards, mesh.shape["dp"], mesh.shape["seq"]),
        mesh=mesh,
        in_specs=(rows, rows) + weights + (vector,) * 4,
        out_specs=(rows, rows) + weights + (vector,) * 4,
        check_vma=False,
    )
```
